512 devices in a mesh: gx: 16 (over x, y), gy: 32 (over z, core).
Axes of the slice: x: 4, y: 4, z: 16, core: 2. Of those that a mesh axis runs over, the one named last changes fastest.
Arguments:
- right_side: float32 [128, 256, 512], P('gx', 'gy'), may hold values from -6 to 6
- coefficient: float32 [128, 256, 512], P('gx', 'gy'), may hold values from 0.1 to 10
Outputs:
- correction: float32 [128, 256, 512], P('gx', 'gy')
- residual: float32 [128, 256, 512], P('gx', 'gy')
The draws below stay inside these ranges and needn't reach their ends.
All inputs are finite; a program needn't handle non-finite values.
Results may differ from the reference program's by a relative error of at most 0.00016.
Values sent between devices are 32-bit elements; how exact they have to be, the bound alone decides.
No kernel may reach another device: no remote copies, remote signals or barrier semaphores. Data moves between devices by JAX's collectives and lax.ppermute only.
A program may use at most 128 MiB of HBM per device.

```python
import math
import jax
import jax.numpy as jnp

NZ = 512
SWEEPS = 2
COARSE_SWEEPS = 8
NX = 128
NY = 256


def draw_right_side(key, part):
    key = jax.random.fold_in(key, 7)
    values = jax.random.normal(key, (NX, NY, NZ), jnp.float32)
    return jnp.clip(values, -6.0, 6.0)


def steps_of(key, extent, pieces, smallest, top_value):
    factor_of, own = 1.0, jax.random.fold_in(key, 6)
    for dim, parts in pieces:
        heights = jnp.exp(jax.random.uniform(jax.random.fold_in(own, dim), (parts,), jnp.float32, smallest / len(pieces), top_value / len(pieces)))
        factor_of = factor_of * jnp.repeat(heights, extent[dim] // parts).reshape([-1 if axis == dim else 1 for axis in range(len(extent))])
    return factor_of


def setup_inputs(seed: int = 0) -> dict:
    splits = jax.random.split(jax.random.key(seed), 3)
    right_side = draw_right_side(jax.random.fold_in(splits[2], 71), 0)
    coefficient = jnp.clip(jnp.exp(math.log(10.0) - 4.6051702 * jax.random.uniform(splits[1], (NX, NY, NZ), jnp.float32) ** steps_of(splits[1], (NX, NY, NZ), ((0, 16), (1, 32)), -0.2, 0.2)), 0.1, 10.0)
    return {"right_side": right_side, "coefficient": coefficient}


absorption = 0.05
damping = 0.8


def block_mean(field):
    shaped = field.reshape(field.shape[0] // 2, 2, field.shape[1] // 2, 2, field.shape[2] // 2, 2)
    return jnp.sum(shaped, axis=(1, 3, 5)) * 0.125


def prolong(field):
    return jnp.repeat(jnp.repeat(jnp.repeat(field, 2, 0), 2, 1), 2, 2)


def face_terms(coef, scale):
    right_x = (coef + jnp.roll(coef, -1, 0)) * 0.5
    right_y = (coef + jnp.roll(coef, -1, 1)) * 0.5
    right_z = (coef + jnp.roll(coef, -1, 2)) * 0.5
    left_x = jnp.roll(right_x, 1, 0)
    left_y = jnp.roll(right_y, 1, 1)
    left_z = jnp.roll(right_z, 1, 2)
    return right_x, left_x, right_y, left_y, right_z, left_z


def apply_operator(field, coef, scale):
    right_x, left_x, right_y, left_y, right_z, left_z = face_terms(coef, scale)
    flux = right_x * (field - jnp.roll(field, -1, 0)) + left_x * (field - jnp.roll(field, 1, 0))
    flux = flux + right_y * (field - jnp.roll(field, -1, 1)) + left_y * (field - jnp.roll(field, 1, 1))
    flux = flux + right_z * (field - jnp.roll(field, -1, 2)) + left_z * (field - jnp.roll(field, 1, 2))
    return absorption * field + scale * flux


def diagonal_of(coef, scale):
    right_x, left_x, right_y, left_y, right_z, left_z = face_terms(coef, scale)
    return absorption + scale * (right_x + left_x + right_y + left_y + right_z + left_z)


def smooth(field, source, coef, scale, count):
    diagonal = diagonal_of(coef, scale)
    for sweep_index in range(count):
        field = field + damping * (source - apply_operator(field, coef, scale)) / diagonal
    return field


def reference(right_side, coefficient):
    coef_half = block_mean(coefficient)
    coef_quarter = block_mean(coef_half)
    fine_iter = smooth(jnp.zeros_like(right_side), right_side, coefficient, 1.0, SWEEPS)
    middle_rhs = block_mean(right_side - apply_operator(fine_iter, coefficient, 1.0))
    middle_iter = smooth(jnp.zeros_like(middle_rhs), middle_rhs, coef_half, 0.25, SWEEPS)
    coarse_rhs = block_mean(middle_rhs - apply_operator(middle_iter, coef_half, 0.25))
    coarse_iter = smooth(jnp.zeros_like(coarse_rhs), coarse_rhs, coef_quarter, 0.0625, COARSE_SWEEPS)
    middle_iter = smooth(middle_iter + prolong(coarse_iter), middle_rhs, coef_half, 0.25, SWEEPS)
    correction = smooth(fine_iter + prolong(middle_iter), right_side, coefficient, 1.0, SWEEPS)
    residual = right_side - apply_operator(correction, coefficient, 1.0)
    return correction, residual
```

```python
import jax
import jax.numpy as jnp
from jax import lax
from jax.experimental import pallas as pl
from jax.experimental.pallas import tpu as pltpu
from jax.sharding import PartitionSpec as P

ABSORPTION = 0.05
DAMPING = 0.8
F32 = jnp.float32
LANES = 128


def z_next(v):
    first = pltpu.roll(v[0], LANES - 1, 1)[None]
    return first if v.shape[0] == 1 else jnp.concatenate([v[1:], first], axis=0)


def z_prev(v):
    last = pltpu.roll(v[-1], 1, 1)[None]
    return last if v.shape[0] == 1 else jnp.concatenate([last, v[:-1]], axis=0)


def y_next(v):
    return pltpu.roll(v, v.shape[1] - 1, 1)


def y_prev(v):
    return pltpu.roll(v, 1, 1)


def flux_sum(u, u_next, flux_low, fx, fy, fz):
    flux_high = fx * (u - u_next)
    flux_y = fy * (u - y_next(u))
    flux_z = fz * (u - z_next(u))
    total = (flux_high - flux_low) + (flux_y - y_prev(flux_y)) + (flux_z - z_prev(flux_z))
    return ABSORPTION * u + total, flux_high


def loop(count, body, carry, unroll):
    return lax.fori_loop(0, count, body, carry, unroll=unroll)


def face_pass(count, k_ref, fx, fy, fz, w, scale, unroll):
    half = 0.5 * scale
    k0, k1 = k_ref[0], k_ref[1]
    low = half * (k0 + k1)
    fx[0] = low

    def body(i, carry):
        k, low = carry
        k_next = k_ref[i + 2]
        high = half * (k + k_next)
        face_y = half * (k + y_next(k))
        face_z = half * (k + z_next(k))
        diag = ABSORPTION + (high + low + face_y + y_prev(face_y) + face_z + z_prev(face_z))
        fx[i + 1] = high
        fy[i] = face_y
        fz[i] = face_z
        w[i] = DAMPING / diag
        return k_next, high

    loop(count, body, (k1, low), unroll)


def sweep_pass(count, u_ref, u_at, faces_at, g_ref, g_at, fx, fy, fz, w, out, out_at, unroll, last=False):
    u0, u1 = u_ref[u_at], u_ref[u_at + 1]
    low = fx[faces_at] * (u0 - u1)

    def body(i, carry):
        u, low = carry
        u_next = u_ref[u_at + 2 + i]
        f = faces_at + i
        applied, high = flux_sum(u, u_next, low, fx[f + 1], fy[f], fz[f])
        rest = g_ref[g_at + i] - applied
        out[out_at + i] = rest if last else u + w[f] * rest
        return u_next, high

    loop(count, body, (u1, low), unroll)


def permutation(inverse):
    z = lax.broadcasted_iota(jnp.int32, (512, 512), 1 if inverse else 0)
    at = lax.broadcasted_iota(jnp.int32, (512, 512), 0 if inverse else 1)
    return jnp.where(z == 4 * (at % LANES) + at // LANES, 1.0, 0.0).astype(F32)


def rearrange(rows, matrix):
    return lax.dot_general(rows, matrix, (((1,), (0,)), ((), ())), precision=lax.Precision.HIGHEST, preferred_element_type=F32)


def permute_kernel(g_ref, k_ref, own, high, low):
    matrix = permutation(False)
    for source, base in ((g_ref, 0), (k_ref, 8)):
        moved = rearrange(source[...].reshape(64, 512), matrix)
        for x in range(8):
            for r in range(4):
                own[base + x, r] = moved[8 * x : 8 * x + 8, LANES * r : LANES * r + LANES]
    high[0:4] = own[4:8]
    high[4:9] = own[11:16]
    low[0:4] = own[0:4]
    low[4:9] = own[8:13]


def wide_kernel(own, left, right, out):
    out[0:4] = left[0:4]
    out[4:12] = own[0:8]
    out[12:16] = right[0:4]
    out[16:21] = left[4:9]
    out[21:29] = own[8:16]
    out[29:34] = right[4:9]


def fine_kernel(own, left, right, piece, u_out, g_out, k_out, g, k, fx, fy, fz, w, uf, u0, res, s1, sc):
    for i in range(34):
        target = g.at[i] if i < 16 else k.at[i - 16]
        target[:, 0:8] = left[i]
        target[:, 8:16] = own[i]
        target[:, 16:24] = right[i]
    face_pass(16, k, fx, fy, fz, w, 1.0, 1)

    def first(i, carry):
        uf[i] = w[i] * g[i]
        return carry

    loop(16, first, 0, 1)
    sweep_pass(14, uf, 0, 1, g, 1, fx, fy, fz, w, u0, 0, 1)
    sweep_pass(8, u0, 2, 4, g, 4, fx, fy, fz, w, res, 0, 1, last=True)
    for x in range(4):
        both = res[2 * x] + res[2 * x + 1]
        s1[x, 0] = both[0] + both[1]
        s1[x, 1] = both[2] + both[3]
    for x in range(6):
        both = k[3 + 2 * x] + k[4 + 2 * x]
        sc[x, 0] = both[0] + both[1]
        sc[x, 1] = both[2] + both[3]

    def rows(ref, x, start):
        return jnp.stack(
            [ref[x, r, pl.ds(start, 8, 2), :] + ref[x, r, pl.ds(start + 1, 8, 2), :] for r in range(2)]
        ) * 0.125

    half = 0.5 * 0.25
    k_mid = [rows(sc, x, 4) for x in range(6)]
    for x in range(4):
        rhs = rows(s1, x, 4)
        here = k_mid[x + 1]
        face_z = half * (here + z_next(here))
        diag = ABSORPTION + (
            half * (here + k_mid[x]) + half * (here + k_mid[x + 2])
            + half * (here + rows(sc, x + 1, 2)) + half * (here + rows(sc, x + 1, 6))
            + face_z + z_prev(face_z)
        )
        piece[0, x] = DAMPING / diag * rhs
        piece[1, x] = here
    u_out[...] = u0[:, :, 4:20, :]
    g_out[...] = g[2:14, :, 4:20, :]
    k_out[...] = k[2:16, :, 4:20, :]


def middle_kernel(me, gathered, coarse, edge, u_out, rhs_out, fx_out, fy_out, fz_out, w_out,
                  uf, k, fx, fy, fz, w, rhs, u1, res, flat, flat_k, k2, r2):
    count = gathered.shape[0]
    for block in range(11):
        source = lax.rem(me[0] + (block - 5 + count * 5), count)
        uf[4 * block : 4 * block + 4] = gathered[source, 0]
        k[4 * block : 4 * block + 4] = gathered[source, 1]
    face_pass(42, k, fx, fy, fz, w, 0.25, 6)

    def right_side(i, carry):
        rhs[i] = uf[i + 1] / w[i]
        return carry

    loop(42, right_side, 0, 6)
    sweep_pass(42, uf, 0, 0, rhs, 0, fx, fy, fz, w, u1, 0, 6)
    sweep_pass(40, u1, 0, 1, rhs, 1, fx, fy, fz, w, res, 0, 5, last=True)

    def add_up(i, carry):
        both = res[2 * i] + res[2 * i + 1]
        flat[pl.ds(pl.multiple_of(8 * i, 8), 8), :] = both[0] + both[1]
        return carry

    loop(20, add_up, 0, 5)

    def add_up_k(i, carry):
        both = k[2 * i] + k[2 * i + 1]
        flat_k[pl.ds(pl.multiple_of(8 * i, 8), 8), :] = both[0] + both[1]
        return carry

    loop(22, add_up_k, 0, 2)
    flat[160:192] = jnp.zeros((32, LANES), F32)
    flat_k[176:256] = jnp.ones((80, LANES), F32)

    def row(ref, at, size):
        return (ref[pl.ds(at, size, 8), :] + ref[pl.ds(at + 1, size, 8), :]) * 0.125

    half = 0.5 * 0.0625
    for j in range(4):
        k2[j] = row(flat_k, 2 * j, 32)
    for j in range(2):
        here = k2[j + 1][0:32]
        face_x = half * (here + pltpu.roll(here, 31, 0))
        face_z = half * (here + pltpu.roll(here, LANES - 1, 1))
        diag = ABSORPTION + (
            face_x + pltpu.roll(face_x, 1, 0) + half * (here + k2[j]) + half * (here + k2[j + 2])
            + face_z + pltpu.roll(face_z, 1, 1)
        )
        r2[...] = DAMPING / diag
        coarse[2 * j] = r2[1:25] * row(flat, 2 * j + 2, 24)
        coarse[2 * j + 1] = k2[j + 1, 1:25]
    u_out[...] = u1[15:27]
    rhs_out[...] = rhs[16:26]
    fx_out[...] = fx[16:27]
    fy_out[...] = fy[16:26]
    fz_out[...] = fz[16:26]
    w_out[...] = w[16:26]
    uf[0:12] = u1[15:27]
    for x in range(12):
        for r in range(2):
            edge[0, 2 * x + r : 2 * x + r + 1, :] = uf[x, r, 4:5, :]
            edge[1, 2 * x + r : 2 * x + r + 1, :] = uf[x, r, 3:4, :]


def coarse_kernel(below, here, above, edge_low, edge_high, u_in, rhs, fx, fy, fz, w, v_out,
                  u, cx, cy, cz, cw, cr, v, va):
    half = 0.5 * 0.0625
    blocks = (below, here, above)

    def first(y):
        return blocks[y // 6][2 * (y % 6)]

    def coef(y):
        return blocks[y // 6][2 * (y % 6) + 1]

    for y in range(18):
        u[y] = first(y)
    cy[0] = half * (coef(0) + coef(1))
    for y in range(1, 17):
        k = coef(y)
        face_x = half * (k + pltpu.roll(k, 23, 0))
        face_z = half * (k + pltpu.roll(k, LANES - 1, 1))
        face_y = half * (k + coef(y + 1))
        diag = ABSORPTION + (
            face_x + pltpu.roll(face_x, 1, 0) + face_y + cy[y - 1] + face_z + pltpu.roll(face_z, 1, 1)
        )
        cx[y], cy[y], cz[y] = face_x, face_y, face_z
        cw[y] = DAMPING / diag
        cr[y] = first(y) * diag * (1.0 / DAMPING)
    for step in range(1, 8):
        now = u[step]
        low = cy[step - 1] * (u[step - 1] - now)
        for y in range(step, 18 - step):
            later = u[y + 1]
            high = cy[y] * (now - later)
            flux_x = cx[y] * (now - pltpu.roll(now, 23, 0))
            flux_z = cz[y] * (now - pltpu.roll(now, LANES - 1, 1))
            applied = ABSORPTION * now + (
                (high - low) + (flux_x - pltpu.roll(flux_x, 1, 0)) + (flux_z - pltpu.roll(flux_z, 1, 1))
            )
            u[y] = now + cw[y] * (cr[y] - applied)
            now, low = later, high
    v[...] = u_in[...]
    for x in range(12):
        for r in range(2):
            v[x, r, 0:1, :] = edge_low[2 * x + r : 2 * x + r + 1, :]
            v[x, r, 7:8, :] = edge_high[2 * x + r : 2 * x + r + 1, :]
    for x in range(6):
        rows = jnp.concatenate(
            [jnp.broadcast_to(u[7 + j, 7 + x : 8 + x, :], (2, LANES)) for j in range(4)], axis=0
        )
        for twin in range(2):
            for r in range(2):
                v[2 * x + twin, r] = v[2 * x + twin, r] + rows
    sweep_pass(10, v, 0, 0, rhs, 0, fx, fy, fz, w, va, 0, 5)
    sweep_pass(8, va, 0, 1, rhs, 1, fx, fy, fz, w, v_out, 0, 4)


def last_kernel(v_here, v_low, v_high, u0, g, k, correction, residual, fx, fy, fz, w, wide, ua, ub, res):
    for x in range(8):
        for r in range(2):
            rows = jnp.concatenate([v_low[x, r, 4:6], v_here[x, r, 2:6], v_high[x, r, 2:4]], axis=0)
            wide[x, r, pl.ds(0, 8, 2), :] = rows
            wide[x, r, pl.ds(1, 8, 2), :] = rows
    face_pass(12, k, fx, fy, fz, w, 1.0, 1)
    for i in range(14):
        fine = wide[(i + 1) // 2]
        ua[i] = u0[i] + jnp.stack([fine[0], fine[0], fine[1], fine[1]])
    sweep_pass(12, ua, 0, 0, g, 0, fx, fy, fz, w, ub, 0, 1)
    sweep_pass(10, ub, 0, 1, g, 1, fx, fy, fz, w, ua, 0, 1)
    sweep_pass(8, ua, 0, 2, g, 2, fx, fy, fz, w, res, 0, 1, last=True)
    matrix = permutation(True)
    for source, at, out in ((ua, 1, correction), (res, 0, residual)):
        rows = [
            jnp.concatenate([source[at + x, r, 4:12, :] for r in range(4)], axis=1) for x in range(8)
        ]
        out[...] = rearrange(jnp.concatenate(rows, axis=0), matrix).reshape(8, 8, 512)


VMEM = pl.BlockSpec(memory_space=pltpu.VMEM)
SMEM = pl.BlockSpec(memory_space=pltpu.SMEM)


def call(kernel, outs, scratch, *arrays, scalars=0):
    return pl.pallas_call(
        kernel,
        out_shape=[jax.ShapeDtypeStruct(shape, F32) for shape in outs],
        in_specs=[SMEM] * scalars + [VMEM] * (len(arrays) - scalars),
        out_specs=[VMEM] * len(outs),
        scratch_shapes=[pltpu.VMEM(shape, F32) for shape in scratch],
        compiler_params=pltpu.CompilerParams(vmem_limit_bytes=32 * 2**20),
    )(*arrays)


def shift(array, axis, by):
    count = lax.axis_size(axis)
    return lax.ppermute(array, axis, [(i, (i + by) % count) for i in range(count)])


def per_device(right_side, coefficient):
    own, high, low = call(
        permute_kernel, [(16, 4, 8, 128), (9, 4, 8, 128), (9, 4, 8, 128)], [], right_side, coefficient
    )
    left, right = shift(high, "gx", 1), shift(low, "gx", -1)
    (wide,) = call(wide_kernel, [(34, 4, 8, 128)], [], own, left, right)
    left, right = shift(wide, "gy", 1), shift(wide, "gy", -1)
    fine = (4, 24, 128)
    piece, u0, g, k = call(
        fine_kernel,
        [(2, 4, 2, 8, 128), (14, 4, 16, 128), (12, 4, 16, 128), (14, 4, 16, 128)],
        [(16, *fine), (18, *fine), (17, *fine), (16, *fine), (16, *fine), (16, *fine), (16, *fine), (14, *fine),
         (8, *fine), (4, 2, 24, 128), (6, 2, 24, 128)],
        wide, left, right,
    )
    count = lax.axis_size("gx")
    gathered = lax.all_to_all(jnp.broadcast_to(piece[None], (count, *piece.shape)), "gx", 0, 0)
    me = lax.axis_index("gx").astype(jnp.int32).reshape(1)
    mid = (2, 8, 128)
    coarse, edge, u1, rhs, fx, fy, fz, w = call(
        middle_kernel,
        [(4, 24, 128), (2, 24, 128), (12, *mid), (10, *mid), (11, *mid), (10, *mid), (10, *mid), (10, *mid)],
        [(44, *mid), (44, *mid), (43, *mid), (42, *mid), (42, *mid), (42, *mid), (42, *mid), (42, *mid), (40, *mid),
         (192, 128), (256, 128), (4, 32, 128), (32, 128)],
        me, gathered, scalars=1,
    )
    low = shift(jnp.concatenate([coarse, edge[0:1]]), "gy", 1)
    high = shift(jnp.concatenate([coarse, edge[1:2]]), "gy", -1)
    three = jnp.concatenate([low[0:4], coarse, high[0:4]])
    below, above = shift(three, "gy", 3), shift(three, "gy", -3)
    rows = (18, 24, 128)
    (v1,) = call(
        coarse_kernel, [(8, *mid)], [rows, rows, rows, rows, rows, rows, (12, *mid), (10, *mid)],
        below, three, above, low[4], high[4], u1, rhs, fx, fy, fz, w,
    )
    low, high = shift(v1, "gy", 1), shift(v1, "gy", -1)
    last = (4, 16, 128)
    return tuple(call(
        last_kernel, [(8, 8, 512), (8, 8, 512)],
        [(13, *last), (12, *last), (12, *last), (12, *last), (8, 2, 16, 128), (14, *last), (12, *last), (8, *last)],
        v1, low, high, u0, g, k,
    ))


def solution(mesh):
    placed = (P("gx", "gy", None), P("gx", "gy", None))
    return jax.shard_map(per_device, mesh=mesh, in_specs=placed, out_specs=placed, check_vma=False)
```

```python
import jax
import jax.numpy as jnp
from jax import lax
from jax.experimental import pallas as pl
from jax.experimental.pallas import tpu as pltpu
from jax.sharding import PartitionSpec as P

ABSORPTION = 0.05
DAMPING = 0.8
F32 = jnp.float32
LANES = 128


def z_next(v):
    first = pltpu.roll(v[0], LANES - 1, 1)[None]
    return first if v.shape[0] == 1 else jnp.concatenate([v[1:], first], axis=0)


def z_prev(v):
    last = pltpu.roll(v[-1], 1, 1)[None]
    return last if v.shape[0] == 1 else jnp.concatenate([last, v[:-1]], axis=0)


def y_next(v):
    return pltpu.roll(v, v.shape[1] - 1, 1)


def y_prev(v):
    return pltpu.roll(v, 1, 1)


def flux_sum(u, u_next, flux_low, fx, fy, fz):
    flux_high = fx * (u - u_next)
    flux_y = fy * (u - y_next(u))
    flux_z = fz * (u - z_next(u))
    total = (flux_high - flux_low) + (flux_y - y_prev(flux_y)) + (flux_z - z_prev(flux_z))
    return ABSORPTION * u + total, flux_high


def loop(count, body, carry, unroll):
    return lax.fori_loop(0, count, body, carry, unroll=unroll)


def face_pass(count, k_ref, fx, fy, fz, w, scale, unroll):
    half = 0.5 * scale
    k0, k1 = k_ref[0], k_ref[1]
    low = half * (k0 + k1)
    fx[0] = low

    def body(i, carry):
        k, low = carry
        k_next = k_ref[i + 2]
        high = half * (k + k_next)
        face_y = half * (k + y_next(k))
        face_z = half * (k + z_next(k))
        diag = ABSORPTION + (high + low + face_y + y_prev(face_y) + face_z + z_prev(face_z))
        fx[i + 1] = high
        fy[i] = face_y
        fz[i] = face_z
        w[i] = DAMPING / diag
        return k_next, high

    loop(count, body, (k1, low), unroll)


def sweep_pass(count, u_ref, u_at, faces_at, g_ref, g_at, fx, fy, fz, w, out, out_at, unroll, last=False):
    u0, u1 = u_ref[u_at], u_ref[u_at + 1]
    low = fx[faces_at] * (u0 - u1)

    def body(i, carry):
        u, low = carry
        u_next = u_ref[u_at + 2 + i]
        f = faces_at + i
        applied, high = flux_sum(u, u_next, low, fx[f + 1], fy[f], fz[f])
        rest = g_ref[g_at + i] - applied
        out[out_at + i] = rest if last else u + w[f] * rest
        return u_next, high

    loop(count, body, (u1, low), unroll)


def permutation(inverse):
    z = lax.broadcasted_iota(jnp.int32, (512, 512), 1 if inverse else 0)
    at = lax.broadcasted_iota(jnp.int32, (512, 512), 0 if inverse else 1)
    return jnp.where(z == 4 * (at % LANES) + at // LANES, 1.0, 0.0).astype(jnp.bfloat16)


def rearrange(rows, matrix):
    count = rows.shape[0]
    top = rows.astype(jnp.bfloat16)
    rest = rows - top.astype(F32)
    middle = rest.astype(jnp.bfloat16)
    bottom = (rest - middle.astype(F32)).astype(jnp.bfloat16)
    parts = jnp.concatenate([top, middle, bottom], axis=0)
    moved = lax.dot_general(parts, matrix, (((1,), (0,)), ((), ())), preferred_element_type=F32)
    return (moved[0:count] + moved[count : 2 * count]) + moved[2 * count :]


def permute_kernel(g_ref, k_ref, own, high, low, held, arrived):
    copies = [pltpu.make_async_copy(ref, held.at[i], arrived.at[i]) for i, ref in enumerate((g_ref, k_ref))]
    for copy in copies:
        copy.start()
    matrix = permutation(False)
    for copy in copies:
        copy.wait()
    moved = rearrange(held[...].reshape(128, 512), matrix)
    for x in range(16):
        for r in range(4):
            own[x, r] = moved[8 * x : 8 * x + 8, LANES * r : LANES * r + LANES]
    high[0:4] = own[4:8]
    high[4:9] = own[11:16]
    low[0:4] = own[0:4]
    low[4:9] = own[8:13]


def wide_kernel(own, left, right, out):
    out[0:4] = left[0:4]
    out[4:12] = own[0:8]
    out[12:16] = right[0:4]
    out[16:21] = left[4:9]
    out[21:29] = own[8:16]
    out[29:34] = right[4:9]


def fine_kernel(own, left, right, piece, u_out, g_out, k_out, g, k, fx, fy, fz, w, uf, u0, res, s1, sc):
    for i in range(34):
        target = g.at[i] if i < 16 else k.at[i - 16]
        target[:, 0:8] = left[i]
        target[:, 8:16] = own[i]
        target[:, 16:24] = right[i]
    face_pass(16, k, fx, fy, fz, w, 1.0, 16)

    def first(i, carry):
        uf[i] = w[i] * g[i]
        return carry

    loop(16, first, 0, 16)
    sweep_pass(14, uf, 0, 1, g, 1, fx, fy, fz, w, u0, 0, 14)
    sweep_pass(8, u0, 2, 4, g, 4, fx, fy, fz, w, res, 0, 8, last=True)
    for x in range(4):
        both = res[2 * x] + res[2 * x + 1]
        s1[x, 0] = both[0] + both[1]
        s1[x, 1] = both[2] + both[3]
    for x in range(6):
        both = k[3 + 2 * x] + k[4 + 2 * x]
        sc[x, 0] = both[0] + both[1]
        sc[x, 1] = both[2] + both[3]

    def rows(ref, x, start):
        return jnp.stack(
            [ref[x, r, pl.ds(start, 8, 2), :] + ref[x, r, pl.ds(start + 1, 8, 2), :] for r in range(2)]
        ) * 0.125

    half = 0.5 * 0.25
    k_mid = [rows(sc, x, 4) for x in range(6)]
    for x in range(4):
        rhs = rows(s1, x, 4)
        here = k_mid[x + 1]
        face_z = half * (here + z_next(here))
        diag = ABSORPTION + (
            half * (here + k_mid[x]) + half * (here + k_mid[x + 2])
            + half * (here + rows(sc, x + 1, 2)) + half * (here + rows(sc, x + 1, 6))
            + face_z + z_prev(face_z)
        )
        first_sweep = DAMPING / diag * rhs
        for to in range(piece.shape[0]):
            piece[to, 0, x] = first_sweep
            piece[to, 1, x] = here
    u_out[...] = u0[:, :, 4:20, :]
    g_out[...] = g[2:14, :, 4:20, :]
    k_out[...] = k[2:16, :, 4:20, :]


def middle_kernel(me, gathered, send_high, send_low, u_out, rhs_out, fx_out, fy_out, fz_out, w_out,
                  uf, k, fx, fy, fz, w, rhs, u1, res, flat, flat_k, k2, r2):
    count = gathered.shape[0]
    for block in range(11):
        source = lax.rem(me[0] + (block - 5 + count * 5), count)
        uf[4 * block : 4 * block + 4] = gathered[source, 0]
        k[4 * block : 4 * block + 4] = gathered[source, 1]
    face_pass(42, k, fx, fy, fz, w, 0.25, 42)

    def right_side(i, carry):
        rhs[i] = uf[i + 1] / w[i]
        return carry

    loop(42, right_side, 0, 42)
    sweep_pass(42, uf, 0, 0, rhs, 0, fx, fy, fz, w, u1, 0, 42)
    sweep_pass(40, u1, 0, 1, rhs, 1, fx, fy, fz, w, res, 0, 40, last=True)

    def add_up(i, carry):
        both = res[2 * i] + res[2 * i + 1]
        flat[pl.ds(pl.multiple_of(8 * i, 8), 8), :] = both[0] + both[1]
        return carry

    loop(20, add_up, 0, 20)

    def add_up_k(i, carry):
        both = k[2 * i] + k[2 * i + 1]
        flat_k[pl.ds(pl.multiple_of(8 * i, 8), 8), :] = both[0] + both[1]
        return carry

    loop(22, add_up_k, 0, 22)
    flat[160:192] = jnp.zeros((32, LANES), F32)
    flat_k[176:256] = jnp.ones((80, LANES), F32)

    def row(ref, at, size):
        return (ref[pl.ds(at, size, 8), :] + ref[pl.ds(at + 1, size, 8), :]) * 0.125

    half = 0.5 * 0.0625
    for j in range(4):
        k2[j] = row(flat_k, 2 * j, 32)
    for j in range(2):
        here = k2[j + 1][0:32]
        face_x = half * (here + pltpu.roll(here, 31, 0))
        face_z = half * (here + pltpu.roll(here, LANES - 1, 1))
        diag = ABSORPTION + (
            face_x + pltpu.roll(face_x, 1, 0) + half * (here + k2[j]) + half * (here + k2[j + 2])
            + face_z + pltpu.roll(face_z, 1, 1)
        )
        r2[...] = DAMPING / diag
        for coarse in (send_high, send_low):
            coarse[2 * j] = r2[1:25] * row(flat, 2 * j + 2, 24)
            coarse[2 * j + 1] = k2[j + 1, 1:25]
    u_out[...] = u1[15:27]
    rhs_out[...] = rhs[16:26]
    fx_out[...] = fx[16:27]
    fy_out[...] = fy[16:26]
    fz_out[...] = fz[16:26]
    w_out[...] = w[16:26]
    uf[0:12] = u1[15:27]
    for x in range(12):
        for r in range(2):
            send_high[4, 2 * x + r : 2 * x + r + 1, :] = uf[x, r, 4:5, :]
            send_low[4, 2 * x + r : 2 * x + r + 1, :] = uf[x, r, 3:4, :]


def three_kernel(here, low, high, out):
    out[0:4] = low[0:4]
    out[4:8] = here[0:4]
    out[8:12] = high[0:4]


def coarse_kernel(below, here, above, left, right, u_in, rhs, fx, fy, fz, w, v_out,
                  u, cx, cy, cz, cw, cr, v, va):
    half = 0.5 * 0.0625
    blocks = (below, here, above)

    def first(y):
        return blocks[y // 6][2 * (y % 6)]

    def coef(y):
        return blocks[y // 6][2 * (y % 6) + 1]

    for y in range(18):
        u[y] = first(y)
    cy[0] = half * (coef(0) + coef(1))
    for y in range(1, 17):
        k = coef(y)
        face_x = half * (k + pltpu.roll(k, 23, 0))
        face_z = half * (k + pltpu.roll(k, LANES - 1, 1))
        face_y = half * (k + coef(y + 1))
        diag = ABSORPTION + (
            face_x + pltpu.roll(face_x, 1, 0) + face_y + cy[y - 1] + face_z + pltpu.roll(face_z, 1, 1)
        )
        cx[y], cy[y], cz[y] = face_x, face_y, face_z
        cw[y] = DAMPING / diag
        cr[y] = first(y) * diag * (1.0 / DAMPING)
    for step in range(1, 8):
        now = u[step]
        low = cy[step - 1] * (u[step - 1] - now)
        for y in range(step, 18 - step):
            later = u[y + 1]
            high = cy[y] * (now - later)
            flux_x = cx[y] * (now - pltpu.roll(now, 23, 0))
            flux_z = cz[y] * (now - pltpu.roll(now, LANES - 1, 1))
            applied = ABSORPTION * now + (
                (high - low) + (flux_x - pltpu.roll(flux_x, 1, 0)) + (flux_z - pltpu.roll(flux_z, 1, 1))
            )
            u[y] = now + cw[y] * (cr[y] - applied)
            now, low = later, high
    v[...] = u_in[...]
    for x in range(12):
        for r in range(2):
            v[x, r, 0:1, :] = left[4, 2 * x + r : 2 * x + r + 1, :]
            v[x, r, 7:8, :] = right[4, 2 * x + r : 2 * x + r + 1, :]
    for x in range(6):
        rows = jnp.concatenate(
            [jnp.broadcast_to(u[7 + j, 7 + x : 8 + x, :], (2, LANES)) for j in range(4)], axis=0
        )
        for twin in range(2):
            for r in range(2):
                v[2 * x + twin, r] = v[2 * x + twin, r] + rows
    sweep_pass(10, v, 0, 0, rhs, 0, fx, fy, fz, w, va, 0, 10)
    sweep_pass(8, va, 0, 1, rhs, 1, fx, fy, fz, w, v_out, 0, 8)


def last_kernel(v_here, v_low, v_high, u0, g, k, correction, residual, fx, fy, fz, w, wide, ua, ub, res):
    for x in range(8):
        for r in range(2):
            rows = jnp.concatenate([v_low[x, r, 4:6], v_here[x, r, 2:6], v_high[x, r, 2:4]], axis=0)
            wide[x, r, pl.ds(0, 8, 2), :] = rows
            wide[x, r, pl.ds(1, 8, 2), :] = rows
    face_pass(12, k, fx, fy, fz, w, 1.0, 12)
    for i in range(14):
        fine = wide[(i + 1) // 2]
        ua[i] = u0[i] + jnp.stack([fine[0], fine[0], fine[1], fine[1]])
    sweep_pass(12, ua, 0, 0, g, 0, fx, fy, fz, w, ub, 0, 12)
    sweep_pass(10, ub, 0, 1, g, 1, fx, fy, fz, w, ua, 0, 10)
    sweep_pass(8, ua, 0, 2, g, 2, fx, fy, fz, w, res, 0, 8, last=True)
    matrix = permutation(True)
    for source, at, out in ((ua, 1, correction), (res, 0, residual)):
        rows = [
            jnp.concatenate([source[at + x, r, 4:12, :] for r in range(4)], axis=1) for x in range(8)
        ]
        out[...] = rearrange(jnp.concatenate(rows, axis=0), matrix).reshape(8, 8, 512)


VMEM = pl.BlockSpec(memory_space=pltpu.VMEM)
SMEM = pl.BlockSpec(memory_space=pltpu.SMEM)
HBM = pl.BlockSpec(memory_space=pltpu.HBM)


def call(kernel, outs, scratch, *arrays, scalars=0, far=0, extra=()):
    return pl.pallas_call(
        kernel,
        out_shape=[jax.ShapeDtypeStruct(shape, F32) for shape in outs],
        in_specs=[SMEM] * scalars + [HBM] * far + [VMEM] * (len(arrays) - scalars - far),
        out_specs=[VMEM] * len(outs),
        scratch_shapes=[pltpu.VMEM(shape, F32) for shape in scratch] + list(extra),
        compiler_params=pltpu.CompilerParams(vmem_limit_bytes=32 * 2**20),
    )(*arrays)


def shift(array, axis, by):
    count = lax.axis_size(axis)
    return lax.ppermute(array, axis, [(i, (i + by) % count) for i in range(count)])


def per_device(right_side, coefficient):
    own, high, low = call(
        permute_kernel, [(16, 4, 8, 128), (9, 4, 8, 128), (9, 4, 8, 128)], [(2, 8, 8, 512)], right_side, coefficient,
        far=2, extra=[pltpu.SemaphoreType.DMA((2,))],
    )
    left, right = shift(high, "gx", 1), shift(low, "gx", -1)
    (wide,) = call(wide_kernel, [(34, 4, 8, 128)], [], own, left, right)
    left, right = shift(wide, "gy", 1), shift(wide, "gy", -1)
    fine = (4, 24, 128)
    count = lax.axis_size("gx")
    piece, u0, g, k = call(
        fine_kernel,
        [(count, 2, 4, 2, 8, 128), (14, 4, 16, 128), (12, 4, 16, 128), (14, 4, 16, 128)],
        [(16, *fine), (18, *fine), (17, *fine), (16, *fine), (16, *fine), (16, *fine), (16, *fine), (14, *fine),
         (8, *fine), (4, 2, 24, 128), (6, 2, 24, 128)],
        wide, left, right,
    )
    gathered = lax.all_to_all(piece, "gx", 0, 0)
    me = lax.axis_index("gx").astype(jnp.int32).reshape(1)
    mid = (2, 8, 128)
    high, low, u1, rhs, fx, fy, fz, w = call(
        middle_kernel,
        [(5, 24, 128), (5, 24, 128), (12, *mid), (10, *mid), (11, *mid), (10, *mid), (10, *mid), (10, *mid)],
        [(44, *mid), (44, *mid), (43, *mid), (42, *mid), (42, *mid), (42, *mid), (42, *mid), (42, *mid), (40, *mid),
         (192, 128), (256, 128), (4, 32, 128), (32, 128)],
        me, gathered, scalars=1,
    )
    here = high
    low, high = shift(high, "gy", 1), shift(low, "gy", -1)
    (three,) = call(three_kernel, [(12, 24, 128)], [], here, low, high)
    below, above = shift(three, "gy", 3), shift(three, "gy", -3)
    rows = (18, 24, 128)
    (v1,) = call(
        coarse_kernel, [(8, *mid)], [rows, rows, rows, rows, rows, rows, (12, *mid), (10, *mid)],
        below, three, above, low, high, u1, rhs, fx, fy, fz, w,
    )
    low, high = shift(v1, "gy", 1), shift(v1, "gy", -1)
    last = (4, 16, 128)
    return tuple(call(
        last_kernel, [(8, 8, 512), (8, 8, 512)],
        [(13, *last), (12, *last), (12, *last), (12, *last), (8, 2, 16, 128), (14, *last), (12, *last), (8, *last)],
        v1, low, high, u0, g, k,
    ))


def solution(mesh):
    placed = (P("gx", "gy", None), P("gx", "gy", None))
    return jax.shard_map(per_device, mesh=mesh, in_specs=placed, out_specs=placed, check_vma=False)
```

```python
import jax
import jax.numpy as jnp
from jax import lax
from jax.experimental import pallas as pl
from jax.experimental.pallas import tpu as pltpu
from jax.sharding import PartitionSpec as P

ABSORPTION = 0.05
DAMPING = 0.8
F32 = jnp.float32
LANES = 128


def z_next(v):
    first = pltpu.roll(v[0], LANES - 1, 1)[None]
    return first if v.shape[0] == 1 else jnp.concatenate([v[1:], first], axis=0)


def z_prev(v):
    last = pltpu.roll(v[-1], 1, 1)[None]
    return last if v.shape[0] == 1 else jnp.concatenate([last, v[:-1]], axis=0)


def y_next(v):
    return pltpu.roll(v, v.shape[1] - 1, 1)


def y_prev(v):
    return pltpu.roll(v, 1, 1)


def flux_sum(u, u_next, flux_low, fx, fy, fz):
    flux_high = fx * (u - u_next)
    flux_y = fy * (u - y_next(u))
    flux_z = fz * (u - z_next(u))
    total = (flux_high - flux_low) + (flux_y - y_prev(flux_y)) + (flux_z - z_prev(flux_z))
    return ABSORPTION * u + total, flux_high


class Slabs:
    def __init__(self, flat, rows):
        self.flat, self.rows = flat, rows

    def at(self, i):
        return pl.ds(pl.multiple_of(i * (4 * self.rows), 8), 4 * self.rows)

    def __getitem__(self, i):
        return self.flat[self.at(i), :].reshape(4, self.rows, LANES)

    def __setitem__(self, i, value):
        self.flat[self.at(i), :] = value.reshape(4 * self.rows, LANES)

    def part(self, i, start, size):
        return jnp.stack([self.flat[pl.ds((4 * i + r) * self.rows + start, size), :] for r in range(4)])

    def put(self, i, start, value):
        for r in range(4):
            self.flat[pl.ds((4 * i + r) * self.rows + start, value.shape[1]), :] = value[r]


def loop(count, body, carry, unroll):
    return lax.fori_loop(0, count, body, carry, unroll=unroll)


def face_pass(count, k_ref, fx, fy, fz, w, scale, unroll):
    half = 0.5 * scale
    k0, k1 = k_ref[0], k_ref[1]
    low = half * (k0 + k1)
    fx[0] = low

    def body(i, carry):
        k, low = carry
        k_next = k_ref[i + 2]
        high = half * (k + k_next)
        face_y = half * (k + y_next(k))
        face_z = half * (k + z_next(k))
        diag = ABSORPTION + (high + low + face_y + y_prev(face_y) + face_z + z_prev(face_z))
        fx[i + 1] = high
        fy[i] = face_y
        fz[i] = face_z
        w[i] = DAMPING / diag
        return k_next, high

    loop(count, body, (k1, low), unroll)


def sweep_pass(count, u_ref, u_at, faces_at, g_ref, g_at, fx, fy, fz, w, out, out_at, unroll, last=False):
    u0, u1 = u_ref[u_at], u_ref[u_at + 1]
    low = fx[faces_at] * (u0 - u1)

    def body(i, carry):
        u, low = carry
        u_next = u_ref[u_at + 2 + i]
        f = faces_at + i
        applied, high = flux_sum(u, u_next, low, fx[f + 1], fy[f], fz[f])
        rest = g_ref[g_at + i] - applied
        out[out_at + i] = rest if last else u + w[f] * rest
        return u_next, high

    loop(count, body, (u1, low), unroll)


def permutation(inverse):
    z = lax.broadcasted_iota(jnp.int32, (512, 512), 1 if inverse else 0)
    at = lax.broadcasted_iota(jnp.int32, (512, 512), 0 if inverse else 1)
    return jnp.where(z == 4 * (at % LANES) + at // LANES, 1.0, 0.0).astype(jnp.bfloat16)


def rearrange(rows, matrix):
    count = rows.shape[0]
    top = rows.astype(jnp.bfloat16)
    rest = rows - top.astype(F32)
    middle = rest.astype(jnp.bfloat16)
    bottom = (rest - middle.astype(F32)).astype(jnp.bfloat16)
    parts = jnp.concatenate([top, middle, bottom], axis=0)
    moved = lax.dot_general(parts, matrix, (((1,), (0,)), ((), ())), preferred_element_type=F32)
    return (moved[0:count] + moved[count : 2 * count]) + moved[2 * count :]


def permute_kernel(me, held, own, to_first, to_second):
    matrix = permutation(False)
    moved = rearrange(held[...].reshape(128, 512), matrix)
    for x in range(16):
        for r in range(4):
            own[x, r] = moved[8 * x : 8 * x + 8, LANES * r : LANES * r + LANES]
    even = lax.rem(me[0], 2) == 0
    for take, high, low in ((even, to_second, to_first), (jnp.logical_not(even), to_first, to_second)):
        @pl.when(take)
        def _(high=high, low=low):
            high[0:4] = own[4:8]
            high[4:9] = own[11:16]
            low[0:4] = own[0:4]
            low[4:9] = own[8:13]


G_REACH = (3, 2, 2, 2, 1, 0)
K_REACH = (4, 3, 3, 3, 2, 1, 0)


def row_parts():
    at = 0
    for array, reaches, border in ((0, G_REACH, 4), (1, K_REACH, 5)):
        for d, reach in enumerate(reaches, 1):
            size = 4 * (8 + 2 * reach)
            yield array, d, border - reach, size, at
            at += size


ROWS = sum(part[3] for part in row_parts())


def wide_kernel(me, own, first, second, flat, to_high, to_low):
    out = Slabs(flat, 8)

    def put(at, source, start, size):
        for i in range(size):
            out[at + i] = source[start + i]

    put(4, own, 0, 8)
    put(21, own, 8, 8)
    even = lax.rem(me[0], 2) == 0
    for take, left, right in ((even, first, second), (jnp.logical_not(even), second, first)):
        @pl.when(take)
        def _(left=left, right=right):
            put(0, left, 0, 4)
            put(12, right, 0, 4)
            put(16, left, 4, 5)
            put(29, right, 4, 5)
    for array, d, column, size, at in row_parts():
        base = (16 * array + column) * 32
        to_high[at : at + size] = flat[pl.ds(base + 8 - d, size, 8), :]
        to_low[at : at + size] = flat[pl.ds(base + d - 1, size, 8), :]


def fine_kernel(own, low, high, piece, u0, g_flat, k_flat, fx, fy, fz, w, uf, res, s1, sc):
    flats = g_flat, k_flat
    own, g, k = Slabs(own, 8), Slabs(g_flat, 24), Slabs(k_flat, 24)
    for i in range(34):
        (g if i < 16 else k).put(i if i < 16 else i - 16, 8, own[i])
    for array, d, column, size, at in row_parts():
        flats[array][pl.ds(column * 96 + 8 - d, size, 24), :] = low[at : at + size]
        flats[array][pl.ds(column * 96 + 15 + d, size, 24), :] = high[at : at + size]
    face_pass(16, k, fx, fy, fz, w, 1.0, 16)

    def first(i, carry):
        uf[i] = w[i] * g[i]
        return carry

    loop(16, first, 0, 16)
    sweep_pass(14, uf, 0, 1, g, 1, fx, fy, fz, w, u0, 0, 14)
    sweep_pass(8, u0, 2, 4, g, 4, fx, fy, fz, w, res, 0, 8, last=True)
    for x in range(4):
        both = res[2 * x] + res[2 * x + 1]
        s1[x, 0] = both[0] + both[1]
        s1[x, 1] = both[2] + both[3]
    for x in range(6):
        both = k[3 + 2 * x] + k[4 + 2 * x]
        sc[x, 0] = both[0] + both[1]
        sc[x, 1] = both[2] + both[3]

    def rows(ref, x, start):
        return jnp.stack(
            [ref[x, r, pl.ds(start, 8, 2), :] + ref[x, r, pl.ds(start + 1, 8, 2), :] for r in range(2)]
        ) * 0.125

    half = 0.5 * 0.25
    k_mid = [rows(sc, x, 4) for x in range(6)]
    for x in range(4):
        rhs = rows(s1, x, 4)
        here = k_mid[x + 1]
        face_z = half * (here + z_next(here))
        diag = ABSORPTION + (
            half * (here + k_mid[x]) + half * (here + k_mid[x + 2])
            + half * (here + rows(sc, x + 1, 2)) + half * (here + rows(sc, x + 1, 6))
            + face_z + z_prev(face_z)
        )
        first_sweep = DAMPING / diag * rhs
        for to in range(piece.shape[0]):
            piece[to, 0, x] = first_sweep
            piece[to, 1, x] = here


def prepare_kernel(u0, g_flat, k_flat, u_out, g_out, fx, fy, fz, w, k_rows):
    g, k = Slabs(g_flat, 24), Slabs(k_flat, 24)
    for i in range(14):
        u_out[i] = u0[i, :, 4:20, :]
        k_rows[i] = k.part(i + 2, 4, 16)
    for i in range(12):
        g_out[i] = g.part(i + 2, 4, 16)
    face_pass(12, k_rows, fx, fy, fz, w, 1.0, 12)


def middle_kernel(me, gathered, send_high, send_low, u_out, rhs_out, fx_out, fy_out, fz_out, w_out,
                  uf, k, fx, fy, fz, w, rhs, u1, res, flat, flat_k, k2, r2):
    count = gathered.shape[0]
    for block in range(11):
        source = lax.rem(me[0] + (block - 5 + count * 5), count)
        uf[4 * block : 4 * block + 4] = gathered[source, 0]
        k[4 * block : 4 * block + 4] = gathered[source, 1]
    face_pass(42, k, fx, fy, fz, w, 0.25, 42)

    def right_side(i, carry):
        rhs[i] = uf[i + 1] / w[i]
        return carry

    loop(42, right_side, 0, 42)
    sweep_pass(42, uf, 0, 0, rhs, 0, fx, fy, fz, w, u1, 0, 42)
    sweep_pass(40, u1, 0, 1, rhs, 1, fx, fy, fz, w, res, 0, 40, last=True)

    def add_up(i, carry):
        both = res[2 * i] + res[2 * i + 1]
        flat[pl.ds(pl.multiple_of(8 * i, 8), 8), :] = both[0] + both[1]
        return carry

    loop(20, add_up, 0, 20)

    def add_up_k(i, carry):
        both = k[2 * i] + k[2 * i + 1]
        flat_k[pl.ds(pl.multiple_of(8 * i, 8), 8), :] = both[0] + both[1]
        return carry

    loop(22, add_up_k, 0, 22)
    flat[160:192] = jnp.zeros((32, LANES), F32)
    flat_k[176:256] = jnp.ones((80, LANES), F32)

    def row(ref, at, size):
        return (ref[pl.ds(at, size, 8), :] + ref[pl.ds(at + 1, size, 8), :]) * 0.125

    half = 0.5 * 0.0625
    for j in range(4):
        k2[j] = row(flat_k, 2 * j, 32)
    for j in range(2):
        here = k2[j + 1][0:32]
        face_x = half * (here + pltpu.roll(here, 31, 0))
        face_z = half * (here + pltpu.roll(here, LANES - 1, 1))
        diag = ABSORPTION + (
            face_x + pltpu.roll(face_x, 1, 0) + half * (here + k2[j]) + half * (here + k2[j + 2])
            + face_z + pltpu.roll(face_z, 1, 1)
        )
        r2[...] = DAMPING / diag
        for coarse in (send_high, send_low):
            coarse[2 * j] = r2[1:25] * row(flat, 2 * j + 2, 24)
            coarse[2 * j + 1] = k2[j + 1, 1:25]
    u_out[...] = u1[15:27]
    rhs_out[...] = rhs[16:26]
    fx_out[...] = fx[16:27]
    fy_out[...] = fy[16:26]
    fz_out[...] = fz[16:26]
    w_out[...] = w[16:26]
    uf[0:12] = u1[15:27]
    for x in range(12):
        for r in range(2):
            send_high[4, 2 * x + r : 2 * x + r + 1, :] = uf[x, r, 4:5, :]
            send_low[4, 2 * x + r : 2 * x + r + 1, :] = uf[x, r, 3:4, :]


def spread(j, upward):
    d = j if upward else 5 - j
    start, size = (2, 16) if d < 4 else (6, 8)
    return start, size, 32 * d if d < 4 else 128 + 16 * (d - 4)


def three_kernel(here, low, high, to_high, to_low):
    blocks = (low, here, high)
    for j in range(6):
        source = blocks[j // 2]
        for out, upward in ((to_high, False), (to_low, True)):
            start, size, at = spread(j, upward)
            for array in range(2):
                out[at + size * array : at + size * array + size] = source[2 * (j % 2) + array, start : start + size]


def coarse_kernel(below, here, above, left, right, u_in, rhs, fx, fy, fz, w, v_out,
                  u, c, cx, cy, cz, cw, cr, v, va):
    half = 0.5 * 0.0625
    for j in range(6):
        for source, upward, y in ((below, False, j), (above, True, 12 + j)):
            start, size, at = spread(j, upward)
            u[y, start : start + size] = source[at : at + size]
            c[y, start : start + size] = source[at + size : at + 2 * size]
        block = (left, here, right)[j // 2]
        u[6 + j] = block[2 * (j % 2)]
        c[6 + j] = block[2 * (j % 2) + 1]

    def coef(y):
        return c[y]

    cy[0] = half * (coef(0) + coef(1))
    for y in range(1, 17):
        k = coef(y)
        face_x = half * (k + pltpu.roll(k, 23, 0))
        face_z = half * (k + pltpu.roll(k, LANES - 1, 1))
        face_y = half * (k + coef(y + 1))
        diag = ABSORPTION + (
            face_x + pltpu.roll(face_x, 1, 0) + face_y + cy[y - 1] + face_z + pltpu.roll(face_z, 1, 1)
        )
        cx[y], cy[y], cz[y] = face_x, face_y, face_z
        cw[y] = DAMPING / diag
        cr[y] = u[y] * diag * (1.0 / DAMPING)
    for step in range(1, 8):
        now = u[step]
        low = cy[step - 1] * (u[step - 1] - now)
        for y in range(step, 18 - step):
            later = u[y + 1]
            high = cy[y] * (now - later)
            flux_x = cx[y] * (now - pltpu.roll(now, 23, 0))
            flux_z = cz[y] * (now - pltpu.roll(now, LANES - 1, 1))
            applied = ABSORPTION * now + (
                (high - low) + (flux_x - pltpu.roll(flux_x, 1, 0)) + (flux_z - pltpu.roll(flux_z, 1, 1))
            )
            u[y] = now + cw[y] * (cr[y] - applied)
            now, low = later, high
    v[...] = u_in[...]
    for x in range(12):
        for r in range(2):
            v[x, r, 0:1, :] = left[4, 2 * x + r : 2 * x + r + 1, :]
            v[x, r, 7:8, :] = right[4, 2 * x + r : 2 * x + r + 1, :]
    for x in range(6):
        rows = jnp.concatenate(
            [jnp.broadcast_to(u[7 + j, 7 + x : 8 + x, :], (2, LANES)) for j in range(4)], axis=0
        )
        for twin in range(2):
            for r in range(2):
                v[2 * x + twin, r] = v[2 * x + twin, r] + rows
    sweep_pass(10, v, 0, 0, rhs, 0, fx, fy, fz, w, va, 0, 10)
    sweep_pass(8, va, 0, 1, rhs, 1, fx, fy, fz, w, v_out, 0, 8)


def last_kernel(v_here, v_low, v_high, u0, g, fx, fy, fz, w, correction, residual, wide, ua, ub, res, held, left):
    for x in range(8):
        for r in range(2):
            rows = jnp.concatenate([v_low[x, r, 4:6], v_here[x, r, 2:6], v_high[x, r, 2:4]], axis=0)
            wide[x, r, pl.ds(0, 8, 2), :] = rows
            wide[x, r, pl.ds(1, 8, 2), :] = rows
    for i in range(14):
        fine = wide[(i + 1) // 2]
        ua[i] = u0[i] + jnp.stack([fine[0], fine[0], fine[1], fine[1]])
    sweep_pass(12, ua, 0, 0, g, 0, fx, fy, fz, w, ub, 0, 12)
    sweep_pass(10, ub, 0, 1, g, 1, fx, fy, fz, w, ua, 0, 10)
    matrix = permutation(True)

    def leave(index, source, at, out):
        rows = [
            jnp.concatenate([source[at + x, r, 4:12, :] for r in range(4)], axis=1) for x in range(8)
        ]
        held[index] = rearrange(jnp.concatenate(rows, axis=0), matrix).reshape(8, 8, 512)
        copy = pltpu.make_async_copy(held.at[index], out, left.at[index])
        copy.start()
        return copy

    first = leave(0, ua, 1, correction)
    sweep_pass(8, ua, 0, 2, g, 2, fx, fy, fz, w, res, 0, 8, last=True)
    second = leave(1, res, 0, residual)
    first.wait()
    second.wait()


VMEM = pl.BlockSpec(memory_space=pltpu.VMEM)
SMEM = pl.BlockSpec(memory_space=pltpu.SMEM)
HBM = pl.BlockSpec(memory_space=pltpu.HBM)


def call(kernel, outs, scratch, *arrays, scalars=0, to_hbm=False, extra=()):
    return pl.pallas_call(
        kernel,
        out_shape=[jax.ShapeDtypeStruct(shape, F32) for shape in outs],
        in_specs=[SMEM] * scalars + [VMEM] * (len(arrays) - scalars),
        out_specs=[HBM if to_hbm else VMEM] * len(outs),
        scratch_shapes=[pltpu.VMEM(shape, F32) for shape in scratch] + list(extra),
        compiler_params=pltpu.CompilerParams(vmem_limit_bytes=32 * 2**20),
    )(*arrays)


def shift(array, axis, by):
    count = lax.axis_size(axis)
    return lax.ppermute(array, axis, [(i, (i + by) % count) for i in range(count)])


def swap(array, axis, start):
    count = lax.axis_size(axis)
    pairs = [(i, (i + 1) % count) for i in range(start, count, 2)]
    return lax.ppermute(array, axis, pairs + [(j, i) for i, j in pairs])


def per_device(right_side, coefficient):
    me = lax.axis_index("gx").astype(jnp.int32).reshape(1)
    own, first, second = call(
        permute_kernel, [(16, 4, 8, 128), (9, 4, 8, 128), (9, 4, 8, 128)], [], me, jnp.stack([right_side, coefficient]),
        scalars=1,
    )
    first, second = swap(first, "gx", 1), swap(second, "gx", 0)
    wide, high, low = call(wide_kernel, [(34 * 32, 128), (ROWS, 128), (ROWS, 128)], [], me, own, first, second, scalars=1)
    low, high = shift(high, "gy", 1), shift(low, "gy", -1)
    fine = (4, 24, 128)
    count = lax.axis_size("gx")
    piece, u0, g, k = call(
        fine_kernel,
        [(count, 2, 4, 2, 8, 128), (14, *fine), (16 * 96, 128), (18 * 96, 128)],
        [(17, *fine), (16, *fine), (16, *fine), (16, *fine), (16, *fine), (8, *fine), (4, 2, 24, 128), (6, 2, 24, 128)],
        wide, low, high,
    )
    piece, u0, g, k, me = lax.optimization_barrier((piece, u0, g, k, me))
    gathered = lax.all_to_all(piece, "gx", 0, 0)
    gathered, u0, g, k, me = lax.optimization_barrier((gathered, u0, g, k, me))
    mid = (2, 8, 128)
    high, low, u1, rhs, fx, fy, fz, w = call(
        middle_kernel,
        [(5, 24, 128), (5, 24, 128), (12, *mid), (10, *mid), (11, *mid), (10, *mid), (10, *mid), (10, *mid)],
        [(44, *mid), (44, *mid), (43, *mid), (42, *mid), (42, *mid), (42, *mid), (42, *mid), (42, *mid), (40, *mid),
         (192, 128), (256, 128), (4, 32, 128), (32, 128)],
        me, gathered, scalars=1,
    )
    here = high
    low, high = shift(high, "gy", 1), shift(low, "gy", -1)
    far_high, far_low = call(three_kernel, [(160, 128), (160, 128)], [], here, low, high)
    below, above = shift(far_high, "gy", 3), shift(far_low, "gy", -3)
    last = (4, 16, 128)
    u0, g, *faces = call(
        prepare_kernel, [(14, *last), (12, *last), (13, *last), (12, *last), (12, *last), (12, *last)], [(14, *last)], u0, g, k
    )
    rows = (18, 24, 128)
    (v1,) = call(
        coarse_kernel, [(8, *mid)], [rows, rows, rows, rows, rows, rows, rows, (12, *mid), (10, *mid)],
        below, here, above, low, high, u1, rhs, fx, fy, fz, w,
    )
    low, high = shift(v1, "gy", 1), shift(v1, "gy", -1)
    return tuple(call(
        last_kernel, [(8, 8, 512), (8, 8, 512)],
        [(8, 2, 16, 128), (14, *last), (12, *last), (8, *last), (2, 8, 8, 512)],
        v1, low, high, u0, g, *faces, to_hbm=True, extra=[pltpu.SemaphoreType.DMA((2,))],
    ))


def solution(mesh):
    placed = (P("gx", "gy", None), P("gx", "gy", None))
    return jax.shard_map(per_device, mesh=mesh, in_specs=placed, out_specs=placed, check_vma=False)
```

```python
import jax
import jax.numpy as jnp
from jax import lax
from jax.experimental import pallas as pl
from jax.experimental.pallas import tpu as pltpu
from jax.sharding import PartitionSpec as P

ABSORPTION = 0.05
DAMPING = 0.8
F32 = jnp.float32
LANES = 128


def z_next(v):
    first = pltpu.roll(v[0], LANES - 1, 1)[None]
    return first if v.shape[0] == 1 else jnp.concatenate([v[1:], first], axis=0)


def z_prev(v):
    last = pltpu.roll(v[-1], 1, 1)[None]
    return last if v.shape[0] == 1 else jnp.concatenate([last, v[:-1]], axis=0)


def y_next(v):
    return pltpu.roll(v, v.shape[1] - 1, 1)


def y_prev(v):
    return pltpu.roll(v, 1, 1)


def flux_sum(u, u_next, flux_low, fx, fy, fz):
    flux_high = fx * (u - u_next)
    flux_y = fy * (u - y_next(u))
    flux_z = fz * (u - z_next(u))
    total = (flux_high - flux_low) + (flux_y - y_prev(flux_y)) + (flux_z - z_prev(flux_z))
    return ABSORPTION * u + total, flux_high


class Slabs:
    def __init__(self, flat, rows, parts=4):
        self.flat, self.rows, self.parts = flat, rows, parts

    def at(self, i):
        size = self.parts * self.rows
        return pl.ds(pl.multiple_of(i * size, 8), size)

    def __getitem__(self, i):
        return self.flat[self.at(i), :].reshape(self.parts, self.rows, LANES)

    def __setitem__(self, i, value):
        self.flat[self.at(i), :] = value.reshape(self.parts * self.rows, LANES)

    def part(self, i, start, size, step=1):
        where = lambda r: pl.ds((self.parts * i + r) * self.rows + start, size, step)
        return jnp.stack([self.flat[where(r), :] for r in range(self.parts)])

    def put(self, i, start, value):
        for r in range(self.parts):
            self.flat[pl.ds((self.parts * i + r) * self.rows + start, value.shape[1]), :] = value[r]


def loop(count, body, carry, unroll):
    return lax.fori_loop(0, count, body, carry, unroll=unroll)


def face_pass(count, k_ref, fx, fy, fz, w, scale, unroll, k_at=0):
    half = 0.5 * scale
    k0, k1 = k_ref[k_at], k_ref[k_at + 1]
    low = half * (k0 + k1)
    fx[0] = low

    def body(i, carry):
        k, low = carry
        k_next = k_ref[k_at + 2 + i]
        high = half * (k + k_next)
        face_y = half * (k + y_next(k))
        face_z = half * (k + z_next(k))
        diag = ABSORPTION + (high + low + face_y + y_prev(face_y) + face_z + z_prev(face_z))
        fx[i + 1] = high
        fy[i] = face_y
        fz[i] = face_z
        w[i] = DAMPING / diag
        return k_next, high

    loop(count, body, (k1, low), unroll)


def sweep_pass(count, u_ref, u_at, faces_at, g_ref, g_at, fx, fy, fz, w, out, out_at, unroll, last=False):
    u0, u1 = u_ref[u_at], u_ref[u_at + 1]
    low = fx[faces_at] * (u0 - u1)

    def body(i, carry):
        u, low = carry
        u_next = u_ref[u_at + 2 + i]
        f = faces_at + i
        applied, high = flux_sum(u, u_next, low, fx[f + 1], fy[f], fz[f])
        rest = g_ref[g_at + i] - applied
        out[out_at + i] = rest if last else u + w[f] * rest
        return u_next, high

    loop(count, body, (u1, low), unroll)


def permutation(inverse):
    z = lax.broadcasted_iota(jnp.int32, (512, 512), 1 if inverse else 0)
    at = lax.broadcasted_iota(jnp.int32, (512, 512), 0 if inverse else 1)
    return jnp.where(z == 4 * (at % LANES) + at // LANES, 1.0, 0.0).astype(jnp.bfloat16)


def rearrange(rows, matrix):
    count = rows.shape[0]
    top = rows.astype(jnp.bfloat16)
    rest = rows - top.astype(F32)
    middle = rest.astype(jnp.bfloat16)
    bottom = (rest - middle.astype(F32)).astype(jnp.bfloat16)
    parts = jnp.concatenate([top, middle, bottom], axis=0)
    moved = lax.dot_general(parts, matrix, (((1,), (0,)), ((), ())), preferred_element_type=F32)
    return (moved[0:count] + moved[count : 2 * count]) + moved[2 * count :]


def permute_kernel(me, held, own, to_first, to_second):
    matrix = permutation(False)
    moved = rearrange(held[...].reshape(128, 512), matrix)
    for x in range(16):
        for r in range(4):
            own[x, r] = moved[8 * x : 8 * x + 8, LANES * r : LANES * r + LANES]
    even = lax.rem(me[0], 2) == 0
    for take, high, low in ((even, to_second, to_first), (jnp.logical_not(even), to_first, to_second)):
        @pl.when(take)
        def _(high=high, low=low):
            high[0:6] = own[2:8]
            low[0:6] = own[0:6]
            high[6:14] = own[8:16]
            low[6:14] = own[8:16]


G_BORDER, K_BORDER = 6, 8
G_SLABS, K_SLABS = 8 + 2 * G_BORDER, 8 + 2 * K_BORDER
G_REACH = (5, 4, 3, 2, 1, 0)
K_REACH = (6, 6, 4, 4, 2, 1, 0)


def row_parts():
    at = 0
    for array, reaches, border in ((0, G_REACH, G_BORDER), (1, K_REACH, K_BORDER)):
        for d, reach in enumerate(reaches, 1):
            size = 4 * (8 + 2 * reach)
            yield array, d, border - reach, size, at
            at += size


ROWS = sum(part[3] for part in row_parts())


def wide_kernel(me, own, first, second, flat, to_high, to_low):
    out = Slabs(flat, 8)

    def put(at, source, start, size):
        for i in range(size):
            out[at + i] = source[start + i]

    put(6, own, 0, 8)
    put(28, own, 8, 8)
    even = lax.rem(me[0], 2) == 0
    for take, left, right in ((even, first, second), (jnp.logical_not(even), second, first)):
        @pl.when(take)
        def _(left=left, right=right):
            put(0, left, 0, 6)
            put(14, right, 0, 6)
            put(20, left, 6, 8)
            put(36, right, 6, 8)
    for array, d, column, size, at in row_parts():
        base = (G_SLABS * array + column) * 32
        to_high[at : at + size] = flat[pl.ds(base + 8 - d, size, 8), :]
        to_low[at : at + size] = flat[pl.ds(base + d - 1, size, 8), :]


def fine_kernel(me, own, low, high, piece, u0, g_flat, k_flat, u1, rhs, fx, fy, fz, w, uf, res, s1, sc,
                mx, my, mz, mw, mf, mr, ck):
    flats = g_flat, k_flat
    own, g, k = Slabs(own, 8), Slabs(g_flat, 24), Slabs(k_flat, 24)
    for i in range(G_SLABS):
        g.put(i, 8, own[i])
    for i in range(K_SLABS):
        k.put(i, 8, own[G_SLABS + i])
    for array, d, column, size, at in row_parts():
        flats[array][pl.ds(column * 96 + 8 - d, size, 24), :] = low[at : at + size]
        flats[array][pl.ds(column * 96 + 15 + d, size, 24), :] = high[at : at + size]
    face_pass(20, k, fx, fy, fz, w, 1.0, 20, k_at=1)

    def first(i, carry):
        uf[i] = w[i] * g[i]
        return carry

    loop(20, first, 0, 20)
    sweep_pass(18, uf, 0, 1, g, 1, fx, fy, fz, w, u0, 0, 18)
    sweep_pass(16, u0, 0, 2, g, 2, fx, fy, fz, w, res, 0, 16, last=True)
    for x in range(8):
        both = res[2 * x] + res[2 * x + 1]
        s1[x, 0] = both[0] + both[1]
        s1[x, 1] = both[2] + both[3]
    for x in range(10):
        both = k[2 + 2 * x] + k[3 + 2 * x]
        sc[x, 0] = both[0] + both[1]
        sc[x, 1] = both[2] + both[3]

    def rows(ref, x, start):
        return jnp.stack(
            [ref[x, r, pl.ds(start, 8, 2), :] + ref[x, r, pl.ds(start + 1, 8, 2), :] for r in range(2)]
        ) * 0.125

    half = 0.5 * 0.25
    k_mid = [rows(sc, x, 4) for x in range(10)]
    mx[0] = half * (k_mid[0] + k_mid[1])
    for x in range(8):
        here = k_mid[x + 1]
        face_x = half * (here + k_mid[x + 2])
        face_y = half * (here + rows(sc, x + 1, 6))
        face_z = half * (here + z_next(here))
        diag = ABSORPTION + (
            mx[x] + face_x + face_y + half * (here + rows(sc, x + 1, 2)) + face_z + z_prev(face_z)
        )
        mx[x + 1], my[x], mz[x] = face_x, face_y, face_z
        mw[x] = DAMPING / diag
        rhs[x] = rows(s1, x, 4)
        mf[x] = mw[x] * rhs[x]
    sweep_pass(6, mf, 0, 1, rhs, 1, mx, my, mz, mw, u1, 0, 6)
    sweep_pass(4, u1, 0, 2, rhs, 2, mx, my, mz, mw, mr, 0, 4, last=True)
    for x in range(4):
        both = k_mid[2 * x + 1] + k_mid[2 * x + 2]
        ck[x] = both[0] + both[1]
    k2 = [(ck[x, pl.ds(0, 4, 2), :] + ck[x, pl.ds(1, 4, 2), :]) * 0.125 for x in range(4)]
    half = 0.5 * 0.0625
    for x in range(2):
        here = k2[x + 1][1:3]
        face_z = half * (here + pltpu.roll(here, LANES - 1, 1))
        diag = ABSORPTION + (
            half * (here + k2[x][1:3]) + half * (here + k2[x + 2][1:3])
            + half * (here + k2[x + 1][0:2]) + half * (here + k2[x + 1][2:4])
            + face_z + pltpu.roll(face_z, 1, 1)
        )
        both = mr[2 * x] + mr[2 * x + 1]
        ck[x] = both[0] + both[1]
        first_sweep = DAMPING / diag * ((ck[x, pl.ds(2, 2, 2), :] + ck[x, pl.ds(3, 2, 2), :]) * 0.125)
        for to in range(piece.shape[0]):
            for j in range(2):
                piece[to, 2 * j + x : 2 * j + x + 1, :] = first_sweep[j : j + 1]
                piece[to, 4 + 2 * j + x : 5 + 2 * j + x, :] = here[j : j + 1]
    count = piece.shape[0]
    for to, column in ((lax.rem(me[0] + 1, count), 0), (lax.rem(me[0] + count - 1, count), 1)):
        for r in range(2):
            for x in range(3):
                at = 8 + 4 * (2 * x + r)
                piece[to, at : at + 4, :] = u1[column + x + 1, r, 2:6, :]
            piece[to, 32 + 4 * r : 36 + 4 * r, :] = rhs[column + 3, r, 2:6, :]


def prepare_middle_kernel(k_flat, fx, fy, fz, w, k_mid, sums):
    k = Slabs(k_flat, 24)
    for x in range(12):
        both = k[2 * x] + k[2 * x + 1]
        for r in range(2):
            sums[r] = both[2 * r] + both[2 * r + 1]
            k_mid[x, r] = (sums[r, pl.ds(4, 8, 2), :] + sums[r, pl.ds(5, 8, 2), :]) * 0.125
    face_pass(10, k_mid, fx, fy, fz, w, 0.25, 10)


def prepare_kernel(u0, g_flat, k_flat, u_out, g_out, fx, fy, fz, w, k_rows):
    g, k = Slabs(g_flat, 24), Slabs(k_flat, 24)
    for i in range(14):
        u_out[i] = u0[i + 2, :, 4:20, :]
        k_rows[i] = k.part(i + 5, 4, 16)
    for i in range(12):
        g_out[i] = g.part(i + 4, 4, 16)
    face_pass(12, k_rows, fx, fy, fz, w, 1.0, 12)


def middle_kernel(me, gathered, u1, rhs, send_high, send_low, u_flat, r_flat):
    count = gathered.shape[0]
    for block in range(11):
        source = lax.rem(me[0] + (block - 5 + count * 5), count)
        for j in range(2):
            for array in range(2):
                at = 4 * array + 2 * j
                pair = gathered[source, at : at + 2, :]
                for out in (send_high, send_low):
                    out[2 * j + array, 2 * block : 2 * block + 2, :] = pair
    u, g = Slabs(u_flat, 8, 2), Slabs(r_flat, 8, 2)
    for x in range(6):
        u[3 + x] = u1[x]
    for x in range(8):
        g[1 + x] = rhs[x]
    for source, column, edge in ((lax.rem(me[0] + count - 1, count), 0, 0), (lax.rem(me[0] + 1, count), 9, 9)):
        for r in range(2):
            for x in range(3):
                at = 8 + 4 * (2 * x + r)
                to = 8 * (2 * (column + x) + r) + 2
                u_flat[to : to + 4, :] = gathered[source, at : at + 4, :]
            to = 8 * (2 * edge + r) + 2
            r_flat[to : to + 4, :] = gathered[source, 32 + 4 * r : 36 + 4 * r, :]
    for out, row, rhs_row in ((send_high, 4, 5), (send_low, 2, 2)):
        out[4] = u_flat[pl.ds(row, 24, 8), :]
        out[5] = u_flat[pl.ds(row + 1, 24, 8), :]
        out[6, 0:20] = r_flat[pl.ds(rhs_row, 20, 8), :]


def spread(j, upward):
    d = j if upward else 5 - j
    start, size = (3, 16) if d < 4 else (7, 8)
    return start, size, 32 * d if d < 4 else 128 + 16 * (d - 4)


def three_kernel(me, here, low, high, to_first, to_second):
    blocks = (low, here, high)
    even = lax.rem(me[0], 2) == 0
    for take, to_high, to_low in ((even, to_second, to_first), (jnp.logical_not(even), to_first, to_second)):
        @pl.when(take)
        def _(to_high=to_high, to_low=to_low):
            for j in range(6):
                source = blocks[j // 2]
                for out, upward in ((to_high, False), (to_low, True)):
                    start, size, at = spread(j, upward)
                    for array in range(2):
                        out[at + size * array : at + size * array + size] = source[2 * (j % 2) + array, start : start + size]


def coarse_kernel(me, first, here, second, left, right, u_in, r_in, fx, fy, fz, w, v_out,
                  u, c, cx, cy, cz, cw, cr, v_flat, r_flat, va):
    half = 0.5 * 0.0625
    even = lax.rem(me[0], 2) == 0
    for take, below, above in ((even, first, second), (jnp.logical_not(even), second, first)):
        @pl.when(take)
        def _(below=below, above=above):
            for j in range(6):
                for source, upward, y in ((below, False, j), (above, True, 12 + j)):
                    start, size, at = spread(j, upward)
                    u[y, start : start + size] = source[at : at + size]
                    c[y, start : start + size] = source[at + size : at + 2 * size]
    for j in range(6):
        block = (left, here, right)[j // 2]
        u[6 + j] = block[2 * (j % 2)]
        c[6 + j] = block[2 * (j % 2) + 1]

    def coef(y):
        return c[y]

    cy[0] = half * (coef(0) + coef(1))
    for y in range(1, 17):
        k = coef(y)
        face_x = half * (k + pltpu.roll(k, 23, 0))
        face_z = half * (k + pltpu.roll(k, LANES - 1, 1))
        face_y = half * (k + coef(y + 1))
        diag = ABSORPTION + (
            face_x + pltpu.roll(face_x, 1, 0) + face_y + cy[y - 1] + face_z + pltpu.roll(face_z, 1, 1)
        )
        cx[y], cy[y], cz[y] = face_x, face_y, face_z
        cw[y] = DAMPING / diag
        cr[y] = u[y] * diag * (1.0 / DAMPING)
    for step in range(1, 8):
        now = u[step]
        low = cy[step - 1] * (u[step - 1] - now)
        for y in range(step, 18 - step):
            later = u[y + 1]
            high = cy[y] * (now - later)
            flux_x = cx[y] * (now - pltpu.roll(now, 23, 0))
            flux_z = cz[y] * (now - pltpu.roll(now, LANES - 1, 1))
            applied = ABSORPTION * now + (
                (high - low) + (flux_x - pltpu.roll(flux_x, 1, 0)) + (flux_z - pltpu.roll(flux_z, 1, 1))
            )
            u[y] = now + cw[y] * (cr[y] - applied)
            now, low = later, high
    v_flat[...] = u_in[...]
    r_flat[...] = r_in[...]
    for source, row, rhs_row in ((left, 0, 1), (right, 6, 6)):
        v_flat[pl.ds(row, 24, 8), :] = source[4]
        v_flat[pl.ds(row + 1, 24, 8), :] = source[5]
        r_flat[pl.ds(rhs_row, 20, 8), :] = source[6, 0:20]
    v, rhs = Slabs(v_flat, 8, 2), Slabs(r_flat, 8, 2)
    for x in range(6):
        rows = jnp.concatenate(
            [jnp.broadcast_to(u[7 + j, 8 + x : 9 + x, :], (2, LANES)) for j in range(4)], axis=0
        )
        for twin in range(2):
            v[2 * x + twin] = v[2 * x + twin] + rows[None]
    sweep_pass(10, v, 0, 0, rhs, 0, fx, fy, fz, w, va, 0, 10)
    sweep_pass(8, va, 0, 1, rhs, 1, fx, fy, fz, w, v_out, 0, 8)


def last_kernel(v_here, v_low, v_high, u0, g, fx, fy, fz, w, correction, residual, wide, ua, ub, res, held, left):
    for x in range(8):
        for r in range(2):
            rows = jnp.concatenate([v_low[x, r, 4:6], v_here[x, r, 2:6], v_high[x, r, 2:4]], axis=0)
            wide[x, r, pl.ds(0, 8, 2), :] = rows
            wide[x, r, pl.ds(1, 8, 2), :] = rows
    for i in range(14):
        fine = wide[(i + 1) // 2]
        ua[i] = u0[i] + jnp.stack([fine[0], fine[0], fine[1], fine[1]])
    sweep_pass(12, ua, 0, 0, g, 0, fx, fy, fz, w, ub, 0, 12)
    sweep_pass(10, ub, 0, 1, g, 1, fx, fy, fz, w, ua, 0, 10)
    matrix = permutation(True)

    def leave(index, source, at, out):
        rows = [
            jnp.concatenate([source[at + x, r, 4:12, :] for r in range(4)], axis=1) for x in range(8)
        ]
        held[index] = rearrange(jnp.concatenate(rows, axis=0), matrix).reshape(8, 8, 512)
        copy = pltpu.make_async_copy(held.at[index], out, left.at[index])
        copy.start()
        return copy

    first = leave(0, ua, 1, correction)
    sweep_pass(8, ua, 0, 2, g, 2, fx, fy, fz, w, res, 0, 8, last=True)
    second = leave(1, res, 0, residual)
    first.wait()
    second.wait()


VMEM = pl.BlockSpec(memory_space=pltpu.VMEM)
SMEM = pl.BlockSpec(memory_space=pltpu.SMEM)
HBM = pl.BlockSpec(memory_space=pltpu.HBM)


def call(kernel, outs, scratch, *arrays, scalars=0, to_hbm=False, extra=()):
    return pl.pallas_call(
        kernel,
        out_shape=[jax.ShapeDtypeStruct(shape, F32) for shape in outs],
        in_specs=[SMEM] * scalars + [VMEM] * (len(arrays) - scalars),
        out_specs=[HBM if to_hbm else VMEM] * len(outs),
        scratch_shapes=[pltpu.VMEM(shape, F32) for shape in scratch] + list(extra),
        compiler_params=pltpu.CompilerParams(vmem_limit_bytes=32 * 2**20),
    )(*arrays)


def shift(array, axis, by):
    count = lax.axis_size(axis)
    return lax.ppermute(array, axis, [(i, (i + by) % count) for i in range(count)])


def swap(array, axis, start, by=1):
    count = lax.axis_size(axis)
    pairs = [(i, (i + by) % count) for i in range(start, count, 2)]
    return lax.ppermute(array, axis, pairs + [(j, i) for i, j in pairs])


def per_device(right_side, coefficient):
    me_x = lax.axis_index("gx").astype(jnp.int32).reshape(1)
    me_y = lax.axis_index("gy").astype(jnp.int32).reshape(1)
    count = lax.axis_size("gx")
    border = (G_BORDER + K_BORDER, 4, 8, 128)
    own, first, second = call(
        permute_kernel, [(16, 4, 8, 128), border, border], [], me_x, jnp.stack([right_side, coefficient]), scalars=1
    )
    first, second = swap(first, "gx", 1), swap(second, "gx", 0)
    wide, high, low = call(
        wide_kernel, [((G_SLABS + K_SLABS) * 32, 128), (ROWS, 128), (ROWS, 128)], [], me_x, own, first, second, scalars=1
    )
    low, high = shift(high, "gy", 1), shift(low, "gy", -1)
    fine, mid, last = (4, 24, 128), (2, 8, 128), (4, 16, 128)
    piece, u0, g, k, u1, rhs = call(
        fine_kernel,
        [(count, 40, 128), (18, *fine), (G_SLABS * 96, 128), (K_SLABS * 96, 128), (6, *mid), (8, *mid)],
        [(21, *fine), (20, *fine), (20, *fine), (20, *fine), (20, *fine), (16, *fine), (8, 2, 24, 128), (10, 2, 24, 128),
         (9, *mid), (8, *mid), (8, *mid), (8, *mid), (8, *mid), (4, *mid), (4, 8, 128)],
        me_x, wide, low, high, scalars=1,
    )
    piece, u0, g, k, u1, rhs = lax.optimization_barrier((piece, u0, g, k, u1, rhs))
    gathered = lax.all_to_all(piece, "gx", 0, 0)
    gathered, u0, g, k, u1, rhs = lax.optimization_barrier((gathered, u0, g, k, u1, rhs))
    high, low, u1, rhs = call(
        middle_kernel, [(7, 24, 128), (7, 24, 128), (192, 128), (160, 128)], [], me_x, gathered, u1, rhs, scalars=1
    )
    here = high
    low, high = shift(high, "gy", 1), shift(low, "gy", -1)
    first, second = call(three_kernel, [(160, 128), (160, 128)], [], me_y, here, low, high, scalars=1)
    first, second = swap(first, "gy", 1, 3), swap(second, "gy", 0, 3)
    faces = call(
        prepare_middle_kernel, [(11, *mid), (10, *mid), (10, *mid), (10, *mid)], [(12, *mid), (2, 24, 128)], k
    )
    rows = (18, 24, 128)
    (v1,) = call(
        coarse_kernel, [(8, *mid)], [rows, rows, rows, rows, rows, rows, rows, (192, 128), (160, 128), (10, *mid)],
        me_y, first, here, second, low, high, u1, rhs, *faces, scalars=1,
    )
    u0, g, *faces = call(
        prepare_kernel, [(14, *last), (12, *last), (13, *last), (12, *last), (12, *last), (12, *last)], [(14, *last)], u0, g, k
    )
    low, high = shift(v1, "gy", 1), shift(v1, "gy", -1)
    return tuple(call(
        last_kernel, [(8, 8, 512), (8, 8, 512)],
        [(8, 2, 16, 128), (14, *last), (12, *last), (8, *last), (2, 8, 8, 512)],
        v1, low, high, u0, g, *faces, to_hbm=True, extra=[pltpu.SemaphoreType.DMA((2,))],
    ))


def solution(mesh):
    placed = (P("gx", "gy", None), P("gx", "gy", None))
    return jax.shard_map(per_device, mesh=mesh, in_specs=placed, out_specs=placed, check_vma=False)
```

```python
import jax
import jax.numpy as jnp
from jax import lax
from jax.experimental import pallas as pl
from jax.experimental.pallas import tpu as pltpu
from jax.sharding import PartitionSpec as P

ABSORPTION = 0.05
DAMPING = 0.8
F32 = jnp.float32
LANES = 128


def z_next(v):
    first = pltpu.roll(v[0], LANES - 1, 1)[None]
    return first if v.shape[0] == 1 else jnp.concatenate([v[1:], first], axis=0)


def z_prev(v):
    last = pltpu.roll(v[-1], 1, 1)[None]
    return last if v.shape[0] == 1 else jnp.concatenate([last, v[:-1]], axis=0)


def y_next(v):
    return pltpu.roll(v, v.shape[1] - 1, 1)


def y_prev(v):
    return pltpu.roll(v, 1, 1)


def flux_sum(u, u_next, flux_low, fx, fy, fz):
    flux_high = fx * (u - u_next)
    flux_y = fy * (u - y_next(u))
    flux_z = fz * (u - z_next(u))
    total = (flux_high - flux_low) + (flux_y - y_prev(flux_y)) + (flux_z - z_prev(flux_z))
    return ABSORPTION * u + total, flux_high


class Slabs:
    def __init__(self, flat, rows, parts=4):
        self.flat, self.rows, self.parts = flat, rows, parts

    def at(self, i):
        size = self.parts * self.rows
        return pl.ds(pl.multiple_of(i * size, 8), size)

    def __getitem__(self, i):
        return self.flat[self.at(i), :].reshape(self.parts, self.rows, LANES)

    def __setitem__(self, i, value):
        self.flat[self.at(i), :] = value.reshape(self.parts * self.rows, LANES)

    def part(self, i, start, size, step=1):
        where = lambda r: pl.ds((self.parts * i + r) * self.rows + start, size, step)
        return jnp.stack([self.flat[where(r), :] for r in range(self.parts)])

    def put(self, i, start, value):
        for r in range(self.parts):
            self.flat[pl.ds((self.parts * i + r) * self.rows + start, value.shape[1]), :] = value[r]


def loop(count, body, carry, unroll):
    return lax.fori_loop(0, count, body, carry, unroll=unroll)


def face_pass(count, k_ref, fx, fy, fz, w, scale, unroll, k_at=0):
    half = 0.5 * scale
    k0, k1 = k_ref[k_at], k_ref[k_at + 1]
    low = half * (k0 + k1)
    fx[0] = low

    def body(i, carry):
        k, low = carry
        k_next = k_ref[k_at + 2 + i]
        high = half * (k + k_next)
        face_y = half * (k + y_next(k))
        face_z = half * (k + z_next(k))
        diag = ABSORPTION + (high + low + face_y + y_prev(face_y) + face_z + z_prev(face_z))
        fx[i + 1] = high
        fy[i] = face_y
        fz[i] = face_z
        w[i] = DAMPING / diag
        return k_next, high

    loop(count, body, (k1, low), unroll)


def sweep_pass(count, u_ref, u_at, faces_at, g_ref, g_at, fx, fy, fz, w, out, out_at, unroll, last=False):
    u0, u1 = u_ref[u_at], u_ref[u_at + 1]
    low = fx[faces_at] * (u0 - u1)

    def body(i, carry):
        u, low = carry
        u_next = u_ref[u_at + 2 + i]
        f = faces_at + i
        applied, high = flux_sum(u, u_next, low, fx[f + 1], fy[f], fz[f])
        rest = g_ref[g_at + i] - applied
        out[out_at + i] = rest if last else u + w[f] * rest
        return u_next, high

    loop(count, body, (u1, low), unroll)


def permutation(inverse):
    z = lax.broadcasted_iota(jnp.int32, (512, 512), 1 if inverse else 0)
    at = lax.broadcasted_iota(jnp.int32, (512, 512), 0 if inverse else 1)
    return jnp.where(z == 4 * (at % LANES) + at // LANES, 1.0, 0.0).astype(jnp.bfloat16)


def rearrange(rows, matrix):
    count = rows.shape[0]
    top = rows.astype(jnp.bfloat16)
    rest = rows - top.astype(F32)
    middle = rest.astype(jnp.bfloat16)
    bottom = (rest - middle.astype(F32)).astype(jnp.bfloat16)
    parts = jnp.concatenate([top, middle, bottom], axis=0)
    moved = lax.dot_general(parts, matrix, (((1,), (0,)), ((), ())), preferred_element_type=F32)
    return (moved[0:count] + moved[count : 2 * count]) + moved[2 * count :]


def permute_kernel(me, held, own_flat, to_first, to_second):
    matrix = permutation(False)
    moved = rearrange(held[...].reshape(128, 512), matrix)
    for x in range(16):
        for r in range(4):
            own_flat[32 * x + 8 * r : 32 * x + 8 * r + 8] = moved[8 * x : 8 * x + 8, LANES * r : LANES * r + LANES]
    own = Slabs(own_flat, 8)
    even = lax.rem(me[0], 2) == 0
    for take, high, low in ((even, to_second, to_first), (jnp.logical_not(even), to_first, to_second)):
        @pl.when(take)
        def _(high=high, low=low):
            for i in range(6):
                high[i] = own[2 + i]
                low[i] = own[i]
            for i in range(6, 14):
                high[i] = own[2 + i]
                low[i] = own[2 + i]


G_BORDER, K_BORDER = 6, 8
G_SLABS, K_SLABS = 8 + 2 * G_BORDER, 8 + 2 * K_BORDER
G_REACH = (5, 4, 3, 2, 1, 0)
K_REACH = (6, 6, 4, 4, 2, 1, 0)


def row_parts():
    for array, reaches, border in ((0, G_REACH, G_BORDER), (1, K_REACH, K_BORDER)):
        for d, reach in enumerate(reaches, 1):
            yield array, d, reach, border


FACE_ROWS = 32 * (len(G_REACH) + len(K_REACH))
CORNER_ROWS = 8 * (sum(G_REACH) + sum(K_REACH))


def face_kernel(own, to_high, to_low):
    for i, (array, d, _, _) in enumerate(row_parts()):
        for out, y in ((to_high, 8 - d), (to_low, d - 1)):
            out[32 * i : 32 * i + 32] = own[pl.ds(256 * array + y, 32, 8), :]


def corners():
    at = 0
    for array, d, reach, border in row_parts():
        for column in (border - reach, border + 8):
            if reach:
                yield array, d, column, 4 * reach, at
                at += 4 * reach


def wide_kernel(me, own, first, second, flat, to_high, to_low):
    out, own = Slabs(flat, 8), Slabs(own, 8)

    def put(at, source, start, size):
        for i in range(size):
            out[at + i] = source[start + i]

    put(6, own, 0, 8)
    put(28, own, 8, 8)
    even = lax.rem(me[0], 2) == 0
    for take, left, right in ((even, first, second), (jnp.logical_not(even), second, first)):
        @pl.when(take)
        def _(left=left, right=right):
            put(0, left, 0, 6)
            put(14, right, 0, 6)
            put(20, left, 6, 8)
            put(36, right, 6, 8)
    for array, d, column, size, at in corners():
        base = (G_SLABS * array + column) * 32
        to_high[at : at + size] = flat[pl.ds(base + 8 - d, size, 8), :]
        to_low[at : at + size] = flat[pl.ds(base + d - 1, size, 8), :]


def fine_kernel(me, own, low, high, low_corners, high_corners, piece, u0, g_flat, k_flat, u1, rhs, fx, fy, fz, w, uf, res, s1, sc,
                mx, my, mz, mw, mf, mr, ck):
    flats = g_flat, k_flat
    own, g, k = Slabs(own, 8), Slabs(g_flat, 24), Slabs(k_flat, 24)
    for i in range(G_SLABS):
        g.put(i, 8, own[i])
    for i in range(K_SLABS):
        k.put(i, 8, own[G_SLABS + i])
    for i, (array, d, _, border) in enumerate(row_parts()):
        flats[array][pl.ds(border * 96 + 8 - d, 32, 24), :] = low[32 * i : 32 * i + 32]
        flats[array][pl.ds(border * 96 + 15 + d, 32, 24), :] = high[32 * i : 32 * i + 32]
    for array, d, column, size, at in corners():
        flats[array][pl.ds(column * 96 + 8 - d, size, 24), :] = low_corners[at : at + size]
        flats[array][pl.ds(column * 96 + 15 + d, size, 24), :] = high_corners[at : at + size]
    face_pass(20, k, fx, fy, fz, w, 1.0, 20, k_at=1)

    def first(i, carry):
        uf[i] = w[i] * g[i]
        return carry

    loop(20, first, 0, 20)
    sweep_pass(18, uf, 0, 1, g, 1, fx, fy, fz, w, u0, 0, 18)
    sweep_pass(16, u0, 0, 2, g, 2, fx, fy, fz, w, res, 0, 16, last=True)
    for x in range(8):
        both = res[2 * x] + res[2 * x + 1]
        s1[x, 0] = both[0] + both[1]
        s1[x, 1] = both[2] + both[3]
    for x in range(10):
        both = k[2 + 2 * x] + k[3 + 2 * x]
        sc[x, 0] = both[0] + both[1]
        sc[x, 1] = both[2] + both[3]

    def rows(ref, x, start):
        return jnp.stack(
            [ref[x, r, pl.ds(start, 8, 2), :] + ref[x, r, pl.ds(start + 1, 8, 2), :] for r in range(2)]
        ) * 0.125

    half = 0.5 * 0.25
    k_mid = [rows(sc, x, 4) for x in range(10)]
    mx[0] = half * (k_mid[0] + k_mid[1])
    for x in range(8):
        here = k_mid[x + 1]
        face_x = half * (here + k_mid[x + 2])
        face_y = half * (here + rows(sc, x + 1, 6))
        face_z = half * (here + z_next(here))
        diag = ABSORPTION + (
            mx[x] + face_x + face_y + half * (here + rows(sc, x + 1, 2)) + face_z + z_prev(face_z)
        )
        mx[x + 1], my[x], mz[x] = face_x, face_y, face_z
        mw[x] = DAMPING / diag
        rhs[x] = rows(s1, x, 4)
        mf[x] = mw[x] * rhs[x]
    sweep_pass(6, mf, 0, 1, rhs, 1, mx, my, mz, mw, u1, 0, 6)
    sweep_pass(4, u1, 0, 2, rhs, 2, mx, my, mz, mw, mr, 0, 4, last=True)
    for x in range(4):
        both = k_mid[2 * x + 1] + k_mid[2 * x + 2]
        ck[x] = both[0] + both[1]
    k2 = [(ck[x, pl.ds(0, 4, 2), :] + ck[x, pl.ds(1, 4, 2), :]) * 0.125 for x in range(4)]
    half = 0.5 * 0.0625
    for x in range(2):
        here = k2[x + 1][1:3]
        face_z = half * (here + pltpu.roll(here, LANES - 1, 1))
        diag = ABSORPTION + (
            half * (here + k2[x][1:3]) + half * (here + k2[x + 2][1:3])
            + half * (here + k2[x + 1][0:2]) + half * (here + k2[x + 1][2:4])
            + face_z + pltpu.roll(face_z, 1, 1)
        )
        both = mr[2 * x] + mr[2 * x + 1]
        ck[x] = both[0] + both[1]
        first_sweep = DAMPING / diag * ((ck[x, pl.ds(2, 2, 2), :] + ck[x, pl.ds(3, 2, 2), :]) * 0.125)
        for j in range(2):
            ck[3, 2 * j + x : 2 * j + x + 1, :] = first_sweep[j : j + 1]
            ck[3, 4 + 2 * j + x : 5 + 2 * j + x, :] = here[j : j + 1]
    level_2 = ck[3]
    for to in range(piece.shape[0]):
        piece[to, 0:8, :] = level_2
    count = piece.shape[0]
    for to, column in ((lax.rem(me[0] + 1, count), 0), (lax.rem(me[0] + count - 1, count), 1)):
        for r in range(2):
            for x in range(3):
                at = 8 + 4 * (2 * x + r)
                piece[to, at : at + 4, :] = u1[column + x + 1, r, 2:6, :]
            piece[to, 32 + 4 * r : 36 + 4 * r, :] = rhs[column + 3, r, 2:6, :]


def prepare_middle_kernel(k_flat, fx, fy, fz, w, k_mid, sums):
    k = Slabs(k_flat, 24)
    for x in range(12):
        both = k[2 * x] + k[2 * x + 1]
        for r in range(2):
            sums[r] = both[2 * r] + both[2 * r + 1]
            k_mid[x, r] = (sums[r, pl.ds(4, 8, 2), :] + sums[r, pl.ds(5, 8, 2), :]) * 0.125
    face_pass(10, k_mid, fx, fy, fz, w, 0.25, 10)


def prepare_kernel(u0, g_flat, k_flat, u_out, g_out, fx, fy, fz, w, k_rows):
    g, k = Slabs(g_flat, 24), Slabs(k_flat, 24)
    for i in range(14):
        u_out[i] = u0[i + 2, :, 4:20, :]
        k_rows[i] = k.part(i + 5, 4, 16)
    for i in range(12):
        g_out[i] = g.part(i + 4, 4, 16)
    face_pass(12, k_rows, fx, fy, fz, w, 1.0, 12)


def middle_kernel(me, gathered, u1, rhs, send, level_1):
    count = gathered.shape[0]
    for block in range(11):
        source = lax.rem(me[0] + (block - 5 + count * 5), count)
        for j in range(2):
            for array in range(2):
                at = 4 * array + 2 * j
                send[2 * j + array, 2 * block : 2 * block + 2, :] = gathered[source, at : at + 2, :]
    u_flat, r_flat = level_1.at[0:192], level_1.at[192:352]
    u, g = Slabs(u_flat, 8, 2), Slabs(r_flat, 8, 2)
    for x in range(6):
        u[3 + x] = u1[x]
    for x in range(8):
        g[1 + x] = rhs[x]
    for source, column, edge in ((lax.rem(me[0] + count - 1, count), 0, 0), (lax.rem(me[0] + 1, count), 9, 9)):
        for r in range(2):
            for x in range(3):
                at = 8 + 4 * (2 * x + r)
                to = 8 * (2 * (column + x) + r) + 2
                u_flat[to : to + 4, :] = gathered[source, at : at + 4, :]
            to = 8 * (2 * edge + r) + 2
            r_flat[to : to + 4, :] = gathered[source, 32 + 4 * r : 36 + 4 * r, :]
    for row in range(4):
        send[4 + row] = u_flat[pl.ds(2 + row, 24, 8), :]
    send[8, 0:20] = r_flat[pl.ds(2, 20, 8), :]
    send[9, 0:20] = r_flat[pl.ds(5, 20, 8), :]


SPREAD = (16, 14, 12, 10, 8, 6)


def spread(j, upward):
    d = j if upward else 5 - j
    return 3 + d, SPREAD[d], 2 * sum(SPREAD[:d])


def three_kernel(me, here, low, high, to_first, to_second):
    blocks = (low, here, high)
    even = lax.rem(me[0], 2) == 0
    for take, to_high, to_low in ((even, to_second, to_first), (jnp.logical_not(even), to_first, to_second)):
        @pl.when(take)
        def _(to_high=to_high, to_low=to_low):
            for j in range(6):
                source = blocks[j // 2]
                for out, upward in ((to_high, False), (to_low, True)):
                    start, size, at = spread(j, upward)
                    for array in range(2):
                        out[at + size * array : at + size * array + size] = source[2 * (j % 2) + array, start : start + size]


def coarse_kernel(me, first, here, second, left, right, level_1, fx, fy, fz, w, v_flat_out, to_high, to_low,
                  u, c, start, cy, weights, v_flat, r_flat, va):
    half = 0.5 * 0.0625
    even = lax.rem(me[0], 2) == 0
    for take, below, above in ((even, first, second), (jnp.logical_not(even), second, first)):
        @pl.when(take)
        def _(below=below, above=above):
            for j in range(6):
                for source, upward, y in ((below, False, j), (above, True, 12 + j)):
                    column, size, at = spread(j, upward)
                    start[y, column : column + size] = source[at : at + size]
                    c[y, column : column + size] = source[at + size : at + 2 * size]
    for j in range(6):
        block = (left, here, right)[j // 2]
        start[6 + j] = block[2 * (j % 2)]
        c[6 + j] = block[2 * (j % 2) + 1]
    cy[0] = half * (c[0] + c[1])
    for y in range(18):
        u[y] = start[y]
    for y in range(1, 17):
        k = c[y]
        right_x = half * (k + pltpu.roll(k, 23, 0))
        right_z = half * (k + pltpu.roll(k, LANES - 1, 1))
        right_y = half * (k + c[y + 1])
        left_x, left_z, left_y = pltpu.roll(right_x, 1, 0), pltpu.roll(right_z, 1, 1), cy[y - 1]
        cy[y] = right_y
        scale = DAMPING / (ABSORPTION + (right_x + left_x + right_y + left_y + right_z + left_z))
        for i, face in enumerate((right_x, left_x, right_y, left_y, right_z, left_z)):
            weights[i, y] = scale * face
    for step in range(1, 8):
        before, now = u[step - 1], u[step]
        for y in range(step, 18 - step):
            later = u[y + 1]
            along_x = weights[0, y] * pltpu.roll(now, 23, 0) + weights[1, y] * pltpu.roll(now, 1, 0)
            along_y = weights[2, y] * later + weights[3, y] * before
            along_z = weights[4, y] * pltpu.roll(now, LANES - 1, 1) + weights[5, y] * pltpu.roll(now, 1, 1)
            u[y] = ((1.0 - DAMPING) * now + start[y]) + along_y + (along_x + along_z)
            before, now = now, later
    v_flat[...] = level_1[0:192]
    r_flat[...] = level_1[192:352]
    for source, row, slab, rhs_row, rhs_slab in ((left, 0, 6, 1, 9), (right, 6, 4, 6, 8)):
        v_flat[pl.ds(row, 24, 8), :] = source[slab]
        v_flat[pl.ds(row + 1, 24, 8), :] = source[slab + 1]
        r_flat[pl.ds(rhs_row, 20, 8), :] = source[rhs_slab, 0:20]
    v, rhs = Slabs(v_flat, 8, 2), Slabs(r_flat, 8, 2)
    for x in range(6):
        rows = jnp.concatenate(
            [jnp.broadcast_to(u[7 + j, 8 + x : 9 + x, :], (2, LANES)) for j in range(4)], axis=0
        )
        for twin in range(2):
            v[2 * x + twin] = v[2 * x + twin] + rows[None]
    sweep_pass(10, v, 0, 0, rhs, 0, fx, fy, fz, w, va, 0, 10)
    sweep_pass(8, va, 0, 1, rhs, 1, fx, fy, fz, w, Slabs(v_flat_out, 8, 2), 0, 8)
    for out, row in ((to_high, 4), (to_low, 2)):
        for i in range(2):
            out[16 * i : 16 * i + 16] = v_flat_out[pl.ds(row + i, 16, 8), :]


def last_kernel(v_here, v_low, v_high, u0, g, fx, fy, fz, w, correction, residual, v_flat, wide, ua, ub, res, held, left):
    v_flat[...] = v_here[...]
    for source, row in ((v_low, 0), (v_high, 6)):
        for i in range(2):
            v_flat[pl.ds(row + i, 16, 8), :] = source[16 * i : 16 * i + 16]
    for x in range(8):
        for r in range(2):
            rows = v_flat[8 * (2 * x + r) : 8 * (2 * x + r) + 8]
            wide[x, r, pl.ds(0, 8, 2), :] = rows
            wide[x, r, pl.ds(1, 8, 2), :] = rows
    for i in range(14):
        fine = wide[(i + 1) // 2]
        ua[i] = u0[i] + jnp.stack([fine[0], fine[0], fine[1], fine[1]])
    sweep_pass(12, ua, 0, 0, g, 0, fx, fy, fz, w, ub, 0, 12)
    sweep_pass(10, ub, 0, 1, g, 1, fx, fy, fz, w, ua, 0, 10)
    matrix = permutation(True)

    def leave(index, source, at, out):
        rows = [
            jnp.concatenate([source[at + x, r, 4:12, :] for r in range(4)], axis=1) for x in range(8)
        ]
        held[index] = rearrange(jnp.concatenate(rows, axis=0), matrix).reshape(8, 8, 512)
        copy = pltpu.make_async_copy(held.at[index], out, left.at[index])
        copy.start()
        return copy

    first = leave(0, ua, 1, correction)
    sweep_pass(8, ua, 0, 2, g, 2, fx, fy, fz, w, res, 0, 8, last=True)
    second = leave(1, res, 0, residual)
    first.wait()
    second.wait()


VMEM = pl.BlockSpec(memory_space=pltpu.VMEM)
SMEM = pl.BlockSpec(memory_space=pltpu.SMEM)
HBM = pl.BlockSpec(memory_space=pltpu.HBM)


def call(kernel, outs, scratch, *arrays, scalars=0, to_hbm=False, extra=()):
    return pl.pallas_call(
        kernel,
        out_shape=[jax.ShapeDtypeStruct(shape, F32) for shape in outs],
        in_specs=[SMEM] * scalars + [VMEM] * (len(arrays) - scalars),
        out_specs=[HBM if to_hbm else VMEM] * len(outs),
        scratch_shapes=[pltpu.VMEM(shape, F32) for shape in scratch] + list(extra),
        compiler_params=pltpu.CompilerParams(vmem_limit_bytes=32 * 2**20),
    )(*arrays)


def shift(array, axis, by):
    count = lax.axis_size(axis)
    return lax.ppermute(array, axis, [(i, (i + by) % count) for i in range(count)])


def swap(array, axis, start, by=1):
    count = lax.axis_size(axis)
    pairs = [(i, (i + by) % count) for i in range(start, count, 2)]
    return lax.ppermute(array, axis, pairs + [(j, i) for i, j in pairs])


def per_device(right_side, coefficient):
    me_x = lax.axis_index("gx").astype(jnp.int32).reshape(1)
    me_y = lax.axis_index("gy").astype(jnp.int32).reshape(1)
    count = lax.axis_size("gx")
    border = (G_BORDER + K_BORDER, 4, 8, 128)
    own, first, second = call(
        permute_kernel, [(512, 128), border, border], [], me_x, jnp.stack([right_side, coefficient]), scalars=1
    )
    first, second = swap(first, "gx", 1), swap(second, "gx", 0)
    high, low = call(face_kernel, [(FACE_ROWS, 128), (FACE_ROWS, 128)], [], own)
    low, high = shift(high, "gy", 1), shift(low, "gy", -1)
    wide, high_corners, low_corners = call(
        wide_kernel, [((G_SLABS + K_SLABS) * 32, 128), (CORNER_ROWS, 128), (CORNER_ROWS, 128)], [],
        me_x, own, first, second, scalars=1,
    )
    low_corners, high_corners = shift(high_corners, "gy", 1), shift(low_corners, "gy", -1)
    fine, mid, last = (4, 24, 128), (2, 8, 128), (4, 16, 128)
    piece, u0, g, k, u1, rhs = call(
        fine_kernel,
        [(count, 40, 128), (18, *fine), (G_SLABS * 96, 128), (K_SLABS * 96, 128), (6, *mid), (8, *mid)],
        [(21, *fine), (20, *fine), (20, *fine), (20, *fine), (20, *fine), (16, *fine), (8, 2, 24, 128), (10, 2, 24, 128),
         (9, *mid), (8, *mid), (8, *mid), (8, *mid), (8, *mid), (4, *mid), (4, 8, 128)],
        me_x, wide, low, high, low_corners, high_corners, scalars=1,
    )
    piece, u0, g, k, u1, rhs = lax.optimization_barrier((piece, u0, g, k, u1, rhs))
    gathered = lax.all_to_all(piece, "gx", 0, 0)
    gathered, u0, g, k, u1, rhs = lax.optimization_barrier((gathered, u0, g, k, u1, rhs))
    here, level_1 = call(
        middle_kernel, [(10, 24, 128), (352, 128)], [], me_x, gathered, u1, rhs, scalars=1
    )
    low, high = shift(here, "gy", 1), shift(here, "gy", -1)
    first, second = call(three_kernel, [(136, 128), (136, 128)], [], me_y, here, low, high, scalars=1)
    first, second = swap(first, "gy", 1, 3), swap(second, "gy", 0, 3)
    faces = call(
        prepare_middle_kernel, [(11, *mid), (10, *mid), (10, *mid), (10, *mid)], [(12, *mid), (2, 24, 128)], k
    )
    rows = (18, 24, 128)
    v1, high_rows, low_rows = call(
        coarse_kernel, [(128, 128), (32, 128), (32, 128)],
        [rows, rows, rows, rows, (6, *rows), (192, 128), (160, 128), (10, *mid)],
        me_y, first, here, second, low, high, level_1, *faces, scalars=1,
    )
    u0, g, *faces = call(
        prepare_kernel, [(14, *last), (12, *last), (13, *last), (12, *last), (12, *last), (12, *last)], [(14, *last)], u0, g, k
    )
    low, high = shift(high_rows, "gy", 1), shift(low_rows, "gy", -1)
    return tuple(call(
        last_kernel, [(8, 8, 512), (8, 8, 512)],
        [(128, 128), (8, 2, 16, 128), (14, *last), (12, *last), (8, *last), (2, 8, 8, 512)],
        v1, low, high, u0, g, *faces, to_hbm=True, extra=[pltpu.SemaphoreType.DMA((2,))],
    ))


def solution(mesh):
    placed = (P("gx", "gy", None), P("gx", "gy", None))
    return jax.shard_map(per_device, mesh=mesh, in_specs=placed, out_specs=placed, check_vma=False)
```

```python
import jax
import jax.numpy as jnp
from jax import lax
from jax.experimental import pallas as pl
from jax.experimental.pallas import tpu as pltpu
from jax.sharding import PartitionSpec as P

ABSORPTION = 0.05
DAMPING = 0.8
F32 = jnp.float32
LANES = 128


def z_next(v):
    first = pltpu.roll(v[0], LANES - 1, 1)[None]
    return first if v.shape[0] == 1 else jnp.concatenate([v[1:], first], axis=0)


def z_prev(v):
    last = pltpu.roll(v[-1], 1, 1)[None]
    return last if v.shape[0] == 1 else jnp.concatenate([last, v[:-1]], axis=0)


def y_next(v):
    return pltpu.roll(v, v.shape[1] - 1, 1)


def y_prev(v):
    return pltpu.roll(v, 1, 1)


def flux_sum(u, u_next, flux_low, fx, fy, fz):
    flux_high = fx * (u - u_next)
    flux_y = fy * (u - y_next(u))
    flux_z = fz * (u - z_next(u))
    total = (flux_high - flux_low) + (flux_y - y_prev(flux_y)) + (flux_z - z_prev(flux_z))
    return ABSORPTION * u + total, flux_high


class Slabs:
    def __init__(self, flat, rows, parts=4):
        self.flat, self.rows, self.parts = flat, rows, parts

    def at(self, i):
        size = self.parts * self.rows
        return pl.ds(i * size, size)

    def __getitem__(self, i):
        return self.flat[self.at(i), :].reshape(self.parts, self.rows, LANES)

    def __setitem__(self, i, value):
        self.flat[self.at(i), :] = value.reshape(self.parts * self.rows, LANES)

    def part(self, i, start, size, step=1):
        where = lambda r: pl.ds((self.parts * i + r) * self.rows + start, size, step)
        return jnp.stack([self.flat[where(r), :] for r in range(self.parts)])

    def put(self, i, start, value):
        for r in range(self.parts):
            self.flat[pl.ds((self.parts * i + r) * self.rows + start, value.shape[1]), :] = value[r]


class Parted:
    def __init__(self, inner, outer, start, stop):
        self.inner, self.outer, self.start, self.stop = inner, outer, start, stop

    def place(self, i):
        if self.start <= i < self.stop:
            return self.inner, i - self.start
        return self.outer, i if i < self.start else i - (self.stop - self.start)

    def __getitem__(self, i):
        buffer, at = self.place(i)
        return buffer[at]

    def __setitem__(self, i, value):
        buffer, at = self.place(i)
        buffer[at] = value

    def part(self, i, start, size):
        buffer, at = self.place(i)
        if isinstance(buffer, (Parted, Slabs)):
            return buffer.part(at, start, size)
        return buffer[at, :, start : start + size, :]


def face_pass(count, k_ref, fx, fy, fz, w, scale, k_at=0, done=()):
    half = 0.5 * scale
    for i in range(count + 1):
        if i not in done or i - 1 not in done:
            fx[i] = half * (k_ref[k_at + i] + k_ref[k_at + 1 + i])
        if i == 0 or i - 1 in done:
            continue
        k = k_ref[k_at + i]
        face_y = half * (k + y_next(k))
        face_z = half * (k + z_next(k))
        diag = ABSORPTION + (fx[i] + fx[i - 1] + face_y + y_prev(face_y) + face_z + z_prev(face_z))
        fy[i - 1] = face_y
        fz[i - 1] = face_z
        w[i - 1] = DAMPING / diag


def sweep_pass(count, u_ref, u_at, faces_at, g_ref, g_at, fx, fy, fz, w, out, out_at, last=False, done=()):
    low = None
    for i in range(count):
        if i in done:
            low = None
            continue
        u, u_next, f = u_ref[u_at + 1 + i], u_ref[u_at + 2 + i], faces_at + i
        if low is None:
            low = fx[f] * (u_ref[u_at + i] - u)
        applied, low = flux_sum(u, u_next, low, fx[f + 1], fy[f], fz[f])
        rest = g_ref[g_at + i] - applied
        out[out_at + i] = rest if last else u + w[f] * rest


def permutation(inverse):
    z = lax.broadcasted_iota(jnp.int32, (512, 512), 1 if inverse else 0)
    at = lax.broadcasted_iota(jnp.int32, (512, 512), 0 if inverse else 1)
    return jnp.where(z == 4 * (at % LANES) + at // LANES, 1.0, 0.0).astype(jnp.bfloat16)


def rearrange(rows, matrix):
    count = rows.shape[0]
    top = rows.astype(jnp.bfloat16)
    rest = rows - top.astype(F32)
    middle = rest.astype(jnp.bfloat16)
    bottom = (rest - middle.astype(F32)).astype(jnp.bfloat16)
    parts = jnp.concatenate([top, middle, bottom], axis=0)
    moved = lax.dot_general(parts, matrix, (((1,), (0,)), ((), ())), preferred_element_type=F32)
    return (moved[0:count] + moved[count : 2 * count]) + moved[2 * count :]


def permute_kernel(me, held, own_flat, to_first, to_second):
    matrix = permutation(False)
    moved = rearrange(held[...].reshape(128, 512), matrix)
    for x in range(16):
        for r in range(4):
            own_flat[32 * x + 8 * r : 32 * x + 8 * r + 8] = moved[8 * x : 8 * x + 8, LANES * r : LANES * r + LANES]
    own = Slabs(own_flat, 8)
    even = lax.rem(me[0], 2) == 0
    for take, high, low in ((even, to_second, to_first), (jnp.logical_not(even), to_first, to_second)):
        @pl.when(take)
        def _(high=high, low=low):
            for i in range(6):
                high[i] = own[2 + i]
                low[i] = own[i]
            for i in range(6, 14):
                high[i] = own[2 + i]
                low[i] = own[2 + i]


G_BORDER, K_BORDER = 6, 8
G_SLABS, K_SLABS = 8 + 2 * G_BORDER, 8 + 2 * K_BORDER
G_REACH = (5, 4, 3, 2, 1, 0)
K_REACH = (6, 6, 4, 4, 2, 1, 0)


def row_parts():
    for array, reaches, border in ((0, G_REACH, G_BORDER), (1, K_REACH, K_BORDER)):
        for d, reach in enumerate(reaches, 1):
            yield array, d, reach, border


FACE_ROWS = 32 * (len(G_REACH) + len(K_REACH))
CORNER_ROWS = 8 * (sum(G_REACH) + sum(K_REACH))


def face_kernel(own, to_high, to_low):
    for i, (array, d, _, _) in enumerate(row_parts()):
        for out, y in ((to_high, 8 - d), (to_low, d - 1)):
            out[32 * i : 32 * i + 32] = own[pl.ds(256 * array + y, 32, 8), :]


def corners():
    at = 0
    for array, d, reach, border in row_parts():
        for column in (border - reach, border + 8):
            if reach:
                yield array, d, column, 4 * reach, at
                at += 4 * reach


def wide_kernel(me, own, first, second, flat, to_high, to_low):
    out, own = Slabs(flat, 8), Slabs(own, 8)

    def put(at, source, start, size):
        for i in range(size):
            out[at + i] = source[start + i]

    put(6, own, 0, 8)
    put(28, own, 8, 8)
    even = lax.rem(me[0], 2) == 0
    for take, left, right in ((even, first, second), (jnp.logical_not(even), second, first)):
        @pl.when(take)
        def _(left=left, right=right):
            put(0, left, 0, 6)
            put(14, right, 0, 6)
            put(20, left, 6, 8)
            put(36, right, 6, 8)
    for array, d, column, size, at in corners():
        base = (G_SLABS * array + column) * 32
        to_high[at : at + size] = flat[pl.ds(base + 8 - d, size, 8), :]
        to_low[at : at + size] = flat[pl.ds(base + d - 1, size, 8), :]


def early_kernel(own, low, high, g_flat, k_flat, fx, fy, fz, w, uf, u0, res):
    own, flats = Slabs(own, 8), (g_flat, k_flat)
    g, k = Slabs(g_flat, 24), Slabs(k_flat, 24)
    for i in range(8):
        g.put(i, 8, own[i])
        k.put(i, 8, own[8 + i])
    for i, (array, d, _, _) in enumerate(row_parts()):
        flats[array][pl.ds(8 - d, 32, 24), :] = low[32 * i : 32 * i + 32]
        flats[array][pl.ds(15 + d, 32, 24), :] = high[32 * i : 32 * i + 32]
    face_pass(6, k, fx, fy, fz, w, 1.0)
    for i in range(6):
        uf[i] = w[i] * g[1 + i]
    sweep_pass(4, uf, 0, 1, g, 2, fx, fy, fz, w, u0, 0)
    sweep_pass(2, u0, 0, 2, g, 3, fx, fy, fz, w, res, 0, last=True)


def fine_kernel(me, wide, low_corners, high_corners, g_early, k_early, fx_early, fy_early, fz_early, w_early, uf_early,
                u0_early, res_early, piece, u0_kept, g_flat, k_flat, u1, rhs, u0_edge, fx, fy, fz, w, uf, res, s1, sc,
                mx, my, mz, mw, mf, mr, ck):
    flats = g_flat, k_flat
    wide, g, k = Slabs(wide, 8), Slabs(g_flat, 24), Slabs(k_flat, 24)
    for i in range(12):
        g.put(i, 8, wide[i if i < 6 else i + 8])
    for i in range(16):
        k.put(i, 8, wide[G_SLABS + (i if i < 8 else i + 8)])
    for array, d, column, size, at in corners():
        slab = column if column < (G_BORDER, K_BORDER)[array] else column - 8
        flats[array][pl.ds(slab * 96 + 8 - d, size, 24), :] = low_corners[at : at + size]
        flats[array][pl.ds(slab * 96 + 15 + d, size, 24), :] = high_corners[at : at + size]
    g, k = Parted(Slabs(g_early, 24), g, 6, 14), Parted(Slabs(k_early, 24), k, 8, 16)
    fx = Parted(fx_early, fx, 7, 14)
    fy, fz, w, uf = [Parted(*pair, 7, 13) for pair in ((fy_early, fy), (fz_early, fz), (w_early, w), (uf_early, uf))]
    u0 = Parted(Parted(u0_early, u0_kept, 5, 9), u0_edge, 2, 16)
    res = Parted(res_early, res, 7, 9)
    face_pass(20, k, fx, fy, fz, w, 1.0, k_at=1, done=range(7, 13))
    for i in range(20):
        if not 7 <= i < 13:
            uf[i] = w[i] * g[i]
    sweep_pass(18, uf, 0, 1, g, 1, fx, fy, fz, w, u0, 0, done=range(7, 11))
    sweep_pass(16, u0, 0, 2, g, 2, fx, fy, fz, w, res, 0, last=True, done=range(7, 9))
    for x in range(8):
        both = res[2 * x] + res[2 * x + 1]
        s1[x, 0] = both[0] + both[1]
        s1[x, 1] = both[2] + both[3]
    for x in range(10):
        both = k[2 + 2 * x] + k[3 + 2 * x]
        sc[x, 0] = both[0] + both[1]
        sc[x, 1] = both[2] + both[3]

    def rows(ref, x, start):
        return jnp.stack(
            [ref[x, r, pl.ds(start, 8, 2), :] + ref[x, r, pl.ds(start + 1, 8, 2), :] for r in range(2)]
        ) * 0.125

    half = 0.5 * 0.25
    k_mid = [rows(sc, x, 4) for x in range(10)]
    mx[0] = half * (k_mid[0] + k_mid[1])
    for x in range(8):
        here = k_mid[x + 1]
        face_x = half * (here + k_mid[x + 2])
        face_y = half * (here + rows(sc, x + 1, 6))
        face_z = half * (here + z_next(here))
        diag = ABSORPTION + (
            mx[x] + face_x + face_y + half * (here + rows(sc, x + 1, 2)) + face_z + z_prev(face_z)
        )
        mx[x + 1], my[x], mz[x] = face_x, face_y, face_z
        mw[x] = DAMPING / diag
        rhs[x] = rows(s1, x, 4)
        mf[x] = mw[x] * rhs[x]
    sweep_pass(6, mf, 0, 1, rhs, 1, mx, my, mz, mw, u1, 0)
    sweep_pass(4, u1, 0, 2, rhs, 2, mx, my, mz, mw, mr, 0, last=True)
    for x in range(4):
        both = k_mid[2 * x + 1] + k_mid[2 * x + 2]
        ck[x] = both[0] + both[1]
    k2 = [(ck[x, pl.ds(0, 4, 2), :] + ck[x, pl.ds(1, 4, 2), :]) * 0.125 for x in range(4)]
    half = 0.5 * 0.0625
    for x in range(2):
        here = k2[x + 1][1:3]
        face_z = half * (here + pltpu.roll(here, LANES - 1, 1))
        diag = ABSORPTION + (
            half * (here + k2[x][1:3]) + half * (here + k2[x + 2][1:3])
            + half * (here + k2[x + 1][0:2]) + half * (here + k2[x + 1][2:4])
            + face_z + pltpu.roll(face_z, 1, 1)
        )
        both = mr[2 * x] + mr[2 * x + 1]
        ck[x] = both[0] + both[1]
        first_sweep = DAMPING / diag * ((ck[x, pl.ds(2, 2, 2), :] + ck[x, pl.ds(3, 2, 2), :]) * 0.125)
        for j in range(2):
            ck[3, 2 * j + x : 2 * j + x + 1, :] = first_sweep[j : j + 1]
            ck[3, 4 + 2 * j + x : 5 + 2 * j + x, :] = here[j : j + 1]
    level_2 = ck[3]
    for to in range(piece.shape[0]):
        piece[to, 0:8, :] = level_2
    count = piece.shape[0]
    for to, column in ((lax.rem(me[0] + 1, count), 0), (lax.rem(me[0] + count - 1, count), 1)):
        for r in range(2):
            for x in range(3):
                at = 8 + 4 * (2 * x + r)
                piece[to, at : at + 4, :] = u1[column + x + 1, r, 2:6, :]
            piece[to, 32 + 4 * r : 36 + 4 * r, :] = rhs[column + 3, r, 2:6, :]


def prepare_middle_kernel(k_early, k_flat, fx, fy, fz, w, k_mid, sums):
    k = Parted(Slabs(k_early, 24), Slabs(k_flat, 24), 8, 16)
    for x in range(12):
        both = k[2 * x] + k[2 * x + 1]
        for r in range(2):
            sums[r] = both[2 * r] + both[2 * r + 1]
            k_mid[x, r] = (sums[r, pl.ds(4, 8, 2), :] + sums[r, pl.ds(5, 8, 2), :]) * 0.125
    face_pass(10, k_mid, fx, fy, fz, w, 0.25)


def prepare_kernel(u0_early, u0, g_early, g_flat, k_early, k_flat, u_out, g_out, fx, fy, fz, w, k_rows):
    g, k = Parted(Slabs(g_early, 24), Slabs(g_flat, 24), 6, 14), Parted(Slabs(k_early, 24), Slabs(k_flat, 24), 8, 16)
    u0 = Parted(u0_early, u0, 5, 9)
    for i in range(14):
        u_out[i] = u0.part(i, 4, 16)
        k_rows[i] = k.part(i + 5, 4, 16)
    for i in range(12):
        g_out[i] = g.part(i + 4, 4, 16)
    face_pass(12, k_rows, fx, fy, fz, w, 1.0)


EDGE_ROWS = 4 * 20 + 2 * 20 + 16


def middle_kernel(me, gathered, u1, rhs, here, to_high, to_low, level_1):
    count = gathered.shape[0]
    for block in range(11):
        source = lax.rem(me[0] + (block - 5 + count * 5), count)
        for j in range(2):
            for array in range(2):
                at = 4 * array + 2 * j
                here[2 * j + array, 2 * block : 2 * block + 2, :] = gathered[source, at : at + 2, :]
    u_flat, r_flat = level_1.at[0:192], level_1.at[192:352]
    u, g = Slabs(u_flat, 8, 2), Slabs(r_flat, 8, 2)
    for x in range(6):
        u[3 + x] = u1[x]
    for x in range(8):
        g[1 + x] = rhs[x]
    for source, column, edge in ((lax.rem(me[0] + count - 1, count), 0, 0), (lax.rem(me[0] + 1, count), 9, 9)):
        for r in range(2):
            for x in range(3):
                at = 8 + 4 * (2 * x + r)
                to = 8 * (2 * (column + x) + r) + 2
                u_flat[to : to + 4, :] = gathered[source, at : at + 4, :]
            to = 8 * (2 * edge + r) + 2
            r_flat[to : to + 4, :] = gathered[source, 32 + 4 * r : 36 + 4 * r, :]
    for out, row, rhs_row in ((to_high, 4, 5), (to_low, 2, 2)):
        for slab in range(4):
            out[20 * slab : 20 * slab + 20] = here[slab, 1:21]
        for i in range(2):
            out[80 + 20 * i : 100 + 20 * i] = level_1[pl.ds(16 + row + i, 20, 8), :]
        out[120:136] = level_1[pl.ds(192 + 16 + rhs_row, 16, 8), :]


SPREAD = (16, 14, 12, 10, 8, 6)


def spread(j, upward):
    d = j if upward else 5 - j
    return 3 + d, SPREAD[d], 2 * sum(SPREAD[:d])


def three_kernel(me, here, low, high, to_first, to_second):
    blocks = (low, here, high)
    even = lax.rem(me[0], 2) == 0
    for take, to_high, to_low in ((even, to_second, to_first), (jnp.logical_not(even), to_first, to_second)):
        @pl.when(take)
        def _(to_high=to_high, to_low=to_low):
            for j in range(6):
                source = blocks[j // 2]
                for out, upward in ((to_high, False), (to_low, True)):
                    start, size, at = spread(j, upward)
                    for array in range(2):
                        slab = 2 * (j % 2) + array
                        if source is here:
                            values = here[slab, start : start + size]
                        else:
                            values = source[20 * slab + start - 1 : 20 * slab + start - 1 + size]
                        out[at + size * array : at + size * array + size] = values


def coarse_kernel(me, first, here, second, left, right, level_1, fx, fy, fz, w, v_flat_out, to_high, to_low,
                  u, c, start, cy, weights, v_flat, r_flat, va):
    half = 0.5 * 0.0625
    even = lax.rem(me[0], 2) == 0
    for take, below, above in ((even, first, second), (jnp.logical_not(even), second, first)):
        @pl.when(take)
        def _(below=below, above=above):
            for j in range(6):
                for source, upward, y in ((below, False, j), (above, True, 12 + j)):
                    column, size, at = spread(j, upward)
                    start[y, column : column + size] = source[at : at + size]
                    c[y, column : column + size] = source[at + size : at + 2 * size]
    for j in range(6):
        block, slab = (left, here, right)[j // 2], 2 * (j % 2)
        if block is here:
            start[6 + j] = here[slab]
            c[6 + j] = here[slab + 1]
        else:
            start[6 + j, 1:21] = block[20 * slab : 20 * slab + 20]
            c[6 + j, 1:21] = block[20 * slab + 20 : 20 * slab + 40]
    cy[0] = half * (c[0] + c[1])
    for y in range(18):
        u[y] = start[y]
    for y in range(1, 17):
        k = c[y]
        right_x = half * (k + pltpu.roll(k, 23, 0))
        right_z = half * (k + pltpu.roll(k, LANES - 1, 1))
        right_y = half * (k + c[y + 1])
        left_x, left_z, left_y = pltpu.roll(right_x, 1, 0), pltpu.roll(right_z, 1, 1), cy[y - 1]
        cy[y] = right_y
        scale = DAMPING / (ABSORPTION + (right_x + left_x + right_y + left_y + right_z + left_z))
        for i, face in enumerate((right_x, left_x, right_y, left_y, right_z, left_z)):
            weights[i, y] = scale * face
    for step in range(1, 8):
        before, now = u[step - 1], u[step]
        for y in range(step, 18 - step):
            later = u[y + 1]
            along_x = weights[0, y] * pltpu.roll(now, 23, 0) + weights[1, y] * pltpu.roll(now, 1, 0)
            along_y = weights[2, y] * later + weights[3, y] * before
            along_z = weights[4, y] * pltpu.roll(now, LANES - 1, 1) + weights[5, y] * pltpu.roll(now, 1, 1)
            u[y] = ((1.0 - DAMPING) * now + start[y]) + along_y + (along_x + along_z)
            before, now = now, later
    v_flat[...] = level_1[0:192]
    r_flat[...] = level_1[192:352]
    for source, row, rhs_row in ((left, 0, 1), (right, 6, 6)):
        for i in range(2):
            v_flat[pl.ds(16 + row + i, 20, 8), :] = source[80 + 20 * i : 100 + 20 * i]
        r_flat[pl.ds(16 + rhs_row, 16, 8), :] = source[120:136]
    v, rhs = Slabs(v_flat, 8, 2), Slabs(r_flat, 8, 2)
    for x in range(6):
        rows = jnp.concatenate(
            [jnp.broadcast_to(u[7 + j, 8 + x : 9 + x, :], (2, LANES)) for j in range(4)], axis=0
        )
        for twin in range(2):
            v[2 * x + twin] = v[2 * x + twin] + rows[None]
    sweep_pass(10, v, 0, 0, rhs, 0, fx, fy, fz, w, va, 0)
    sweep_pass(8, va, 0, 1, rhs, 1, fx, fy, fz, w, Slabs(v_flat_out, 8, 2), 0)
    for out, row in ((to_high, 4), (to_low, 2)):
        for i in range(2):
            out[16 * i : 16 * i + 16] = v_flat_out[pl.ds(row + i, 16, 8), :]


def last_kernel(v_here, v_low, v_high, u0, g, fx, fy, fz, w, correction, residual, v_flat, wide, ua, ub, res, held, left):
    v_flat[...] = v_here[...]
    for source, row in ((v_low, 0), (v_high, 6)):
        for i in range(2):
            v_flat[pl.ds(row + i, 16, 8), :] = source[16 * i : 16 * i + 16]
    for x in range(8):
        for r in range(2):
            rows = v_flat[8 * (2 * x + r) : 8 * (2 * x + r) + 8]
            wide[x, r, pl.ds(0, 8, 2), :] = rows
            wide[x, r, pl.ds(1, 8, 2), :] = rows
    for i in range(14):
        fine = wide[(i + 1) // 2]
        ua[i] = u0[i] + jnp.stack([fine[0], fine[0], fine[1], fine[1]])
    sweep_pass(12, ua, 0, 0, g, 0, fx, fy, fz, w, ub, 0)
    sweep_pass(10, ub, 0, 1, g, 1, fx, fy, fz, w, ua, 0)
    matrix = permutation(True)

    def leave(index, source, at, out):
        rows = [
            jnp.concatenate([source[at + x, r, 4:12, :] for r in range(4)], axis=1) for x in range(8)
        ]
        held[index] = rearrange(jnp.concatenate(rows, axis=0), matrix).reshape(8, 8, 512)
        copy = pltpu.make_async_copy(held.at[index], out, left.at[index])
        copy.start()
        return copy

    first = leave(0, ua, 1, correction)
    sweep_pass(8, ua, 0, 2, g, 2, fx, fy, fz, w, res, 0, last=True)
    second = leave(1, res, 0, residual)
    first.wait()
    second.wait()


VMEM = pl.BlockSpec(memory_space=pltpu.VMEM)
SMEM = pl.BlockSpec(memory_space=pltpu.SMEM)
HBM = pl.BlockSpec(memory_space=pltpu.HBM)


def call(kernel, outs, scratch, *arrays, scalars=0, to_hbm=False, extra=()):
    return pl.pallas_call(
        kernel,
        out_shape=[jax.ShapeDtypeStruct(shape, F32) for shape in outs],
        in_specs=[SMEM] * scalars + [VMEM] * (len(arrays) - scalars),
        out_specs=[HBM if to_hbm else VMEM] * len(outs),
        scratch_shapes=[pltpu.VMEM(shape, F32) for shape in scratch] + list(extra),
        compiler_params=pltpu.CompilerParams(vmem_limit_bytes=32 * 2**20),
    )(*arrays)


def shift(array, axis, by):
    count = lax.axis_size(axis)
    return lax.ppermute(array, axis, [(i, (i + by) % count) for i in range(count)])


def swap(array, axis, start, by=1):
    count = lax.axis_size(axis)
    pairs = [(i, (i + by) % count) for i in range(start, count, 2)]
    return lax.ppermute(array, axis, pairs + [(j, i) for i, j in pairs])


def per_device(right_side, coefficient):
    me_x = lax.axis_index("gx").astype(jnp.int32).reshape(1)
    me_y = lax.axis_index("gy").astype(jnp.int32).reshape(1)
    count = lax.axis_size("gx")
    border = (G_BORDER + K_BORDER, 4, 8, 128)
    own, first, second = call(
        permute_kernel, [(512, 128), border, border], [], me_x, jnp.stack([right_side, coefficient]), scalars=1
    )
    first, second = swap(first, "gx", 1), swap(second, "gx", 0)
    high, low = call(face_kernel, [(FACE_ROWS, 128), (FACE_ROWS, 128)], [], own)
    low, high = shift(high, "gy", 1), shift(low, "gy", -1)
    wide, high_corners, low_corners = call(
        wide_kernel, [((G_SLABS + K_SLABS) * 32, 128), (CORNER_ROWS, 128), (CORNER_ROWS, 128)], [],
        me_x, own, first, second, scalars=1,
    )
    low_corners, high_corners = shift(high_corners, "gy", 1), shift(low_corners, "gy", -1)
    fine, mid, last = (4, 24, 128), (2, 8, 128), (4, 16, 128)
    early = call(
        early_kernel,
        [(8 * 96, 128), (8 * 96, 128), (7, *fine), (6, *fine), (6, *fine), (6, *fine), (6, *fine), (4, *fine), (2, *fine)],
        [], own, low, high,
    )
    g_early, k_early, u0_early = early[0], early[1], early[7]
    piece, u0, g, k, u1, rhs = call(
        fine_kernel,
        [(count, 40, 128), (10, *fine), (12 * 96, 128), (16 * 96, 128), (6, *mid), (8, *mid)],
        [(4, *fine), (14, *fine), (14, *fine), (14, *fine), (14, *fine), (14, *fine), (14, *fine), (8, 2, 24, 128), (10, 2, 24, 128),
         (9, *mid), (8, *mid), (8, *mid), (8, *mid), (8, *mid), (4, *mid), (4, 8, 128)],
        me_x, wide, low_corners, high_corners, *early, scalars=1,
    )
    piece, u0, g, k, u1, rhs = lax.optimization_barrier((piece, u0, g, k, u1, rhs))
    gathered = lax.all_to_all(piece, "gx", 0, 0)
    gathered, u0, g, k, u1, rhs = lax.optimization_barrier((gathered, u0, g, k, u1, rhs))
    here, high, low, level_1 = call(
        middle_kernel, [(4, 24, 128), (EDGE_ROWS, 128), (EDGE_ROWS, 128), (352, 128)], [], me_x, gathered, u1, rhs, scalars=1
    )
    low, high = shift(high, "gy", 1), shift(low, "gy", -1)
    first, second = call(three_kernel, [(136, 128), (136, 128)], [], me_y, here, low, high, scalars=1)
    first, second = swap(first, "gy", 1, 3), swap(second, "gy", 0, 3)
    faces = call(
        prepare_middle_kernel, [(11, *mid), (10, *mid), (10, *mid), (10, *mid)], [(12, *mid), (2, 24, 128)], k_early, k
    )
    rows = (18, 24, 128)
    v1, high_rows, low_rows = call(
        coarse_kernel, [(128, 128), (32, 128), (32, 128)],
        [rows, rows, rows, rows, (6, *rows), (192, 128), (160, 128), (10, *mid)],
        me_y, first, here, second, low, high, level_1, *faces, scalars=1,
    )
    u0, g, *faces = call(
        prepare_kernel, [(14, *last), (12, *last), (13, *last), (12, *last), (12, *last), (12, *last)], [(14, *last)],
        u0_early, u0, g_early, g, k_early, k,
    )
    low, high = shift(high_rows, "gy", 1), shift(low_rows, "gy", -1)
    return tuple(call(
        last_kernel, [(8, 8, 512), (8, 8, 512)],
        [(128, 128), (8, 2, 16, 128), (14, *last), (12, *last), (8, *last), (2, 8, 8, 512)],
        v1, low, high, u0, g, *faces, to_hbm=True, extra=[pltpu.SemaphoreType.DMA((2,))],
    ))


def solution(mesh):
    placed = (P("gx", "gy", None), P("gx", "gy", None))
    return jax.shard_map(per_device, mesh=mesh, in_specs=placed, out_specs=placed, check_vma=False)
```

```python
import jax
import jax.numpy as jnp
from jax import lax
from jax.experimental import pallas as pl
from jax.experimental.pallas import tpu as pltpu
from jax.sharding import PartitionSpec as P

ABSORPTION = 0.05
DAMPING = 0.8
F32 = jnp.float32
LANES = 128


def z_next(v):
    first = pltpu.roll(v[0], LANES - 1, 1)[None]
    return first if v.shape[0] == 1 else jnp.concatenate([v[1:], first], axis=0)


def z_prev(v):
    last = pltpu.roll(v[-1], 1, 1)[None]
    return last if v.shape[0] == 1 else jnp.concatenate([last, v[:-1]], axis=0)


def y_next(v):
    return pltpu.roll(v, v.shape[1] - 1, 1)


def y_prev(v):
    return pltpu.roll(v, 1, 1)


def flux_sum(u, u_next, flux_low, fx, fy, fz):
    flux_high = fx * (u - u_next)
    flux_y = fy * (u - y_next(u))
    flux_z = fz * (u - z_next(u))
    total = (flux_high - flux_low) + (flux_y - y_prev(flux_y)) + (flux_z - z_prev(flux_z))
    return ABSORPTION * u + total, flux_high


class Slabs:
    def __init__(self, flat, rows, parts=4):
        self.flat, self.rows, self.parts = flat, rows, parts

    def at(self, i):
        size = self.parts * self.rows
        return pl.ds(i * size, size)

    def __getitem__(self, i):
        return self.flat[self.at(i), :].reshape(self.parts, self.rows, LANES)

    def __setitem__(self, i, value):
        self.flat[self.at(i), :] = value.reshape(self.parts * self.rows, LANES)

    def part(self, i, start, size, step=1):
        where = lambda r: pl.ds((self.parts * i + r) * self.rows + start, size, step)
        return jnp.stack([self.flat[where(r), :] for r in range(self.parts)])

    def put(self, i, start, value):
        for r in range(self.parts):
            self.flat[pl.ds((self.parts * i + r) * self.rows + start, value.shape[1]), :] = value[r]


class Parted:
    def __init__(self, inner, outer, start, stop):
        self.inner, self.outer, self.start, self.stop = inner, outer, start, stop

    def place(self, i):
        if self.start <= i < self.stop:
            return self.inner, i - self.start
        return self.outer, i if i < self.start else i - (self.stop - self.start)

    def __getitem__(self, i):
        buffer, at = self.place(i)
        return buffer[at]

    def __setitem__(self, i, value):
        buffer, at = self.place(i)
        buffer[at] = value

    def part(self, i, start, size):
        buffer, at = self.place(i)
        if isinstance(buffer, (Parted, Slabs)):
            return buffer.part(at, start, size)
        return buffer[at, :, start : start + size, :]


def get(ref, i, rows):
    if rows is None:
        return ref[i]
    return ref.part(i, *rows) if hasattr(ref, "part") else ref[i, :, rows[0] : rows[0] + rows[1], :]


def put(ref, i, rows, value):
    if isinstance(ref, Parted):
        put(*ref.place(i), rows, value)
    elif rows is None:
        ref[i] = value
    else:
        ref[i, :, rows[0] : rows[0] + rows[1], :] = value


def every_row(i):
    return None


def face_pass(count, k_ref, fx, fy, fz, w, scale, k_at=0, done=(), rows=every_row):
    half = 0.5 * scale
    for i in range(count + 1):
        if i not in done or i - 1 not in done:
            fx[i] = half * (k_ref[k_at + i] + k_ref[k_at + 1 + i])
        if i == 0 or i - 1 in done:
            continue
        some = rows(i - 1)
        k = get(k_ref, k_at + i, some)
        face_y = half * (k + y_next(k))
        face_z = half * (k + z_next(k))
        diag = ABSORPTION + (get(fx, i, some) + get(fx, i - 1, some) + face_y + y_prev(face_y) + face_z + z_prev(face_z))
        put(fy, i - 1, some, face_y)
        put(fz, i - 1, some, face_z)
        put(w, i - 1, some, DAMPING / diag)


def sweep_pass(count, u_ref, u_at, faces_at, g_ref, g_at, fx, fy, fz, w, out, out_at, last=False, done=(), rows=every_row):
    low, low_rows = None, None
    for i in range(count):
        if i in done:
            low = None
            continue
        some, f = rows(i), faces_at + i
        u, u_next = get(u_ref, u_at + 1 + i, some), get(u_ref, u_at + 2 + i, some)
        if low is None or low_rows != some:
            low = get(fx, f, some) * (get(u_ref, u_at + i, some) - u)
        applied, low = flux_sum(u, u_next, low, get(fx, f + 1, some), get(fy, f, some), get(fz, f, some))
        low_rows = some
        rest = get(g_ref, g_at + i, some) - applied
        put(out, out_at + i, some, rest if last else u + get(w, f, some) * rest)


def permutation(inverse):
    z = lax.broadcasted_iota(jnp.int32, (512, 512), 1 if inverse else 0)
    at = lax.broadcasted_iota(jnp.int32, (512, 512), 0 if inverse else 1)
    return jnp.where(z == 4 * (at % LANES) + at // LANES, 1.0, 0.0).astype(jnp.bfloat16)


def rearrange(rows, matrix):
    count = rows.shape[0]
    top = rows.astype(jnp.bfloat16)
    rest = rows - top.astype(F32)
    middle = rest.astype(jnp.bfloat16)
    bottom = (rest - middle.astype(F32)).astype(jnp.bfloat16)
    parts = jnp.concatenate([top, middle, bottom], axis=0)
    moved = lax.dot_general(parts, matrix, (((1,), (0,)), ((), ())), preferred_element_type=F32)
    return (moved[0:count] + moved[count : 2 * count]) + moved[2 * count :]


def permute_kernel(me, held, own_flat, to_first, to_second):
    matrix = permutation(False)
    moved = rearrange(held[...].reshape(128, 512), matrix)
    for x in range(16):
        for r in range(4):
            own_flat[32 * x + 8 * r : 32 * x + 8 * r + 8] = moved[8 * x : 8 * x + 8, LANES * r : LANES * r + LANES]
    own = Slabs(own_flat, 8)
    even = lax.rem(me[0], 2) == 0
    for take, high, low in ((even, to_second, to_first), (jnp.logical_not(even), to_first, to_second)):
        @pl.when(take)
        def _(high=high, low=low):
            for i in range(6):
                high[i] = own[2 + i]
                low[i] = own[i]
            for i in range(6, 14):
                high[i] = own[2 + i]
                low[i] = own[2 + i]


G_BORDER, K_BORDER = 6, 8
G_SLABS, K_SLABS = 8 + 2 * G_BORDER, 8 + 2 * K_BORDER
G_REACH = (5, 4, 3, 2, 1, 0)
K_REACH = (6, 6, 4, 4, 2, 1, 0)


def row_parts():
    for array, reaches, border in ((0, G_REACH, G_BORDER), (1, K_REACH, K_BORDER)):
        for d, reach in enumerate(reaches, 1):
            yield array, d, reach, border


FACE_ROWS = 32 * (len(G_REACH) + len(K_REACH))
CORNER_ROWS = 8 * (sum(G_REACH) + sum(K_REACH))


def face_kernel(own, to_high, to_low):
    for i, (array, d, _, _) in enumerate(row_parts()):
        for out, y in ((to_high, 8 - d), (to_low, d - 1)):
            out[32 * i : 32 * i + 32] = own[pl.ds(256 * array + y, 32, 8), :]


def corners():
    at = 0
    for array, d, reach, border in row_parts():
        for column in (border - reach, border + 8):
            if reach:
                yield array, d, column, 4 * reach, at
                at += 4 * reach


def wide_kernel(me, own, first, second, flat, to_high, to_low):
    out, own = Slabs(flat, 8), Slabs(own, 8)

    def put(at, source, start, size):
        for i in range(size):
            out[at + i] = source[start + i]

    put(6, own, 0, 8)
    put(28, own, 8, 8)
    even = lax.rem(me[0], 2) == 0
    for take, left, right in ((even, first, second), (jnp.logical_not(even), second, first)):
        @pl.when(take)
        def _(left=left, right=right):
            put(0, left, 0, 6)
            put(14, right, 0, 6)
            put(20, left, 6, 8)
            put(36, right, 6, 8)
    for array, d, column, size, at in corners():
        base = (G_SLABS * array + column) * 32
        to_high[at : at + size] = flat[pl.ds(base + 8 - d, size, 8), :]
        to_low[at : at + size] = flat[pl.ds(base + d - 1, size, 8), :]


def early_kernel(own, low, high, g_flat, k_flat, fx, fy, fz, w, uf, u0, res):
    own, flats = Slabs(own, 8), (g_flat, k_flat)
    g, k = Slabs(g_flat, 24), Slabs(k_flat, 24)
    for i in range(8):
        g.put(i, 8, own[i])
        k.put(i, 8, own[8 + i])
    for i, (array, d, _, _) in enumerate(row_parts()):
        flats[array][pl.ds(8 - d, 32, 24), :] = low[32 * i : 32 * i + 32]
        flats[array][pl.ds(15 + d, 32, 24), :] = high[32 * i : 32 * i + 32]
    face_pass(6, k, fx, fy, fz, w, 1.0)
    for i in range(6):
        uf[i] = w[i] * g[1 + i]
    sweep_pass(4, uf, 0, 1, g, 2, fx, fy, fz, w, u0, 0)
    sweep_pass(2, u0, 0, 2, g, 3, fx, fy, fz, w, res, 0, last=True)


def fine_kernel(me, wide, low_corners, high_corners, g_early, k_early, fx_early, fy_early, fz_early, w_early, uf_early,
                u0_early, res_early, piece, u0_kept, g_flat, k_flat, u1, rhs, u0_edge, fx, fy, fz, w, uf, res, s1, sc,
                mx, my, mz, mw, mf, mr, ck):
    flats = g_flat, k_flat
    wide, g, k = Slabs(wide, 8), Slabs(g_flat, 24), Slabs(k_flat, 24)
    for i in range(12):
        g.put(i, 8, wide[i if i < 6 else i + 8])
    for i in range(16):
        k.put(i, 8, wide[G_SLABS + (i if i < 8 else i + 8)])
    for array, d, column, size, at in corners():
        slab = column if column < (G_BORDER, K_BORDER)[array] else column - 8
        flats[array][pl.ds(slab * 96 + 8 - d, size, 24), :] = low_corners[at : at + size]
        flats[array][pl.ds(slab * 96 + 15 + d, size, 24), :] = high_corners[at : at + size]
    g, k = Parted(Slabs(g_early, 24), g, 6, 14), Parted(Slabs(k_early, 24), k, 8, 16)
    fx = Parted(fx_early, fx, 7, 14)
    fy, fz, w, uf = [Parted(*pair, 7, 13) for pair in ((fy_early, fy), (fz_early, fz), (w_early, w), (uf_early, uf))]
    u0 = Parted(Parted(u0_early, u0_kept, 5, 9), u0_edge, 2, 16)
    res = Parted(res_early, res, 7, 9)
    def beside(first_x, border):
        return lambda i: (4, 16) if first_x + i <= -border or first_x + i >= 7 + border else None

    face_pass(20, k, fx, fy, fz, w, 1.0, k_at=1, done=range(7, 13), rows=beside(-6, 3))
    for i in range(20):
        if not 7 <= i < 13:
            some = beside(-6, 3)(i)
            put(uf, i, some, get(w, i, some) * get(g, i, some))
    sweep_pass(18, uf, 0, 1, g, 1, fx, fy, fz, w, u0, 0, done=range(7, 11), rows=beside(-5, 2))
    sweep_pass(16, u0, 0, 2, g, 2, fx, fy, fz, w, res, 0, last=True, done=range(7, 9), rows=beside(-4, 1))
    for x in range(8):
        both = res[2 * x] + res[2 * x + 1]
        s1[x, 0] = both[0] + both[1]
        s1[x, 1] = both[2] + both[3]
    for x in range(10):
        both = k[2 + 2 * x] + k[3 + 2 * x]
        sc[x, 0] = both[0] + both[1]
        sc[x, 1] = both[2] + both[3]

    def rows(ref, x, start):
        return jnp.stack(
            [ref[x, r, pl.ds(start, 8, 2), :] + ref[x, r, pl.ds(start + 1, 8, 2), :] for r in range(2)]
        ) * 0.125

    half = 0.5 * 0.25
    k_mid = [rows(sc, x, 4) for x in range(10)]
    mx[0] = half * (k_mid[0] + k_mid[1])
    for x in range(8):
        here = k_mid[x + 1]
        face_x = half * (here + k_mid[x + 2])
        face_y = half * (here + rows(sc, x + 1, 6))
        face_z = half * (here + z_next(here))
        diag = ABSORPTION + (
            mx[x] + face_x + face_y + half * (here + rows(sc, x + 1, 2)) + face_z + z_prev(face_z)
        )
        mx[x + 1], my[x], mz[x] = face_x, face_y, face_z
        mw[x] = DAMPING / diag
        rhs[x] = rows(s1, x, 4)
        mf[x] = mw[x] * rhs[x]
    sweep_pass(6, mf, 0, 1, rhs, 1, mx, my, mz, mw, u1, 0)
    sweep_pass(4, u1, 0, 2, rhs, 2, mx, my, mz, mw, mr, 0, last=True)
    for x in range(4):
        both = k_mid[2 * x + 1] + k_mid[2 * x + 2]
        ck[x] = both[0] + both[1]
    k2 = [(ck[x, pl.ds(0, 4, 2), :] + ck[x, pl.ds(1, 4, 2), :]) * 0.125 for x in range(4)]
    half = 0.5 * 0.0625
    for x in range(2):
        here = k2[x + 1][1:3]
        face_z = half * (here + pltpu.roll(here, LANES - 1, 1))
        diag = ABSORPTION + (
            half * (here + k2[x][1:3]) + half * (here + k2[x + 2][1:3])
            + half * (here + k2[x + 1][0:2]) + half * (here + k2[x + 1][2:4])
            + face_z + pltpu.roll(face_z, 1, 1)
        )
        both = mr[2 * x] + mr[2 * x + 1]
        ck[x] = both[0] + both[1]
        first_sweep = DAMPING / diag * ((ck[x, pl.ds(2, 2, 2), :] + ck[x, pl.ds(3, 2, 2), :]) * 0.125)
        for j in range(2):
            ck[3, 2 * j + x : 2 * j + x + 1, :] = first_sweep[j : j + 1]
            ck[3, 4 + 2 * j + x : 5 + 2 * j + x, :] = here[j : j + 1]
    level_2 = ck[3]
    for to in range(piece.shape[0]):
        piece[to, 0:8, :] = level_2
    count = piece.shape[0]
    for to, column in ((lax.rem(me[0] + 1, count), 0), (lax.rem(me[0] + count - 1, count), 1)):
        for r in range(2):
            for x in range(3):
                at = 8 + 4 * (2 * x + r)
                piece[to, at : at + 4, :] = u1[column + x + 1, r, 2:6, :]
            piece[to, 32 + 4 * r : 36 + 4 * r, :] = rhs[column + 3, r, 2:6, :]


def prepare_middle_kernel(k_early, k_flat, fx, fy, fz, w, k_mid, sums):
    k = Parted(Slabs(k_early, 24), Slabs(k_flat, 24), 8, 16)
    for x in range(12):
        both = k[2 * x] + k[2 * x + 1]
        for r in range(2):
            sums[r] = both[2 * r] + both[2 * r + 1]
            k_mid[x, r] = (sums[r, pl.ds(4, 8, 2), :] + sums[r, pl.ds(5, 8, 2), :]) * 0.125
    face_pass(10, k_mid, fx, fy, fz, w, 0.25)


def prepare_kernel(u0_early, u0, g_early, g_flat, k_early, k_flat, u_out, g_out, fx, fy, fz, w, k_rows):
    g, k = Parted(Slabs(g_early, 24), Slabs(g_flat, 24), 6, 14), Parted(Slabs(k_early, 24), Slabs(k_flat, 24), 8, 16)
    u0 = Parted(u0_early, u0, 5, 9)
    for i in range(14):
        u_out[i] = u0.part(i, 4, 16)
        k_rows[i] = k.part(i + 5, 4, 16)
    for i in range(12):
        g_out[i] = g.part(i + 4, 4, 16)
    face_pass(12, k_rows, fx, fy, fz, w, 1.0)


EDGE_ROWS = 4 * 20 + 2 * 20 + 16


def middle_kernel(me, gathered, u1, rhs, here, to_high, to_low, level_1):
    count = gathered.shape[0]
    for block in range(11):
        source = lax.rem(me[0] + (block - 5 + count * 5), count)
        for j in range(2):
            for array in range(2):
                at = 4 * array + 2 * j
                here[2 * j + array, 2 * block : 2 * block + 2, :] = gathered[source, at : at + 2, :]
    u_flat, r_flat = level_1.at[0:192], level_1.at[192:352]
    u, g = Slabs(u_flat, 8, 2), Slabs(r_flat, 8, 2)
    for x in range(6):
        u[3 + x] = u1[x]
    for x in range(8):
        g[1 + x] = rhs[x]
    for source, column, edge in ((lax.rem(me[0] + count - 1, count), 0, 0), (lax.rem(me[0] + 1, count), 9, 9)):
        for r in range(2):
            for x in range(3):
                at = 8 + 4 * (2 * x + r)
                to = 8 * (2 * (column + x) + r) + 2
                u_flat[to : to + 4, :] = gathered[source, at : at + 4, :]
            to = 8 * (2 * edge + r) + 2
            r_flat[to : to + 4, :] = gathered[source, 32 + 4 * r : 36 + 4 * r, :]
    for out, row, rhs_row in ((to_high, 4, 5), (to_low, 2, 2)):
        for slab in range(4):
            out[20 * slab : 20 * slab + 20] = here[slab, 1:21]
        for i in range(2):
            out[80 + 20 * i : 100 + 20 * i] = level_1[pl.ds(16 + row + i, 20, 8), :]
        out[120:136] = level_1[pl.ds(192 + 16 + rhs_row, 16, 8), :]


SPREAD = (16, 14, 12, 10, 8, 6)


def spread(j, upward):
    d = j if upward else 5 - j
    return 3 + d, SPREAD[d], 2 * sum(SPREAD[:d])


def three_kernel(me, here, low, high, to_first, to_second):
    blocks = (low, here, high)
    even = lax.rem(me[0], 2) == 0
    for take, to_high, to_low in ((even, to_second, to_first), (jnp.logical_not(even), to_first, to_second)):
        @pl.when(take)
        def _(to_high=to_high, to_low=to_low):
            for j in range(6):
                source = blocks[j // 2]
                for out, upward in ((to_high, False), (to_low, True)):
                    start, size, at = spread(j, upward)
                    for array in range(2):
                        slab = 2 * (j % 2) + array
                        if source is here:
                            values = here[slab, start : start + size]
                        else:
                            values = source[20 * slab + start - 1 : 20 * slab + start - 1 + size]
                        out[at + size * array : at + size * array + size] = values


def window(reach):
    return (7, 8) if reach <= 3 else (3, 16) if reach <= 7 else (1, 24)


def coarse_kernel(me, first, here, second, left, right, level_1, fx, fy, fz, w, v_flat_out, to_high, to_low,
                  u, other, c, start, weights, v_flat, r_flat, va):
    half = 0.5 * 0.0625
    even = lax.rem(me[0], 2) == 0
    for take, below, above in ((even, first, second), (jnp.logical_not(even), second, first)):
        @pl.when(take)
        def _(below=below, above=above):
            for j in range(6):
                for source, upward, y in ((below, False, j), (above, True, 12 + j)):
                    column, size, at = spread(j, upward)
                    start[y, column : column + size] = source[at : at + size]
                    c[y, column : column + size] = source[at + size : at + 2 * size]
    for j in range(6):
        block, slab = (left, here, right)[j // 2], 2 * (j % 2)
        if block is here:
            start[6 + j, 0:24] = here[slab]
            c[6 + j, 0:24] = here[slab + 1]
        else:
            start[6 + j, 1:21] = block[20 * slab : 20 * slab + 20]
            c[6 + j, 1:21] = block[20 * slab + 20 : 20 * slab + 40]

    def reach(y, step):
        return 9 - step - max(0, 7 - y, y - 10)

    def at(ref, y, lo, size):
        return ref[y, lo : lo + size]

    for y in range(1, 17):
        lo, size = window(reach(y, 1))
        k = at(c, y, lo, size)
        face_z = half * (k + pltpu.roll(k, LANES - 1, 1))
        faces = [half * (k + at(c, y, lo + 1, size)), half * (k + at(c, y, lo - 1, size))]
        faces += [half * (k + at(c, y + 1, lo, size)), half * (k + at(c, y - 1, lo, size))]
        faces += [face_z, pltpu.roll(face_z, 1, 1)]
        scale = DAMPING / (ABSORPTION + ((faces[0] + faces[1]) + (faces[2] + faces[3]) + (faces[4] + faces[5])))
        for i, face in enumerate(faces):
            weights[i, y, lo : lo + size] = scale * face
    old = start
    for step in range(1, 8):
        new = (u, other)[step % 2]
        for y in range(step, 18 - step):
            lo, size = window(reach(y, step))
            now = at(old, y, lo, size)
            along_x = at(weights.at[0], y, lo, size) * at(old, y, lo + 1, size) + at(weights.at[1], y, lo, size) * at(old, y, lo - 1, size)
            along_y = at(weights.at[2], y, lo, size) * at(old, y + 1, lo, size) + at(weights.at[3], y, lo, size) * at(old, y - 1, lo, size)
            along_z = (
                at(weights.at[4], y, lo, size) * pltpu.roll(now, LANES - 1, 1)
                + at(weights.at[5], y, lo, size) * pltpu.roll(now, 1, 1)
            )
            new[y, lo : lo + size] = ((1.0 - DAMPING) * now + at(start, y, lo, size)) + along_y + (along_x + along_z)
        old = new
    u = old
    v_flat[...] = level_1[0:192]
    r_flat[...] = level_1[192:352]
    for source, row, rhs_row in ((left, 0, 1), (right, 6, 6)):
        for i in range(2):
            v_flat[pl.ds(16 + row + i, 20, 8), :] = source[80 + 20 * i : 100 + 20 * i]
        r_flat[pl.ds(16 + rhs_row, 16, 8), :] = source[120:136]
    v, rhs = Slabs(v_flat, 8, 2), Slabs(r_flat, 8, 2)
    for x in range(6):
        rows = jnp.concatenate(
            [jnp.broadcast_to(u[7 + j, 8 + x : 9 + x, :], (2, LANES)) for j in range(4)], axis=0
        )
        for twin in range(2):
            v[2 * x + twin] = v[2 * x + twin] + rows[None]
    sweep_pass(10, v, 0, 0, rhs, 0, fx, fy, fz, w, va, 0)
    sweep_pass(8, va, 0, 1, rhs, 1, fx, fy, fz, w, Slabs(v_flat_out, 8, 2), 0)
    for out, row in ((to_high, 4), (to_low, 2)):
        for i in range(2):
            out[16 * i : 16 * i + 16] = v_flat_out[pl.ds(row + i, 16, 8), :]


def last_kernel(v_here, v_low, v_high, u0, g, fx, fy, fz, w, correction, residual, v_flat, wide, ua, ub, res, held, left):
    v_flat[...] = v_here[...]
    for source, row in ((v_low, 0), (v_high, 6)):
        for i in range(2):
            v_flat[pl.ds(row + i, 16, 8), :] = source[16 * i : 16 * i + 16]
    for x in range(8):
        for r in range(2):
            rows = v_flat[8 * (2 * x + r) : 8 * (2 * x + r) + 8]
            wide[x, r, pl.ds(0, 8, 2), :] = rows
            wide[x, r, pl.ds(1, 8, 2), :] = rows
    for i in range(14):
        fine = wide[(i + 1) // 2]
        ua[i] = u0[i] + jnp.stack([fine[0], fine[0], fine[1], fine[1]])
    sweep_pass(12, ua, 0, 0, g, 0, fx, fy, fz, w, ub, 0)
    sweep_pass(10, ub, 0, 1, g, 1, fx, fy, fz, w, ua, 0)
    matrix = permutation(True)

    def leave(index, source, at, out):
        rows = [
            jnp.concatenate([source[at + x, r, 4:12, :] for r in range(4)], axis=1) for x in range(8)
        ]
        held[index] = rearrange(jnp.concatenate(rows, axis=0), matrix).reshape(8, 8, 512)
        copy = pltpu.make_async_copy(held.at[index], out, left.at[index])
        copy.start()
        return copy

    first = leave(0, ua, 1, correction)
    sweep_pass(8, ua, 0, 2, g, 2, fx, fy, fz, w, res, 0, last=True)
    second = leave(1, res, 0, residual)
    first.wait()
    second.wait()


VMEM = pl.BlockSpec(memory_space=pltpu.VMEM)
SMEM = pl.BlockSpec(memory_space=pltpu.SMEM)
HBM = pl.BlockSpec(memory_space=pltpu.HBM)


def call(kernel, outs, scratch, *arrays, scalars=0, to_hbm=False, extra=()):
    return pl.pallas_call(
        kernel,
        out_shape=[jax.ShapeDtypeStruct(shape, F32) for shape in outs],
        in_specs=[SMEM] * scalars + [VMEM] * (len(arrays) - scalars),
        out_specs=[HBM if to_hbm else VMEM] * len(outs),
        scratch_shapes=[pltpu.VMEM(shape, F32) for shape in scratch] + list(extra),
        compiler_params=pltpu.CompilerParams(vmem_limit_bytes=32 * 2**20),
    )(*arrays)


def shift(array, axis, by):
    count = lax.axis_size(axis)
    return lax.ppermute(array, axis, [(i, (i + by) % count) for i in range(count)])


def swap(array, axis, start, by=1):
    count = lax.axis_size(axis)
    pairs = [(i, (i + by) % count) for i in range(start, count, 2)]
    return lax.ppermute(array, axis, pairs + [(j, i) for i, j in pairs])


def per_device(right_side, coefficient):
    me_x = lax.axis_index("gx").astype(jnp.int32).reshape(1)
    me_y = lax.axis_index("gy").astype(jnp.int32).reshape(1)
    count = lax.axis_size("gx")
    border = (G_BORDER + K_BORDER, 4, 8, 128)
    own, first, second = call(
        permute_kernel, [(512, 128), border, border], [], me_x, jnp.stack([right_side, coefficient]), scalars=1
    )
    first, second = swap(first, "gx", 1), swap(second, "gx", 0)
    high, low = call(face_kernel, [(FACE_ROWS, 128), (FACE_ROWS, 128)], [], own)
    low, high = shift(high, "gy", 1), shift(low, "gy", -1)
    wide, high_corners, low_corners = call(
        wide_kernel, [((G_SLABS + K_SLABS) * 32, 128), (CORNER_ROWS, 128), (CORNER_ROWS, 128)], [],
        me_x, own, first, second, scalars=1,
    )
    low_corners, high_corners = shift(high_corners, "gy", 1), shift(low_corners, "gy", -1)
    fine, mid, last = (4, 24, 128), (2, 8, 128), (4, 16, 128)
    early = call(
        early_kernel,
        [(8 * 96, 128), (8 * 96, 128), (7, *fine), (6, *fine), (6, *fine), (6, *fine), (6, *fine), (4, *fine), (2, *fine)],
        [], own, low, high,
    )
    g_early, k_early, u0_early = early[0], early[1], early[7]
    piece, u0, g, k, u1, rhs = call(
        fine_kernel,
        [(count, 40, 128), (10, *fine), (12 * 96, 128), (16 * 96, 128), (6, *mid), (8, *mid)],
        [(4, *fine), (14, *fine), (14, *fine), (14, *fine), (14, *fine), (14, *fine), (14, *fine), (8, 2, 24, 128), (10, 2, 24, 128),
         (9, *mid), (8, *mid), (8, *mid), (8, *mid), (8, *mid), (4, *mid), (4, 8, 128)],
        me_x, wide, low_corners, high_corners, *early, scalars=1,
    )
    piece, u0, g, k, u1, rhs = lax.optimization_barrier((piece, u0, g, k, u1, rhs))
    gathered = lax.all_to_all(piece, "gx", 0, 0)
    gathered, u0, g, k, u1, rhs = lax.optimization_barrier((gathered, u0, g, k, u1, rhs))
    here, high, low, level_1 = call(
        middle_kernel, [(4, 24, 128), (EDGE_ROWS, 128), (EDGE_ROWS, 128), (352, 128)], [], me_x, gathered, u1, rhs, scalars=1
    )
    low, high = shift(high, "gy", 1), shift(low, "gy", -1)
    first, second = call(three_kernel, [(136, 128), (136, 128)], [], me_y, here, low, high, scalars=1)
    first, second = swap(first, "gy", 1, 3), swap(second, "gy", 0, 3)
    faces = call(
        prepare_middle_kernel, [(11, *mid), (10, *mid), (10, *mid), (10, *mid)], [(12, *mid), (2, 24, 128)], k_early, k
    )
    rows = (18, 32, 128)
    v1, high_rows, low_rows = call(
        coarse_kernel, [(128, 128), (32, 128), (32, 128)],
        [rows, rows, rows, rows, (6, *rows), (192, 128), (160, 128), (10, *mid)],
        me_y, first, here, second, low, high, level_1, *faces, scalars=1,
    )
    u0, g, *faces = call(
        prepare_kernel, [(14, *last), (12, *last), (13, *last), (12, *last), (12, *last), (12, *last)], [(14, *last)],
        u0_early, u0, g_early, g, k_early, k,
    )
    low, high = shift(high_rows, "gy", 1), shift(low_rows, "gy", -1)
    return tuple(call(
        last_kernel, [(8, 8, 512), (8, 8, 512)],
        [(128, 128), (8, 2, 16, 128), (14, *last), (12, *last), (8, *last), (2, 8, 8, 512)],
        v1, low, high, u0, g, *faces, to_hbm=True, extra=[pltpu.SemaphoreType.DMA((2,))],
    ))


def solution(mesh):
    placed = (P("gx", "gy", None), P("gx", "gy", None))
    return jax.shard_map(per_device, mesh=mesh, in_specs=placed, out_specs=placed, check_vma=False)
```

```python
import jax
import jax.numpy as jnp
import ml_dtypes
import numpy as np
from jax import lax
from jax.experimental import pallas as pl
from jax.experimental.pallas import tpu as pltpu
from jax.sharding import PartitionSpec as P

ABSORPTION = 0.05
DAMPING = 0.8
F32 = jnp.float32
LANES = 128


def z_next(v):
    first = pltpu.roll(v[0], LANES - 1, 1)[None]
    return first if v.shape[0] == 1 else jnp.concatenate([v[1:], first], axis=0)


def z_prev(v):
    last = pltpu.roll(v[-1], 1, 1)[None]
    return last if v.shape[0] == 1 else jnp.concatenate([last, v[:-1]], axis=0)


def y_next(v):
    return pltpu.roll(v, v.shape[1] - 1, 1)


def y_prev(v):
    return pltpu.roll(v, 1, 1)


def flux_sum(u, u_next, flux_low, fx, fy, fz):
    flux_high = fx * (u - u_next)
    flux_y = fy * (u - y_next(u))
    flux_z = fz * (u - z_next(u))
    total = (flux_high - flux_low) + (flux_y - y_prev(flux_y)) + (flux_z - z_prev(flux_z))
    return ABSORPTION * u + total, flux_high


class Slabs:
    def __init__(self, flat, rows, parts=4):
        self.flat, self.rows, self.parts = flat, rows, parts

    def at(self, i):
        size = self.parts * self.rows
        return pl.ds(i * size, size)

    def __getitem__(self, i):
        return self.flat[self.at(i), :].reshape(self.parts, self.rows, LANES)

    def __setitem__(self, i, value):
        self.flat[self.at(i), :] = value.reshape(self.parts * self.rows, LANES)

    def part(self, i, start, size, step=1):
        where = lambda r: pl.ds((self.parts * i + r) * self.rows + start, size, step)
        return jnp.stack([self.flat[where(r), :] for r in range(self.parts)])

    def put(self, i, start, value):
        for r in range(self.parts):
            self.flat[pl.ds((self.parts * i + r) * self.rows + start, value.shape[1]), :] = value[r]


class Parted:
    def __init__(self, inner, outer, start, stop):
        self.inner, self.outer, self.start, self.stop = inner, outer, start, stop

    def place(self, i):
        if self.start <= i < self.stop:
            return self.inner, i - self.start
        return self.outer, i if i < self.start else i - (self.stop - self.start)

    def __getitem__(self, i):
        buffer, at = self.place(i)
        return buffer[at]

    def __setitem__(self, i, value):
        buffer, at = self.place(i)
        buffer[at] = value

    def part(self, i, start, size):
        buffer, at = self.place(i)
        if isinstance(buffer, (Parted, Slabs)):
            return buffer.part(at, start, size)
        return buffer[at, :, start : start + size, :]


def get(ref, i, rows):
    if rows is None:
        return ref[i]
    return ref.part(i, *rows) if hasattr(ref, "part") else ref[i, :, rows[0] : rows[0] + rows[1], :]


def put(ref, i, rows, value):
    if isinstance(ref, Parted):
        put(*ref.place(i), rows, value)
    elif rows is None:
        ref[i] = value
    else:
        ref[i, :, rows[0] : rows[0] + rows[1], :] = value


def every_row(i):
    return None


def face_pass(count, k_ref, fx, fy, fz, w, scale, k_at=0, done=(), rows=every_row):
    half = 0.5 * scale
    for i in range(count + 1):
        if i not in done or i - 1 not in done:
            fx[i] = half * (k_ref[k_at + i] + k_ref[k_at + 1 + i])
        if i == 0 or i - 1 in done:
            continue
        some = rows(i - 1)
        k = get(k_ref, k_at + i, some)
        face_y = half * (k + y_next(k))
        face_z = half * (k + z_next(k))
        diag = ABSORPTION + (get(fx, i, some) + get(fx, i - 1, some) + face_y + y_prev(face_y) + face_z + z_prev(face_z))
        put(fy, i - 1, some, face_y)
        put(fz, i - 1, some, face_z)
        put(w, i - 1, some, DAMPING / diag)


def sweep_pass(count, u_ref, u_at, faces_at, g_ref, g_at, fx, fy, fz, w, out, out_at, last=False, done=(), rows=every_row):
    low, low_rows = None, None
    for i in range(count):
        if i in done:
            low = None
            continue
        some, f = rows(i), faces_at + i
        u, u_next = get(u_ref, u_at + 1 + i, some), get(u_ref, u_at + 2 + i, some)
        if low is None or low_rows != some:
            low = get(fx, f, some) * (get(u_ref, u_at + i, some) - u)
        applied, low = flux_sum(u, u_next, low, get(fx, f + 1, some), get(fy, f, some), get(fz, f, some))
        low_rows = some
        rest = get(g_ref, g_at + i, some) - applied
        put(out, out_at + i, some, rest if last else u + get(w, f, some) * rest)


def inverse_permutation():
    z, at = np.arange(512)[None, :], np.arange(512)[:, None]
    return jnp.asarray((z == 4 * (at % LANES) + at // LANES).astype(ml_dtypes.bfloat16))


def permutation(inverse):
    z = lax.broadcasted_iota(jnp.int32, (512, 512), 1 if inverse else 0)
    at = lax.broadcasted_iota(jnp.int32, (512, 512), 0 if inverse else 1)
    return jnp.where(z == 4 * (at % LANES) + at // LANES, 1.0, 0.0).astype(jnp.bfloat16)


def rearrange(rows, matrix):
    count = rows.shape[0]
    top = rows.astype(jnp.bfloat16)
    rest = rows - top.astype(F32)
    middle = rest.astype(jnp.bfloat16)
    bottom = (rest - middle.astype(F32)).astype(jnp.bfloat16)
    parts = jnp.concatenate([top, middle, bottom], axis=0)
    moved = lax.dot_general(parts, matrix, (((1,), (0,)), ((), ())), preferred_element_type=F32)
    return (moved[0:count] + moved[count : 2 * count]) + moved[2 * count :]


def permute_kernel(me, held, own_flat, to_first, to_second):
    matrix = permutation(False)
    moved = rearrange(held[...].reshape(128, 512), matrix)
    for x in range(16):
        for r in range(4):
            own_flat[32 * x + 8 * r : 32 * x + 8 * r + 8] = moved[8 * x : 8 * x + 8, LANES * r : LANES * r + LANES]
    own = Slabs(own_flat, 8)
    even = lax.rem(me[0], 2) == 0
    for take, high, low in ((even, to_second, to_first), (jnp.logical_not(even), to_first, to_second)):
        @pl.when(take)
        def _(high=high, low=low):
            for i in range(6):
                high[i] = own[2 + i]
                low[i] = own[i]
            for i in range(6, 14):
                high[i] = own[2 + i]
                low[i] = own[2 + i]


G_BORDER, K_BORDER = 6, 8
G_SLABS, K_SLABS = 8 + 2 * G_BORDER, 8 + 2 * K_BORDER
G_REACH = (5, 4, 3, 2, 1, 0)
K_REACH = (6, 6, 4, 4, 2, 1, 0)


def row_parts():
    for array, reaches, border in ((0, G_REACH, G_BORDER), (1, K_REACH, K_BORDER)):
        for d, reach in enumerate(reaches, 1):
            yield array, d, reach, border


FACE_ROWS = 32 * (len(G_REACH) + len(K_REACH))
CORNER_ROWS = 8 * (sum(G_REACH) + sum(K_REACH))


def face_kernel(own, to_high, to_low):
    for i, (array, d, _, _) in enumerate(row_parts()):
        for out, y in ((to_high, 8 - d), (to_low, d - 1)):
            out[32 * i : 32 * i + 32] = own[pl.ds(256 * array + y, 32, 8), :]


def corners():
    at = 0
    for array, d, reach, border in row_parts():
        for column in (border - reach, border + 8):
            if reach:
                yield array, d, column, 4 * reach, at
                at += 4 * reach


def wide_kernel(me, own, first, second, flat, to_high, to_low):
    out, own = Slabs(flat, 8), Slabs(own, 8)

    def put(at, source, start, size):
        for i in range(size):
            out[at + i] = source[start + i]

    put(6, own, 0, 8)
    put(28, own, 8, 8)
    even = lax.rem(me[0], 2) == 0
    for take, left, right in ((even, first, second), (jnp.logical_not(even), second, first)):
        @pl.when(take)
        def _(left=left, right=right):
            put(0, left, 0, 6)
            put(14, right, 0, 6)
            put(20, left, 6, 8)
            put(36, right, 6, 8)
    for array, d, column, size, at in corners():
        base = (G_SLABS * array + column) * 32
        to_high[at : at + size] = flat[pl.ds(base + 8 - d, size, 8), :]
        to_low[at : at + size] = flat[pl.ds(base + d - 1, size, 8), :]


def early_kernel(own, low, high, g_flat, k_flat, fx, fy, fz, w, uf, u0, res):
    own, flats = Slabs(own, 8), (g_flat, k_flat)
    g, k = Slabs(g_flat, 24), Slabs(k_flat, 24)
    for i in range(8):
        g.put(i, 8, own[i])
        k.put(i, 8, own[8 + i])
    for i, (array, d, _, _) in enumerate(row_parts()):
        flats[array][pl.ds(8 - d, 32, 24), :] = low[32 * i : 32 * i + 32]
        flats[array][pl.ds(15 + d, 32, 24), :] = high[32 * i : 32 * i + 32]
    face_pass(6, k, fx, fy, fz, w, 1.0)
    for i in range(6):
        uf[i] = w[i] * g[1 + i]
    sweep_pass(4, uf, 0, 1, g, 2, fx, fy, fz, w, u0, 0)
    sweep_pass(2, u0, 0, 2, g, 3, fx, fy, fz, w, res, 0, last=True)


def fine_kernel(me, wide, low_corners, high_corners, g_early, k_early, fx_early, fy_early, fz_early, w_early, uf_early,
                u0_early, res_early, piece, u0_kept, g_flat, k_flat, u1, rhs, u0_edge, fx, fy, fz, w, uf, res, s1, sc,
                mx, my, mz, mw, mf, mr, ck):
    flats = g_flat, k_flat
    wide, g, k = Slabs(wide, 8), Slabs(g_flat, 24), Slabs(k_flat, 24)
    for i in range(12):
        g.put(i, 8, wide[i if i < 6 else i + 8])
    for i in range(16):
        k.put(i, 8, wide[G_SLABS + (i if i < 8 else i + 8)])
    for array, d, column, size, at in corners():
        slab = column if column < (G_BORDER, K_BORDER)[array] else column - 8
        flats[array][pl.ds(slab * 96 + 8 - d, size, 24), :] = low_corners[at : at + size]
        flats[array][pl.ds(slab * 96 + 15 + d, size, 24), :] = high_corners[at : at + size]
    g, k = Parted(Slabs(g_early, 24), g, 6, 14), Parted(Slabs(k_early, 24), k, 8, 16)
    fx = Parted(fx_early, fx, 7, 14)
    fy, fz, w, uf = [Parted(*pair, 7, 13) for pair in ((fy_early, fy), (fz_early, fz), (w_early, w), (uf_early, uf))]
    u0 = Parted(Parted(u0_early, u0_kept, 5, 9), u0_edge, 2, 16)
    res = Parted(res_early, res, 7, 9)
    def beside(first_x, border):
        return lambda i: (4, 16) if first_x + i <= -border or first_x + i >= 7 + border else None

    face_pass(20, k, fx, fy, fz, w, 1.0, k_at=1, done=range(7, 13), rows=beside(-6, 3))
    for i in range(20):
        if not 7 <= i < 13:
            some = beside(-6, 3)(i)
            put(uf, i, some, get(w, i, some) * get(g, i, some))
    sweep_pass(18, uf, 0, 1, g, 1, fx, fy, fz, w, u0, 0, done=range(7, 11), rows=beside(-5, 2))
    sweep_pass(16, u0, 0, 2, g, 2, fx, fy, fz, w, res, 0, last=True, done=range(7, 9), rows=beside(-4, 1))
    for x in range(8):
        both = res[2 * x] + res[2 * x + 1]
        s1[x, 0] = both[0] + both[1]
        s1[x, 1] = both[2] + both[3]
    for x in range(10):
        both = k[2 + 2 * x] + k[3 + 2 * x]
        sc[x, 0] = both[0] + both[1]
        sc[x, 1] = both[2] + both[3]

    def rows(ref, x, start):
        return jnp.stack(
            [ref[x, r, pl.ds(start, 8, 2), :] + ref[x, r, pl.ds(start + 1, 8, 2), :] for r in range(2)]
        ) * 0.125

    half = 0.5 * 0.25
    k_mid = [rows(sc, x, 4) for x in range(10)]
    mx[0] = half * (k_mid[0] + k_mid[1])
    for x in range(8):
        here = k_mid[x + 1]
        face_x = half * (here + k_mid[x + 2])
        face_y = half * (here + rows(sc, x + 1, 6))
        face_z = half * (here + z_next(here))
        diag = ABSORPTION + (
            mx[x] + face_x + face_y + half * (here + rows(sc, x + 1, 2)) + face_z + z_prev(face_z)
        )
        mx[x + 1], my[x], mz[x] = face_x, face_y, face_z
        mw[x] = DAMPING / diag
        rhs[x] = rows(s1, x, 4)
        mf[x] = mw[x] * rhs[x]
    sweep_pass(6, mf, 0, 1, rhs, 1, mx, my, mz, mw, u1, 0)
    sweep_pass(4, u1, 0, 2, rhs, 2, mx, my, mz, mw, mr, 0, last=True)
    for x in range(4):
        both = k_mid[2 * x + 1] + k_mid[2 * x + 2]
        ck[x] = both[0] + both[1]
    k2 = [(ck[x, pl.ds(0, 4, 2), :] + ck[x, pl.ds(1, 4, 2), :]) * 0.125 for x in range(4)]
    half = 0.5 * 0.0625
    for x in range(2):
        here = k2[x + 1][1:3]
        face_z = half * (here + pltpu.roll(here, LANES - 1, 1))
        diag = ABSORPTION + (
            half * (here + k2[x][1:3]) + half * (here + k2[x + 2][1:3])
            + half * (here + k2[x + 1][0:2]) + half * (here + k2[x + 1][2:4])
            + face_z + pltpu.roll(face_z, 1, 1)
        )
        both = mr[2 * x] + mr[2 * x + 1]
        ck[x] = both[0] + both[1]
        first_sweep = DAMPING / diag * ((ck[x, pl.ds(2, 2, 2), :] + ck[x, pl.ds(3, 2, 2), :]) * 0.125)
        for j in range(2):
            ck[3, 2 * j + x : 2 * j + x + 1, :] = first_sweep[j : j + 1]
            ck[3, 4 + 2 * j + x : 5 + 2 * j + x, :] = here[j : j + 1]
    level_2 = ck[3]
    for to in range(piece.shape[0]):
        piece[to, 0:8, :] = level_2
    count = piece.shape[0]
    for to, column in ((lax.rem(me[0] + 1, count), 0), (lax.rem(me[0] + count - 1, count), 1)):
        for r in range(2):
            for x in range(3):
                at = 8 + 4 * (2 * x + r)
                piece[to, at : at + 4, :] = u1[column + x + 1, r, 2:6, :]
            piece[to, 32 + 4 * r : 36 + 4 * r, :] = rhs[column + 3, r, 2:6, :]


def prepare_middle_kernel(k_early, k_flat, fx, fy, fz, w, k_mid, sums):
    k = Parted(Slabs(k_early, 24), Slabs(k_flat, 24), 8, 16)
    for x in range(12):
        both = k[2 * x] + k[2 * x + 1]
        for r in range(2):
            sums[r] = both[2 * r] + both[2 * r + 1]
            k_mid[x, r] = (sums[r, pl.ds(4, 8, 2), :] + sums[r, pl.ds(5, 8, 2), :]) * 0.125
    face_pass(10, k_mid, fx, fy, fz, w, 0.25)


def prepare_kernel(u0_early, u0, g_early, g_flat, k_early, k_flat, u_out, g_out, fx, fy, fz, w, k_rows):
    g, k = Parted(Slabs(g_early, 24), Slabs(g_flat, 24), 6, 14), Parted(Slabs(k_early, 24), Slabs(k_flat, 24), 8, 16)
    u0 = Parted(u0_early, u0, 5, 9)
    for i in range(14):
        u_out[i] = u0.part(i, 4, 16)
        k_rows[i] = k.part(i + 5, 4, 16)
    for i in range(12):
        g_out[i] = g.part(i + 4, 4, 16)
    face_pass(12, k_rows, fx, fy, fz, w, 1.0)


EDGE_ROWS = 4 * 20 + 2 * 20 + 16


def middle_kernel(me, gathered, u1, rhs, here, to_high, to_low, level_1):
    count = gathered.shape[0]
    for block in range(11):
        source = lax.rem(me[0] + (block - 5 + count * 5), count)
        for j in range(2):
            for array in range(2):
                at = 4 * array + 2 * j
                here[2 * j + array, 2 * block : 2 * block + 2, :] = gathered[source, at : at + 2, :]
    u_flat, r_flat = level_1.at[0:192], level_1.at[192:352]
    u, g = Slabs(u_flat, 8, 2), Slabs(r_flat, 8, 2)
    for x in range(6):
        u[3 + x] = u1[x]
    for x in range(8):
        g[1 + x] = rhs[x]
    for source, column, edge in ((lax.rem(me[0] + count - 1, count), 0, 0), (lax.rem(me[0] + 1, count), 9, 9)):
        for r in range(2):
            for x in range(3):
                at = 8 + 4 * (2 * x + r)
                to = 8 * (2 * (column + x) + r) + 2
                u_flat[to : to + 4, :] = gathered[source, at : at + 4, :]
            to = 8 * (2 * edge + r) + 2
            r_flat[to : to + 4, :] = gathered[source, 32 + 4 * r : 36 + 4 * r, :]
    for out, row, rhs_row in ((to_high, 4, 5), (to_low, 2, 2)):
        for slab in range(4):
            out[20 * slab : 20 * slab + 20] = here[slab, 1:21]
        for i in range(2):
            out[80 + 20 * i : 100 + 20 * i] = level_1[pl.ds(16 + row + i, 20, 8), :]
        out[120:136] = level_1[pl.ds(192 + 16 + rhs_row, 16, 8), :]


SPREAD = (16, 14, 12, 10, 8, 6)


def spread(j, upward):
    d = j if upward else 5 - j
    return 3 + d, SPREAD[d], 2 * sum(SPREAD[:d])


def three_kernel(me, here, low, high, to_first, to_second):
    blocks = (low, here, high)
    even = lax.rem(me[0], 2) == 0
    for take, to_high, to_low in ((even, to_second, to_first), (jnp.logical_not(even), to_first, to_second)):
        @pl.when(take)
        def _(to_high=to_high, to_low=to_low):
            for j in range(6):
                source = blocks[j // 2]
                for out, upward in ((to_high, False), (to_low, True)):
                    start, size, at = spread(j, upward)
                    for array in range(2):
                        slab = 2 * (j % 2) + array
                        if source is here:
                            values = here[slab, start : start + size]
                        else:
                            values = source[20 * slab + start - 1 : 20 * slab + start - 1 + size]
                        out[at + size * array : at + size * array + size] = values


def window(reach):
    return (7, 8) if reach <= 3 else (3, 16) if reach <= 7 else (1, 24)


def coarse_kernel(me, first, here, second, left, right, level_1, fx, fy, fz, w, v_flat_out, to_high, to_low,
                  u, other, c, start, weights, v_flat, r_flat, va):
    half = 0.5 * 0.0625
    even = lax.rem(me[0], 2) == 0
    for take, below, above in ((even, first, second), (jnp.logical_not(even), second, first)):
        @pl.when(take)
        def _(below=below, above=above):
            for j in range(6):
                for source, upward, y in ((below, False, j), (above, True, 12 + j)):
                    column, size, at = spread(j, upward)
                    start[y, column : column + size] = source[at : at + size]
                    c[y, column : column + size] = source[at + size : at + 2 * size]
    for j in range(6):
        block, slab = (left, here, right)[j // 2], 2 * (j % 2)
        if block is here:
            start[6 + j, 0:24] = here[slab]
            c[6 + j, 0:24] = here[slab + 1]
        else:
            start[6 + j, 1:21] = block[20 * slab : 20 * slab + 20]
            c[6 + j, 1:21] = block[20 * slab + 20 : 20 * slab + 40]

    def reach(y, step):
        return 9 - step - max(0, 7 - y, y - 10)

    def at(ref, y, lo, size):
        return ref[y, lo : lo + size]

    for y in range(1, 17):
        lo, size = window(reach(y, 1))
        k = at(c, y, lo, size)
        face_z = half * (k + pltpu.roll(k, LANES - 1, 1))
        faces = [half * (k + at(c, y, lo + 1, size)), half * (k + at(c, y, lo - 1, size))]
        faces += [half * (k + at(c, y + 1, lo, size)), half * (k + at(c, y - 1, lo, size))]
        faces += [face_z, pltpu.roll(face_z, 1, 1)]
        scale = DAMPING / (ABSORPTION + ((faces[0] + faces[1]) + (faces[2] + faces[3]) + (faces[4] + faces[5])))
        for i, face in enumerate(faces):
            weights[i, y, lo : lo + size] = scale * face
    old = start
    for step in range(1, 8):
        new = (u, other)[step % 2]
        for y in range(step, 18 - step):
            lo, size = window(reach(y, step))
            now = at(old, y, lo, size)
            along_x = at(weights.at[0], y, lo, size) * at(old, y, lo + 1, size) + at(weights.at[1], y, lo, size) * at(old, y, lo - 1, size)
            along_y = at(weights.at[2], y, lo, size) * at(old, y + 1, lo, size) + at(weights.at[3], y, lo, size) * at(old, y - 1, lo, size)
            along_z = (
                at(weights.at[4], y, lo, size) * pltpu.roll(now, LANES - 1, 1)
                + at(weights.at[5], y, lo, size) * pltpu.roll(now, 1, 1)
            )
            new[y, lo : lo + size] = ((1.0 - DAMPING) * now + at(start, y, lo, size)) + along_y + (along_x + along_z)
        old = new
    u = old
    v_flat[...] = level_1[0:192]
    r_flat[...] = level_1[192:352]
    for source, row, rhs_row in ((left, 0, 1), (right, 6, 6)):
        for i in range(2):
            v_flat[pl.ds(16 + row + i, 20, 8), :] = source[80 + 20 * i : 100 + 20 * i]
        r_flat[pl.ds(16 + rhs_row, 16, 8), :] = source[120:136]
    v, rhs = Slabs(v_flat, 8, 2), Slabs(r_flat, 8, 2)
    for x in range(6):
        rows = jnp.concatenate(
            [jnp.broadcast_to(u[7 + j, 8 + x : 9 + x, :], (2, LANES)) for j in range(4)], axis=0
        )
        for twin in range(2):
            v[2 * x + twin] = v[2 * x + twin] + rows[None]
    sweep_pass(10, v, 0, 0, rhs, 0, fx, fy, fz, w, va, 0)
    sweep_pass(8, va, 0, 1, rhs, 1, fx, fy, fz, w, Slabs(v_flat_out, 8, 2), 0)
    for out, row in ((to_high, 4), (to_low, 2)):
        for i in range(2):
            out[16 * i : 16 * i + 16] = v_flat_out[pl.ds(row + i, 16, 8), :]


def last_kernel(v_here, v_low, v_high, u0, g, fx, fy, fz, w, matrix, correction, residual, v_flat, wide, ua, ub, res, held, left):
    v_flat[...] = v_here[...]
    for source, row in ((v_low, 0), (v_high, 6)):
        for i in range(2):
            v_flat[pl.ds(row + i, 16, 8), :] = source[16 * i : 16 * i + 16]
    for x in range(8):
        for r in range(2):
            rows = v_flat[8 * (2 * x + r) : 8 * (2 * x + r) + 8]
            wide[x, r, pl.ds(0, 8, 2), :] = rows
            wide[x, r, pl.ds(1, 8, 2), :] = rows
    for i in range(14):
        fine = wide[(i + 1) // 2]
        ua[i] = u0[i] + jnp.stack([fine[0], fine[0], fine[1], fine[1]])
    sweep_pass(12, ua, 0, 0, g, 0, fx, fy, fz, w, ub, 0)
    sweep_pass(10, ub, 0, 1, g, 1, fx, fy, fz, w, ua, 0)
    copies = []

    def leave(index, source, at, out, start, size):
        rows = [
            jnp.concatenate([source[at + x, r, 4:12, :] for r in range(4)], axis=1) for x in range(start, start + size)
        ]
        held[index, start : start + size] = rearrange(jnp.concatenate(rows, axis=0), matrix[...]).reshape(size, 8, 512)
        part = pl.ds(start, size)
        copy = pltpu.make_async_copy(held.at[index, part], out.at[part], left.at[len(copies)])
        copy.start()
        copies.append(copy)

    leave(0, ua, 1, correction, 0, 8)
    sweep_pass(4, ua, 0, 2, g, 2, fx, fy, fz, w, res, 0, last=True)
    leave(1, res, 0, residual, 0, 4)
    sweep_pass(4, ua, 4, 6, g, 6, fx, fy, fz, w, res, 4, last=True)
    leave(1, res, 0, residual, 4, 4)
    for copy in copies:
        copy.wait()


VMEM = pl.BlockSpec(memory_space=pltpu.VMEM)
SMEM = pl.BlockSpec(memory_space=pltpu.SMEM)
HBM = pl.BlockSpec(memory_space=pltpu.HBM)


def call(kernel, outs, scratch, *arrays, scalars=0, to_hbm=False, extra=()):
    return pl.pallas_call(
        kernel,
        out_shape=[jax.ShapeDtypeStruct(shape, F32) for shape in outs],
        in_specs=[SMEM] * scalars + [VMEM] * (len(arrays) - scalars),
        out_specs=[HBM if to_hbm else VMEM] * len(outs),
        scratch_shapes=[pltpu.VMEM(shape, F32) for shape in scratch] + list(extra),
        compiler_params=pltpu.CompilerParams(vmem_limit_bytes=32 * 2**20),
    )(*arrays)


def shift(array, axis, by):
    count = lax.axis_size(axis)
    return lax.ppermute(array, axis, [(i, (i + by) % count) for i in range(count)])


def swap(array, axis, start, by=1):
    count = lax.axis_size(axis)
    pairs = [(i, (i + by) % count) for i in range(start, count, 2)]
    return lax.ppermute(array, axis, pairs + [(j, i) for i, j in pairs])


def per_device(right_side, coefficient):
    me_x = lax.axis_index("gx").astype(jnp.int32).reshape(1)
    me_y = lax.axis_index("gy").astype(jnp.int32).reshape(1)
    count = lax.axis_size("gx")
    border = (G_BORDER + K_BORDER, 4, 8, 128)
    own, first, second = call(
        permute_kernel, [(512, 128), border, border], [], me_x, jnp.stack([right_side, coefficient]), scalars=1
    )
    first, second = swap(first, "gx", 1), swap(second, "gx", 0)
    high, low = call(face_kernel, [(FACE_ROWS, 128), (FACE_ROWS, 128)], [], own)
    low, high = shift(high, "gy", 1), shift(low, "gy", -1)
    wide, high_corners, low_corners = call(
        wide_kernel, [((G_SLABS + K_SLABS) * 32, 128), (CORNER_ROWS, 128), (CORNER_ROWS, 128)], [],
        me_x, own, first, second, scalars=1,
    )
    low_corners, high_corners = shift(high_corners, "gy", 1), shift(low_corners, "gy", -1)
    fine, mid, last = (4, 24, 128), (2, 8, 128), (4, 16, 128)
    early = call(
        early_kernel,
        [(8 * 96, 128), (8 * 96, 128), (7, *fine), (6, *fine), (6, *fine), (6, *fine), (6, *fine), (4, *fine), (2, *fine)],
        [], own, low, high,
    )
    g_early, k_early, u0_early = early[0], early[1], early[7]
    piece, u0, g, k, u1, rhs = call(
        fine_kernel,
        [(count, 40, 128), (10, *fine), (12 * 96, 128), (16 * 96, 128), (6, *mid), (8, *mid)],
        [(4, *fine), (14, *fine), (14, *fine), (14, *fine), (14, *fine), (14, *fine), (14, *fine), (8, 2, 24, 128), (10, 2, 24, 128),
         (9, *mid), (8, *mid), (8, *mid), (8, *mid), (8, *mid), (4, *mid), (4, 8, 128)],
        me_x, wide, low_corners, high_corners, *early, scalars=1,
    )
    piece, u0, g, k, u1, rhs = lax.optimization_barrier((piece, u0, g, k, u1, rhs))
    gathered = lax.all_to_all(piece, "gx", 0, 0)
    gathered, u0, g, k, u1, rhs = lax.optimization_barrier((gathered, u0, g, k, u1, rhs))
    here, high, low, level_1 = call(
        middle_kernel, [(4, 24, 128), (EDGE_ROWS, 128), (EDGE_ROWS, 128), (352, 128)], [], me_x, gathered, u1, rhs, scalars=1
    )
    low, high = shift(high, "gy", 1), shift(low, "gy", -1)
    first, second = call(three_kernel, [(136, 128), (136, 128)], [], me_y, here, low, high, scalars=1)
    first, second = swap(first, "gy", 1, 3), swap(second, "gy", 0, 3)
    faces = call(
        prepare_middle_kernel, [(11, *mid), (10, *mid), (10, *mid), (10, *mid)], [(12, *mid), (2, 24, 128)], k_early, k
    )
    rows = (18, 32, 128)
    v1, high_rows, low_rows = call(
        coarse_kernel, [(128, 128), (32, 128), (32, 128)],
        [rows, rows, rows, rows, (6, *rows), (192, 128), (160, 128), (10, *mid)],
        me_y, first, here, second, low, high, level_1, *faces, scalars=1,
    )
    u0, g, *faces = call(
        prepare_kernel, [(14, *last), (12, *last), (13, *last), (12, *last), (12, *last), (12, *last)], [(14, *last)],
        u0_early, u0, g_early, g, k_early, k,
    )
    low, high = shift(high_rows, "gy", 1), shift(low_rows, "gy", -1)
    return tuple(call(
        last_kernel, [(8, 8, 512), (8, 8, 512)],
        [(128, 128), (8, 2, 16, 128), (14, *last), (12, *last), (8, *last), (2, 8, 8, 512)],
        v1, low, high, u0, g, *faces, inverse_permutation(), to_hbm=True, extra=[pltpu.SemaphoreType.DMA((3,))],
    ))


def solution(mesh):
    placed = (P("gx", "gy", None), P("gx", "gy", None))
    return jax.shard_map(per_device, mesh=mesh, in_specs=placed, out_specs=placed, check_vma=False)
```

```python
import jax
import jax.numpy as jnp
import ml_dtypes
import numpy as np
from jax import lax
from jax.experimental import pallas as pl
from jax.experimental.pallas import tpu as pltpu
from jax.sharding import PartitionSpec as P

ABSORPTION = 0.05
DAMPING = 0.8
F32 = jnp.float32
LANES = 128


def z_next(v):
    first = pltpu.roll(v[0], LANES - 1, 1)[None]
    return first if v.shape[0] == 1 else jnp.concatenate([v[1:], first], axis=0)


def z_prev(v):
    last = pltpu.roll(v[-1], 1, 1)[None]
    return last if v.shape[0] == 1 else jnp.concatenate([last, v[:-1]], axis=0)


def y_next(v):
    return pltpu.roll(v, v.shape[1] - 1, 1)


def y_prev(v):
    return pltpu.roll(v, 1, 1)


def flux_sum(u, u_next, flux_low, fx, fy, fz):
    flux_high = fx * (u - u_next)
    flux_y = fy * (u - y_next(u))
    flux_z = fz * (u - z_next(u))
    total = (flux_high - flux_low) + (flux_y - y_prev(flux_y)) + (flux_z - z_prev(flux_z))
    return ABSORPTION * u + total, flux_high


class Slabs:
    def __init__(self, flat, rows, parts=4):
        self.flat, self.rows, self.parts = flat, rows, parts

    def at(self, i):
        size = self.parts * self.rows
        return pl.ds(i * size, size)

    def __getitem__(self, i):
        return self.flat[self.at(i), :].reshape(self.parts, self.rows, LANES)

    def __setitem__(self, i, value):
        self.flat[self.at(i), :] = value.reshape(self.parts * self.rows, LANES)

    def part(self, i, start, size, step=1):
        where = lambda r: pl.ds((self.parts * i + r) * self.rows + start, size, step)
        return jnp.stack([self.flat[where(r), :] for r in range(self.parts)])

    def put(self, i, start, value):
        for r in range(self.parts):
            self.flat[pl.ds((self.parts * i + r) * self.rows + start, value.shape[1]), :] = value[r]


class Parted:
    def __init__(self, inner, outer, start, stop):
        self.inner, self.outer, self.start, self.stop = inner, outer, start, stop

    def place(self, i):
        if self.start <= i < self.stop:
            return self.inner, i - self.start
        return self.outer, i if i < self.start else i - (self.stop - self.start)

    def __getitem__(self, i):
        buffer, at = self.place(i)
        return buffer[at]

    def __setitem__(self, i, value):
        buffer, at = self.place(i)
        buffer[at] = value

    def part(self, i, start, size):
        buffer, at = self.place(i)
        if isinstance(buffer, (Parted, Slabs)):
            return buffer.part(at, start, size)
        return buffer[at, :, start : start + size, :]


def get(ref, i, rows):
    if rows is None:
        return ref[i]
    return ref.part(i, *rows) if hasattr(ref, "part") else ref[i, :, rows[0] : rows[0] + rows[1], :]


def put(ref, i, rows, value):
    if isinstance(ref, Parted):
        put(*ref.place(i), rows, value)
    elif rows is None:
        ref[i] = value
    else:
        ref[i, :, rows[0] : rows[0] + rows[1], :] = value


def every_row(i):
    return None


def face_pass(count, k_ref, fx, fy, fz, w, scale, k_at=0, done=(), rows=every_row):
    half = 0.5 * scale
    for i in range(count + 1):
        if i not in done or i - 1 not in done:
            fx[i] = half * (k_ref[k_at + i] + k_ref[k_at + 1 + i])
        if i == 0 or i - 1 in done:
            continue
        some = rows(i - 1)
        k = get(k_ref, k_at + i, some)
        face_y = half * (k + y_next(k))
        face_z = half * (k + z_next(k))
        diag = ABSORPTION + (get(fx, i, some) + get(fx, i - 1, some) + face_y + y_prev(face_y) + face_z + z_prev(face_z))
        put(fy, i - 1, some, face_y)
        put(fz, i - 1, some, face_z)
        put(w, i - 1, some, DAMPING / diag)


def sweep_pass(count, u_ref, u_at, faces_at, g_ref, g_at, fx, fy, fz, w, out, out_at, last=False, done=(), rows=every_row):
    low, low_rows = None, None
    for i in range(count):
        if i in done:
            low = None
            continue
        some, f = rows(i), faces_at + i
        u, u_next = get(u_ref, u_at + 1 + i, some), get(u_ref, u_at + 2 + i, some)
        if low is None or low_rows != some:
            low = get(fx, f, some) * (get(u_ref, u_at + i, some) - u)
        applied, low = flux_sum(u, u_next, low, get(fx, f + 1, some), get(fy, f, some), get(fz, f, some))
        low_rows = some
        rest = get(g_ref, g_at + i, some) - applied
        put(out, out_at + i, some, rest if last else u + get(w, f, some) * rest)


def inverse_permutation():
    z, at = np.arange(512)[None, :], np.arange(512)[:, None]
    return jnp.asarray((z == 4 * (at % LANES) + at // LANES).astype(ml_dtypes.bfloat16))


def permutation(inverse):
    z = lax.broadcasted_iota(jnp.int32, (512, 512), 1 if inverse else 0)
    at = lax.broadcasted_iota(jnp.int32, (512, 512), 0 if inverse else 1)
    return jnp.where(z == 4 * (at % LANES) + at // LANES, 1.0, 0.0).astype(jnp.bfloat16)


def rearrange(rows, matrix):
    count = rows.shape[0]
    top = rows.astype(jnp.bfloat16)
    rest = rows - top.astype(F32)
    middle = rest.astype(jnp.bfloat16)
    bottom = (rest - middle.astype(F32)).astype(jnp.bfloat16)
    parts = jnp.concatenate([top, middle, bottom], axis=0)
    moved = lax.dot_general(parts, matrix, (((1,), (0,)), ((), ())), preferred_element_type=F32)
    return (moved[0:count] + moved[count : 2 * count]) + moved[2 * count :]


def permute_kernel(me, held, own_flat, to_first, to_second):
    matrix = permutation(False)
    moved = rearrange(held[...].reshape(128, 512), matrix)
    for x in range(16):
        for r in range(4):
            own_flat[32 * x + 8 * r : 32 * x + 8 * r + 8] = moved[8 * x : 8 * x + 8, LANES * r : LANES * r + LANES]
    own = Slabs(own_flat, 8)
    even = lax.rem(me[0], 2) == 0
    for take, high, low in ((even, to_second, to_first), (jnp.logical_not(even), to_first, to_second)):
        @pl.when(take)
        def _(high=high, low=low):
            for i in range(6):
                high[i] = own[2 + i]
                low[i] = own[i]
            for i in range(6, 14):
                high[i] = own[2 + i]
                low[i] = own[2 + i]


G_BORDER, K_BORDER = 6, 8
G_SLABS, K_SLABS = 8 + 2 * G_BORDER, 8 + 2 * K_BORDER
G_REACH = (5, 4, 3, 2, 1, 0)
K_REACH = (6, 6, 4, 4, 2, 1, 0)


def row_parts():
    for array, reaches, border in ((0, G_REACH, G_BORDER), (1, K_REACH, K_BORDER)):
        for d, reach in enumerate(reaches, 1):
            yield array, d, reach, border


FACE_ROWS = 32 * (len(G_REACH) + len(K_REACH))
CORNER_ROWS = 8 * (sum(G_REACH) + sum(K_REACH)) + 8


def face_kernel(own, to_high, to_low):
    for i, (array, d, _, _) in enumerate(row_parts()):
        for out, y in ((to_high, 8 - d), (to_low, d - 1)):
            out[32 * i : 32 * i + 32] = own[pl.ds(256 * array + y, 32, 8), :]


def corners():
    at = 0
    for array, d, reach, border in row_parts():
        for column in (border - reach, border + 8):
            if reach:
                yield array, d, column, 4 * reach, at
                at += 4 * reach


def wide_kernel(me, own, first, second, flat, to_high, to_low):
    out, own = Slabs(flat, 8), Slabs(own, 8)

    def put(at, source, start, size):
        for i in range(size):
            out[at + i] = source[start + i]

    put(6, own, 0, 8)
    put(28, own, 8, 8)
    even = lax.rem(me[0], 2) == 0
    for take, left, right in ((even, first, second), (jnp.logical_not(even), second, first)):
        @pl.when(take)
        def _(left=left, right=right):
            put(0, left, 0, 6)
            put(14, right, 0, 6)
            put(20, left, 6, 8)
            put(36, right, 6, 8)
    for array, d, column, size, at in corners():
        base = (G_SLABS * array + column) * 32
        to_high[at : at + size] = flat[pl.ds(base + 8 - d, size, 8), :]
        to_low[at : at + size] = flat[pl.ds(base + d - 1, size, 8), :]


def early_kernel(own, low, high, g_flat, k_flat, fx, fy, fz, w, uf, u0, res):
    own, flats = Slabs(own, 8), (g_flat, k_flat)
    g, k = Slabs(g_flat, 24), Slabs(k_flat, 24)
    for i in range(8):
        g.put(i, 8, own[i])
        k.put(i, 8, own[8 + i])
    for i, (array, d, _, _) in enumerate(row_parts()):
        flats[array][pl.ds(8 - d, 32, 24), :] = low[32 * i : 32 * i + 32]
        flats[array][pl.ds(15 + d, 32, 24), :] = high[32 * i : 32 * i + 32]
    face_pass(6, k, fx, fy, fz, w, 1.0)
    for i in range(6):
        uf[i] = w[i] * g[1 + i]
    sweep_pass(4, uf, 0, 1, g, 2, fx, fy, fz, w, u0, 0)
    sweep_pass(2, u0, 0, 2, g, 3, fx, fy, fz, w, res, 0, last=True)


def fine_kernel(me, wide, low_corners, high_corners, g_early, k_early, fx_early, fy_early, fz_early, w_early, uf_early,
                u0_early, res_early, piece, u0_kept, g_flat, k_flat, u1, rhs, u0_edge, fx, fy, fz, w, uf, res, s1, sc,
                mx, my, mz, mw, mf, mr, ck, near):
    flats = g_flat, k_flat
    wide, g, k = Slabs(wide, 8), Slabs(g_flat, 24), Slabs(k_flat, 24)
    for i in range(12):
        g.put(i, 8, wide[i if i < 6 else i + 8])
    for i in range(16):
        k.put(i, 8, wide[G_SLABS + (i if i < 8 else i + 8)])
    for array, d, column, size, at in corners():
        slab = column if column < (G_BORDER, K_BORDER)[array] else column - 8
        flats[array][pl.ds(slab * 96 + 8 - d, size, 24), :] = low_corners[at : at + size]
        flats[array][pl.ds(slab * 96 + 15 + d, size, 24), :] = high_corners[at : at + size]
    g, k = Parted(Slabs(g_early, 24), g, 6, 14), Parted(Slabs(k_early, 24), k, 8, 16)
    fx = Parted(fx_early, fx, 7, 14)
    fy, fz, w, uf = [Parted(*pair, 7, 13) for pair in ((fy_early, fy), (fz_early, fz), (w_early, w), (uf_early, uf))]
    u0 = Parted(Parted(u0_early, u0_kept, 5, 9), u0_edge, 2, 16)
    res = Parted(res_early, res, 7, 9)
    def beside(first_x, border):
        return lambda i: (4, 16) if first_x + i <= -border or first_x + i >= 7 + border else None

    face_pass(20, k, fx, fy, fz, w, 1.0, k_at=1, done=range(7, 13), rows=beside(-6, 3))
    for i in range(20):
        if not 7 <= i < 13:
            some = beside(-6, 3)(i)
            put(uf, i, some, get(w, i, some) * get(g, i, some))
    sweep_pass(18, uf, 0, 1, g, 1, fx, fy, fz, w, u0, 0, done=range(7, 11), rows=beside(-5, 2))
    sweep_pass(16, u0, 0, 2, g, 2, fx, fy, fz, w, res, 0, last=True, done=range(7, 9), rows=beside(-4, 1))
    for x in range(8):
        both = res[2 * x] + res[2 * x + 1]
        s1[x, 0] = both[0] + both[1]
        s1[x, 1] = both[2] + both[3]
    for x in range(10):
        both = k[2 + 2 * x] + k[3 + 2 * x]
        sc[x, 0] = both[0] + both[1]
        sc[x, 1] = both[2] + both[3]

    def rows(ref, x, start):
        return jnp.stack(
            [ref[x, r, pl.ds(start, 8, 2), :] + ref[x, r, pl.ds(start + 1, 8, 2), :] for r in range(2)]
        ) * 0.125

    half = 0.5 * 0.25
    k_mid = [rows(sc, x, 4) for x in range(10)]
    mx[0] = half * (k_mid[0] + k_mid[1])
    for x in range(8):
        here = k_mid[x + 1]
        face_x = half * (here + k_mid[x + 2])
        face_y = half * (here + rows(sc, x + 1, 6))
        face_z = half * (here + z_next(here))
        diag = ABSORPTION + (
            mx[x] + face_x + face_y + half * (here + rows(sc, x + 1, 2)) + face_z + z_prev(face_z)
        )
        mx[x + 1], my[x], mz[x] = face_x, face_y, face_z
        mw[x] = DAMPING / diag
        rhs[x] = rows(s1, x, 4)
        mf[x] = mw[x] * rhs[x]
    sweep_pass(6, mf, 0, 1, rhs, 1, mx, my, mz, mw, u1, 0)
    sweep_pass(4, u1, 0, 2, rhs, 2, mx, my, mz, mw, mr, 0, last=True)
    for x in range(4):
        both = k_mid[2 * x + 1] + k_mid[2 * x + 2]
        ck[x, 0:8] = both[0] + both[1]
    k2 = [(ck[x, pl.ds(0, 4, 2), :] + ck[x, pl.ds(1, 4, 2), :]) * 0.125 for x in range(4)]
    half = 0.5 * 0.0625
    for x in range(2):
        here = k2[x + 1][1:3]
        face_z = half * (here + pltpu.roll(here, LANES - 1, 1))
        diag = ABSORPTION + (
            half * (here + k2[x][1:3]) + half * (here + k2[x + 2][1:3])
            + half * (here + k2[x + 1][0:2]) + half * (here + k2[x + 1][2:4])
            + face_z + pltpu.roll(face_z, 1, 1)
        )
        both = mr[2 * x] + mr[2 * x + 1]
        ck[x, 0:8] = both[0] + both[1]
        first_sweep = DAMPING / diag * ((ck[x, pl.ds(2, 2, 2), :] + ck[x, pl.ds(3, 2, 2), :]) * 0.125)
        for j in range(2):
            ck[3, 2 * j + x : 2 * j + x + 1, :] = first_sweep[j : j + 1]
            ck[3, 4 + 2 * j + x : 5 + 2 * j + x, :] = here[j : j + 1]
    level_2 = ck[3, 0:8]
    for to in range(piece.shape[0]):
        piece[to, 0:8, :] = level_2
    count = piece.shape[0]
    for to, column in ((lax.rem(me[0] + 1, count), 0), (lax.rem(me[0] + count - 1, count), 1)):
        for r in range(2):
            for x in range(3):
                at = 4 * (2 * x + r)
                near[column, at : at + 4, :] = u1[column + x + 1, r, 2:6, :]
            near[column, 24 + 4 * r : 28 + 4 * r, :] = rhs[column + 3, r, 2:6, :]
        piece[to, 8:40, :] = near[column, 0:32, :]


def prepare_middle_kernel(k_early, k_flat, fx, fy, fz, w, k_mid, sums):
    k = Parted(Slabs(k_early, 24), Slabs(k_flat, 24), 8, 16)
    for x in range(12):
        both = k[2 * x] + k[2 * x + 1]
        for r in range(2):
            sums[r] = both[2 * r] + both[2 * r + 1]
            k_mid[x, r] = (sums[r, pl.ds(4, 8, 2), :] + sums[r, pl.ds(5, 8, 2), :]) * 0.125
    face_pass(10, k_mid, fx, fy, fz, w, 0.25)


def prepare_kernel(u0_early, u0, g_early, g_flat, k_early, k_flat, u_out, g_out, fx, fy, fz, w, k_rows):
    g, k = Parted(Slabs(g_early, 24), Slabs(g_flat, 24), 6, 14), Parted(Slabs(k_early, 24), Slabs(k_flat, 24), 8, 16)
    u0 = Parted(u0_early, u0, 5, 9)
    for i in range(14):
        u_out[i] = u0.part(i, 4, 16)
        k_rows[i] = k.part(i + 5, 4, 16)
    for i in range(12):
        g_out[i] = g.part(i + 4, 4, 16)
    face_pass(12, k_rows, fx, fy, fz, w, 1.0)


EDGE_ROWS = 4 * 20 + 2 * 20 + 16


def middle_kernel(me, gathered, u1, rhs, here, to_high, to_low, level_1):
    count = gathered.shape[0]
    for block in range(11):
        source = lax.rem(me[0] + (block - 5 + count * 5), count)
        for j in range(2):
            for array in range(2):
                at = 4 * array + 2 * j
                here[2 * j + array, 2 * block : 2 * block + 2, :] = gathered[source, at : at + 2, :]
    u_flat, r_flat = level_1.at[0:192], level_1.at[192:360]
    u, g = Slabs(u_flat, 8, 2), Slabs(r_flat, 8, 2)
    for x in range(6):
        u[3 + x] = u1[x]
    for x in range(8):
        g[1 + x] = rhs[x]
    for source, column, edge in ((lax.rem(me[0] + count - 1, count), 0, 0), (lax.rem(me[0] + 1, count), 9, 9)):
        for r in range(2):
            for x in range(3):
                at = 8 + 4 * (2 * x + r)
                to = 8 * (2 * (column + x) + r) + 2
                u_flat[to : to + 4, :] = gathered[source, at : at + 4, :]
            to = 8 * (2 * edge + r) + 2
            r_flat[to : to + 4, :] = gathered[source, 32 + 4 * r : 36 + 4 * r, :]
    for out, row, rhs_row in ((to_high, 4, 5), (to_low, 2, 2)):
        for slab in range(4):
            out[20 * slab : 20 * slab + 20] = here[slab, 1:21]
        for i in range(2):
            out[80 + 20 * i : 100 + 20 * i] = level_1[pl.ds(16 + row + i, 20, 8), :]
        out[120:136] = level_1[pl.ds(192 + 16 + rhs_row, 16, 8), :]


SPREAD = (16, 14, 12, 10, 8, 6)


def spread(j, upward):
    d = j if upward else 5 - j
    return 3 + d, SPREAD[d], 2 * sum(SPREAD[:d])


def three_kernel(me, here, low, high, to_first, to_second):
    blocks = (low, here, high)
    even = lax.rem(me[0], 2) == 0
    for take, to_high, to_low in ((even, to_second, to_first), (jnp.logical_not(even), to_first, to_second)):
        @pl.when(take)
        def _(to_high=to_high, to_low=to_low):
            for j in range(6):
                source = blocks[j // 2]
                for out, upward in ((to_high, False), (to_low, True)):
                    start, size, at = spread(j, upward)
                    for array in range(2):
                        slab = 2 * (j % 2) + array
                        if source is here:
                            values = here[slab, start : start + size]
                        else:
                            values = source[20 * slab + start - 1 : 20 * slab + start - 1 + size]
                        out[at + size * array : at + size * array + size] = values


def window(reach):
    return (7, 8) if reach <= 3 else (3, 16) if reach <= 7 else (1, 24)


def coarse_kernel(me, first, here, second, left, right, level_1, fx, fy, fz, w, v_flat_out, to_high, to_low,
                  u, other, c, start, weights, v_flat, r_flat, va):
    half = 0.5 * 0.0625
    even = lax.rem(me[0], 2) == 0
    for take, below, above in ((even, first, second), (jnp.logical_not(even), second, first)):
        @pl.when(take)
        def _(below=below, above=above):
            for j in range(6):
                for source, upward, y in ((below, False, j), (above, True, 12 + j)):
                    column, size, at = spread(j, upward)
                    start[y, column : column + size] = source[at : at + size]
                    c[y, column : column + size] = source[at + size : at + 2 * size]
    for j in range(6):
        block, slab = (left, here, right)[j // 2], 2 * (j % 2)
        if block is here:
            start[6 + j, 0:24] = here[slab, 0:24]
            c[6 + j, 0:24] = here[slab + 1, 0:24]
        else:
            start[6 + j, 1:21] = block[20 * slab : 20 * slab + 20]
            c[6 + j, 1:21] = block[20 * slab + 20 : 20 * slab + 40]

    def reach(y, step):
        return 9 - step - max(0, 7 - y, y - 10)

    def at(ref, y, lo, size):
        return ref[y, lo : lo + size]

    for y in range(1, 17):
        lo, size = window(reach(y, 1))
        k = at(c, y, lo, size)
        face_z = half * (k + pltpu.roll(k, LANES - 1, 1))
        faces = [half * (k + at(c, y, lo + 1, size)), half * (k + at(c, y, lo - 1, size))]
        faces += [half * (k + at(c, y + 1, lo, size)), half * (k + at(c, y - 1, lo, size))]
        faces += [face_z, pltpu.roll(face_z, 1, 1)]
        scale = DAMPING / (ABSORPTION + ((faces[0] + faces[1]) + (faces[2] + faces[3]) + (faces[4] + faces[5])))
        for i, face in enumerate(faces):
            weights[i, y, lo : lo + size] = scale * face
    old = start
    for step in range(1, 8):
        new = (u, other)[step % 2]
        for y in range(step, 18 - step):
            lo, size = window(reach(y, step))
            now = at(old, y, lo, size)
            along_x = at(weights.at[0], y, lo, size) * at(old, y, lo + 1, size) + at(weights.at[1], y, lo, size) * at(old, y, lo - 1, size)
            along_y = at(weights.at[2], y, lo, size) * at(old, y + 1, lo, size) + at(weights.at[3], y, lo, size) * at(old, y - 1, lo, size)
            along_z = (
                at(weights.at[4], y, lo, size) * pltpu.roll(now, LANES - 1, 1)
                + at(weights.at[5], y, lo, size) * pltpu.roll(now, 1, 1)
            )
            new[y, lo : lo + size] = ((1.0 - DAMPING) * now + at(start, y, lo, size)) + along_y + (along_x + along_z)
        old = new
    u = old
    v_flat[0:192] = level_1[0:192]
    r_flat[0:160] = level_1[192:352]
    for source, row, rhs_row in ((left, 0, 1), (right, 6, 6)):
        for i in range(2):
            v_flat[pl.ds(16 + row + i, 20, 8), :] = source[80 + 20 * i : 100 + 20 * i]
        r_flat[pl.ds(16 + rhs_row, 16, 8), :] = source[120:136]
    v, rhs = Slabs(v_flat, 8, 2), Slabs(r_flat, 8, 2)
    for x in range(6):
        rows = jnp.concatenate(
            [jnp.broadcast_to(u[7 + j, 8 + x : 9 + x, :], (2, LANES)) for j in range(4)], axis=0
        )
        for twin in range(2):
            v[2 * x + twin] = v[2 * x + twin] + rows[None]
    sweep_pass(10, v, 0, 0, rhs, 0, fx, fy, fz, w, va, 0)
    sweep_pass(8, va, 0, 1, rhs, 1, fx, fy, fz, w, Slabs(v_flat_out, 8, 2), 0)
    for out, row in ((to_high, 4), (to_low, 2)):
        for i in range(2):
            out[16 * i : 16 * i + 16] = v_flat_out[pl.ds(row + i, 16, 8), :]


def last_kernel(v_here, v_low, v_high, u0, g, fx, fy, fz, w, matrix, correction, residual, v_flat, wide, ua, ub, res, held, left):
    v_flat[...] = v_here[...]
    for source, row in ((v_low, 0), (v_high, 6)):
        for i in range(2):
            v_flat[pl.ds(row + i, 16, 8), :] = source[16 * i : 16 * i + 16]
    for x in range(8):
        for r in range(2):
            rows = v_flat[8 * (2 * x + r) : 8 * (2 * x + r) + 8]
            wide[x, r, pl.ds(0, 8, 2), :] = rows
            wide[x, r, pl.ds(1, 8, 2), :] = rows
    for i in range(14):
        fine = wide[(i + 1) // 2]
        ua[i] = u0[i] + jnp.stack([fine[0], fine[0], fine[1], fine[1]])
    sweep_pass(12, ua, 0, 0, g, 0, fx, fy, fz, w, ub, 0)
    sweep_pass(10, ub, 0, 1, g, 1, fx, fy, fz, w, ua, 0)
    copies = []

    def leave(index, source, at, out, start, size):
        rows = [
            jnp.concatenate([source[at + x, r, 4:12, :] for r in range(4)], axis=1) for x in range(start, start + size)
        ]
        held[index, start : start + size] = rearrange(jnp.concatenate(rows, axis=0), matrix[...]).reshape(size, 8, 512)
        part = pl.ds(start, size)
        copy = pltpu.make_async_copy(held.at[index, part], out.at[part], left.at[len(copies)])
        copy.start()
        copies.append(copy)

    leave(0, ua, 1, correction, 0, 8)
    sweep_pass(4, ua, 0, 2, g, 2, fx, fy, fz, w, res, 0, last=True)
    leave(1, res, 0, residual, 0, 4)
    sweep_pass(4, ua, 4, 6, g, 6, fx, fy, fz, w, res, 4, last=True)
    leave(1, res, 0, residual, 4, 4)
    for copy in copies:
        copy.wait()


VMEM = pl.BlockSpec(memory_space=pltpu.VMEM)
SMEM = pl.BlockSpec(memory_space=pltpu.SMEM)
HBM = pl.BlockSpec(memory_space=pltpu.HBM)


def call(kernel, outs, scratch, *arrays, scalars=0, to_hbm=False, extra=()):
    return pl.pallas_call(
        kernel,
        out_shape=[jax.ShapeDtypeStruct(shape, F32) for shape in outs],
        in_specs=[SMEM] * scalars + [VMEM] * (len(arrays) - scalars),
        out_specs=[HBM if to_hbm else VMEM] * len(outs),
        scratch_shapes=[pltpu.VMEM(shape, F32) for shape in scratch] + list(extra),
        compiler_params=pltpu.CompilerParams(vmem_limit_bytes=32 * 2**20),
    )(*arrays)


def shift(array, axis, by):
    count = lax.axis_size(axis)
    return lax.ppermute(array, axis, [(i, (i + by) % count) for i in range(count)])


def swap(array, axis, start, by=1):
    count = lax.axis_size(axis)
    pairs = [(i, (i + by) % count) for i in range(start, count, 2)]
    return lax.ppermute(array, axis, pairs + [(j, i) for i, j in pairs])


def per_device(right_side, coefficient):
    me_x = lax.axis_index("gx").astype(jnp.int32).reshape(1)
    me_y = lax.axis_index("gy").astype(jnp.int32).reshape(1)
    count = lax.axis_size("gx")
    border = (G_BORDER + K_BORDER, 4, 8, 128)
    own, first, second = call(
        permute_kernel, [(512, 128), border, border], [], me_x, jnp.stack([right_side, coefficient]), scalars=1
    )
    first, second = swap(first, "gx", 1), swap(second, "gx", 0)
    high, low = call(face_kernel, [(FACE_ROWS, 128), (FACE_ROWS, 128)], [], own)
    low, high = shift(high, "gy", 1), shift(low, "gy", -1)
    wide, high_corners, low_corners = call(
        wide_kernel, [((G_SLABS + K_SLABS) * 32, 128), (CORNER_ROWS, 128), (CORNER_ROWS, 128)], [],
        me_x, own, first, second, scalars=1,
    )
    low_corners, high_corners = shift(high_corners, "gy", 1), shift(low_corners, "gy", -1)
    fine, mid, last = (4, 24, 128), (2, 8, 128), (4, 16, 128)
    early = call(
        early_kernel,
        [(8 * 96, 128), (8 * 96, 128), (7, *fine), (6, *fine), (6, *fine), (6, *fine), (6, *fine), (4, *fine), (2, *fine)],
        [], own, low, high,
    )
    g_early, k_early, u0_early = early[0], early[1], early[7]
    piece, u0, g, k, u1, rhs = call(
        fine_kernel,
        [(count, 40, 128), (10, *fine), (12 * 96, 128), (16 * 96, 128), (6, *mid), (8, *mid)],
        [(4, *fine), (14, *fine), (14, *fine), (14, *fine), (14, *fine), (14, *fine), (14, *fine), (8, 2, 24, 128), (10, 2, 24, 128),
         (9, *mid), (8, *mid), (8, *mid), (8, *mid), (8, *mid), (4, *mid), (4, 16, 128), (2, 40, 128)],
        me_x, wide, low_corners, high_corners, *early, scalars=1,
    )
    piece, u0, g, k, u1, rhs = lax.optimization_barrier((piece, u0, g, k, u1, rhs))
    gathered = lax.all_to_all(piece, "gx", 0, 0)
    gathered, u0, g, k, u1, rhs = lax.optimization_barrier((gathered, u0, g, k, u1, rhs))
    here, high, low, level_1 = call(
        middle_kernel, [(4, 32, 128), (EDGE_ROWS, 128), (EDGE_ROWS, 128), (360, 128)], [], me_x, gathered, u1, rhs, scalars=1
    )
    low, high = shift(high, "gy", 1), shift(low, "gy", -1)
    first, second = call(three_kernel, [(136, 128), (136, 128)], [], me_y, here, low, high, scalars=1)
    first, second = swap(first, "gy", 1, 3), swap(second, "gy", 0, 3)
    faces = call(
        prepare_middle_kernel, [(11, *mid), (10, *mid), (10, *mid), (10, *mid)], [(12, *mid), (2, 24, 128)], k_early, k
    )
    rows = (18, 32, 128)
    v1, high_rows, low_rows = call(
        coarse_kernel, [(128, 128), (32, 128), (32, 128)],
        [rows, rows, rows, rows, (6, *rows), (216, 128), (168, 128), (10, *mid)],
        me_y, first, here, second, low, high, level_1, *faces, scalars=1,
    )
    u0, g, *faces = call(
        prepare_kernel, [(14, *last), (12, *last), (13, *last), (12, *last), (12, *last), (12, *last)], [(14, *last)],
        u0_early, u0, g_early, g, k_early, k,
    )
    low, high = shift(high_rows, "gy", 1), shift(low_rows, "gy", -1)
    return tuple(call(
        last_kernel, [(8, 8, 512), (8, 8, 512)],
        [(128, 128), (8, 2, 16, 128), (14, *last), (12, *last), (8, *last), (2, 8, 8, 512)],
        v1, low, high, u0, g, *faces, inverse_permutation(), to_hbm=True, extra=[pltpu.SemaphoreType.DMA((3,))],
    ))


def solution(mesh):
    placed = (P("gx", "gy", None), P("gx", "gy", None))
    return jax.shard_map(per_device, mesh=mesh, in_specs=placed, out_specs=placed, check_vma=False)
```

```python
import jax
import jax.numpy as jnp
import ml_dtypes
import numpy as np
from jax import lax
from jax.experimental import pallas as pl
from jax.experimental.pallas import tpu as pltpu
from jax.sharding import PartitionSpec as P

ABSORPTION = 0.05
DAMPING = 0.8
F32 = jnp.float32
LANES = 128


def z_next(v):
    first = pltpu.roll(v[0], LANES - 1, 1)[None]
    return first if v.shape[0] == 1 else jnp.concatenate([v[1:], first], axis=0)


def z_prev(v):
    last = pltpu.roll(v[-1], 1, 1)[None]
    return last if v.shape[0] == 1 else jnp.concatenate([last, v[:-1]], axis=0)


def y_next(v):
    return pltpu.roll(v, v.shape[1] - 1, 1)


def y_prev(v):
    return pltpu.roll(v, 1, 1)


def flux_sum(u, u_next, flux_low, fx, fy, fz):
    flux_high = fx * (u - u_next)
    flux_y = fy * (u - y_next(u))
    flux_z = fz * (u - z_next(u))
    total = (flux_high - flux_low) + (flux_y - y_prev(flux_y)) + (flux_z - z_prev(flux_z))
    return ABSORPTION * u + total, flux_high


class Slabs:
    def __init__(self, flat, rows, parts=4):
        self.flat, self.rows, self.parts = flat, rows, parts

    def at(self, i):
        size = self.parts * self.rows
        return pl.ds(i * size, size)

    def __getitem__(self, i):
        return self.flat[self.at(i), :].reshape(self.parts, self.rows, LANES)

    def __setitem__(self, i, value):
        self.flat[self.at(i), :] = value.reshape(self.parts * self.rows, LANES)

    def part(self, i, start, size, step=1):
        where = lambda r: pl.ds((self.parts * i + r) * self.rows + start, size, step)
        return jnp.stack([self.flat[where(r), :] for r in range(self.parts)])

    def put(self, i, start, value):
        for r in range(self.parts):
            self.flat[pl.ds((self.parts * i + r) * self.rows + start, value.shape[1]), :] = value[r]


class Parted:
    def __init__(self, inner, outer, start, stop):
        self.inner, self.outer, self.start, self.stop = inner, outer, start, stop

    def place(self, i):
        if self.start <= i < self.stop:
            return self.inner, i - self.start
        return self.outer, i if i < self.start else i - (self.stop - self.start)

    def __getitem__(self, i):
        buffer, at = self.place(i)
        return buffer[at]

    def __setitem__(self, i, value):
        buffer, at = self.place(i)
        buffer[at] = value

    def part(self, i, start, size):
        buffer, at = self.place(i)
        if isinstance(buffer, (Parted, Slabs)):
            return buffer.part(at, start, size)
        return buffer[at, :, start : start + size, :]


def get(ref, i, rows):
    if rows is None:
        return ref[i]
    return ref.part(i, *rows) if hasattr(ref, "part") else ref[i, :, rows[0] : rows[0] + rows[1], :]


def put(ref, i, rows, value):
    if isinstance(ref, Parted):
        put(*ref.place(i), rows, value)
    elif rows is None:
        ref[i] = value
    else:
        ref[i, :, rows[0] : rows[0] + rows[1], :] = value


def every_row(i):
    return None


def face_pass(count, k_ref, fx, fy, fz, w, scale, k_at=0, done=(), rows=every_row):
    half = 0.5 * scale
    for i in range(count + 1):
        if i not in done or i - 1 not in done:
            fx[i] = half * (k_ref[k_at + i] + k_ref[k_at + 1 + i])
        if i == 0 or i - 1 in done:
            continue
        some = rows(i - 1)
        k = get(k_ref, k_at + i, some)
        face_y = half * (k + y_next(k))
        face_z = half * (k + z_next(k))
        diag = ABSORPTION + (get(fx, i, some) + get(fx, i - 1, some) + face_y + y_prev(face_y) + face_z + z_prev(face_z))
        put(fy, i - 1, some, face_y)
        put(fz, i - 1, some, face_z)
        put(w, i - 1, some, DAMPING / diag)


def sweep_pass(count, u_ref, u_at, faces_at, g_ref, g_at, fx, fy, fz, w, out, out_at, last=False, done=(), rows=every_row):
    low, low_rows = None, None
    for i in range(count):
        if i in done:
            low = None
            continue
        some, f = rows(i), faces_at + i
        u, u_next = get(u_ref, u_at + 1 + i, some), get(u_ref, u_at + 2 + i, some)
        if low is None or low_rows != some:
            low = get(fx, f, some) * (get(u_ref, u_at + i, some) - u)
        applied, low = flux_sum(u, u_next, low, get(fx, f + 1, some), get(fy, f, some), get(fz, f, some))
        low_rows = some
        rest = get(g_ref, g_at + i, some) - applied
        put(out, out_at + i, some, rest if last else u + get(w, f, some) * rest)


def neighbour_sweep(count, u_ref, g_ref, at, fx, fy, fz, w, out):
    for i in range(count):
        f, u = at + i, u_ref[1 + i]
        face_y, face_z = fy[f], fz[f]
        along_x = fx[f + 1] * u_ref[2 + i] + fx[f] * u_ref[i]
        along_y = face_y * y_next(u) + y_prev(face_y) * y_prev(u)
        along_z = face_z * z_next(u) + z_prev(face_z) * z_prev(u)
        out[i] = (1.0 - DAMPING) * u + w[f] * ((g_ref[f] + along_x) + (along_y + along_z))


def inverse_permutation():
    z, at = np.arange(512)[None, :], np.arange(512)[:, None]
    return jnp.asarray((z == 4 * (at % LANES) + at // LANES).astype(ml_dtypes.bfloat16))


def permutation(inverse):
    z = lax.broadcasted_iota(jnp.int32, (512, 512), 1 if inverse else 0)
    at = lax.broadcasted_iota(jnp.int32, (512, 512), 0 if inverse else 1)
    return jnp.where(z == 4 * (at % LANES) + at // LANES, 1.0, 0.0).astype(jnp.bfloat16)


def rearrange(rows, matrix):
    count = rows.shape[0]
    top = rows.astype(jnp.bfloat16)
    rest = rows - top.astype(F32)
    middle = rest.astype(jnp.bfloat16)
    bottom = (rest - middle.astype(F32)).astype(jnp.bfloat16)
    parts = jnp.concatenate([top, middle, bottom], axis=0)
    moved = lax.dot_general(parts, matrix, (((1,), (0,)), ((), ())), preferred_element_type=F32)
    return (moved[0:count] + moved[count : 2 * count]) + moved[2 * count :]


def permute_kernel(me, held, own_flat, to_first, to_second):
    matrix = permutation(False)
    moved = rearrange(held[...].reshape(128, 512), matrix)
    for x in range(16):
        for r in range(4):
            own_flat[32 * x + 8 * r : 32 * x + 8 * r + 8] = moved[8 * x : 8 * x + 8, LANES * r : LANES * r + LANES]
    own = Slabs(own_flat, 8)
    even = lax.rem(me[0], 2) == 0
    for take, high, low in ((even, to_second, to_first), (jnp.logical_not(even), to_first, to_second)):
        @pl.when(take)
        def _(high=high, low=low):
            for i in range(6):
                high[i] = own[2 + i]
                low[i] = own[i]
            for i in range(6, 14):
                high[i] = own[2 + i]
                low[i] = own[2 + i]


G_BORDER, K_BORDER = 6, 8
G_SLABS, K_SLABS = 8 + 2 * G_BORDER, 8 + 2 * K_BORDER
G_REACH = (5, 4, 3, 2, 1, 0)
K_REACH = (6, 6, 4, 4, 2, 1, 0)


def row_parts():
    for array, reaches, border in ((0, G_REACH, G_BORDER), (1, K_REACH, K_BORDER)):
        for d, reach in enumerate(reaches, 1):
            yield array, d, reach, border


FACE_ROWS = 32 * (len(G_REACH) + len(K_REACH))
CORNER_ROWS = 8 * (sum(G_REACH) + sum(K_REACH)) + 8


def face_kernel(own, to_high, to_low):
    for i, (array, d, _, _) in enumerate(row_parts()):
        for out, y in ((to_high, 8 - d), (to_low, d - 1)):
            out[32 * i : 32 * i + 32] = own[pl.ds(256 * array + y, 32, 8), :]


def corners():
    at = 0
    for array, d, reach, border in row_parts():
        for column in (border - reach, border + 8):
            if reach:
                yield array, d, column, 4 * reach, at
                at += 4 * reach


def wide_kernel(me, own, first, second, flat, to_high, to_low):
    out, own = Slabs(flat, 8), Slabs(own, 8)

    def put(at, source, start, size):
        for i in range(size):
            out[at + i] = source[start + i]

    put(6, own, 0, 8)
    put(28, own, 8, 8)
    even = lax.rem(me[0], 2) == 0
    for take, left, right in ((even, first, second), (jnp.logical_not(even), second, first)):
        @pl.when(take)
        def _(left=left, right=right):
            put(0, left, 0, 6)
            put(14, right, 0, 6)
            put(20, left, 6, 8)
            put(36, right, 6, 8)
    for array, d, column, size, at in corners():
        base = (G_SLABS * array + column) * 32
        to_high[at : at + size] = flat[pl.ds(base + 8 - d, size, 8), :]
        to_low[at : at + size] = flat[pl.ds(base + d - 1, size, 8), :]


def early_kernel(own, low, high, g_flat, k_flat, fx, fy, fz, w, uf, u0, res):
    own, flats = Slabs(own, 8), (g_flat, k_flat)
    g, k = Slabs(g_flat, 24), Slabs(k_flat, 24)
    for i in range(8):
        g.put(i, 8, own[i])
        k.put(i, 8, own[8 + i])
    for i, (array, d, _, _) in enumerate(row_parts()):
        flats[array][pl.ds(8 - d, 32, 24), :] = low[32 * i : 32 * i + 32]
        flats[array][pl.ds(15 + d, 32, 24), :] = high[32 * i : 32 * i + 32]
    face_pass(6, k, fx, fy, fz, w, 1.0)
    for i in range(6):
        uf[i] = w[i] * g[1 + i]
    sweep_pass(4, uf, 0, 1, g, 2, fx, fy, fz, w, u0, 0)
    sweep_pass(2, u0, 0, 2, g, 3, fx, fy, fz, w, res, 0, last=True)


def fine_kernel(me, wide, low_corners, high_corners, g_early, k_early, fx_early, fy_early, fz_early, w_early, uf_early,
                u0_early, res_early, piece, u0_kept, g_flat, k_flat, u1, rhs, u0_edge, fx, fy, fz, w, uf, res, s1, sc,
                mx, my, mz, mw, mf, mr, ck, near):
    flats = g_flat, k_flat
    wide, g, k = Slabs(wide, 8), Slabs(g_flat, 24), Slabs(k_flat, 24)
    for i in range(12):
        g.put(i, 8, wide[i if i < 6 else i + 8])
    for i in range(16):
        k.put(i, 8, wide[G_SLABS + (i if i < 8 else i + 8)])
    for array, d, column, size, at in corners():
        slab = column if column < (G_BORDER, K_BORDER)[array] else column - 8
        flats[array][pl.ds(slab * 96 + 8 - d, size, 24), :] = low_corners[at : at + size]
        flats[array][pl.ds(slab * 96 + 15 + d, size, 24), :] = high_corners[at : at + size]
    g, k = Parted(Slabs(g_early, 24), g, 6, 14), Parted(Slabs(k_early, 24), k, 8, 16)
    fx = Parted(fx_early, fx, 7, 14)
    fy, fz, w, uf = [Parted(*pair, 7, 13) for pair in ((fy_early, fy), (fz_early, fz), (w_early, w), (uf_early, uf))]
    u0 = Parted(Parted(u0_early, u0_kept, 5, 9), u0_edge, 2, 16)
    res = Parted(res_early, res, 7, 9)
    def beside(first_x, border):
        return lambda i: (4, 16) if first_x + i <= -border or first_x + i >= 7 + border else None

    face_pass(20, k, fx, fy, fz, w, 1.0, k_at=1, done=range(7, 13), rows=beside(-6, 3))
    for i in range(20):
        if not 7 <= i < 13:
            some = beside(-6, 3)(i)
            put(uf, i, some, get(w, i, some) * get(g, i, some))
    sweep_pass(18, uf, 0, 1, g, 1, fx, fy, fz, w, u0, 0, done=range(7, 11), rows=beside(-5, 2))
    sweep_pass(16, u0, 0, 2, g, 2, fx, fy, fz, w, res, 0, last=True, done=range(7, 9), rows=beside(-4, 1))
    for x in range(8):
        both = res[2 * x] + res[2 * x + 1]
        s1[x, 0] = both[0] + both[1]
        s1[x, 1] = both[2] + both[3]
    for x in range(10):
        both = k[2 + 2 * x] + k[3 + 2 * x]
        sc[x, 0] = both[0] + both[1]
        sc[x, 1] = both[2] + both[3]

    def rows(ref, x, start):
        return jnp.stack(
            [ref[x, r, pl.ds(start, 8, 2), :] + ref[x, r, pl.ds(start + 1, 8, 2), :] for r in range(2)]
        ) * 0.125

    half = 0.5 * 0.25
    k_mid = [rows(sc, x, 4) for x in range(10)]
    mx[0] = half * (k_mid[0] + k_mid[1])
    for x in range(8):
        here = k_mid[x + 1]
        face_x = half * (here + k_mid[x + 2])
        face_y = half * (here + rows(sc, x + 1, 6))
        face_z = half * (here + z_next(here))
        diag = ABSORPTION + (
            mx[x] + face_x + face_y + half * (here + rows(sc, x + 1, 2)) + face_z + z_prev(face_z)
        )
        mx[x + 1], my[x], mz[x] = face_x, face_y, face_z
        mw[x] = DAMPING / diag
        rhs[x] = rows(s1, x, 4)
        mf[x] = mw[x] * rhs[x]
    sweep_pass(6, mf, 0, 1, rhs, 1, mx, my, mz, mw, u1, 0)
    sweep_pass(4, u1, 0, 2, rhs, 2, mx, my, mz, mw, mr, 0, last=True)
    for x in range(4):
        both = k_mid[2 * x + 1] + k_mid[2 * x + 2]
        ck[x, 0:8] = both[0] + both[1]
    k2 = [(ck[x, pl.ds(0, 4, 2), :] + ck[x, pl.ds(1, 4, 2), :]) * 0.125 for x in range(4)]
    half = 0.5 * 0.0625
    for x in range(2):
        here = k2[x + 1][1:3]
        face_z = half * (here + pltpu.roll(here, LANES - 1, 1))
        diag = ABSORPTION + (
            half * (here + k2[x][1:3]) + half * (here + k2[x + 2][1:3])
            + half * (here + k2[x + 1][0:2]) + half * (here + k2[x + 1][2:4])
            + face_z + pltpu.roll(face_z, 1, 1)
        )
        both = mr[2 * x] + mr[2 * x + 1]
        ck[x, 0:8] = both[0] + both[1]
        first_sweep = DAMPING / diag * ((ck[x, pl.ds(2, 2, 2), :] + ck[x, pl.ds(3, 2, 2), :]) * 0.125)
        for j in range(2):
            ck[3, 2 * j + x : 2 * j + x + 1, :] = first_sweep[j : j + 1]
            ck[3, 4 + 2 * j + x : 5 + 2 * j + x, :] = here[j : j + 1]
    level_2 = ck[3, 0:8]
    for to in range(piece.shape[0]):
        piece[to, 0:8, :] = level_2
    count = piece.shape[0]
    for to, column in ((lax.rem(me[0] + 1, count), 0), (lax.rem(me[0] + count - 1, count), 1)):
        for r in range(2):
            for x in range(3):
                at = 4 * (2 * x + r)
                near[column, at : at + 4, :] = u1[column + x + 1, r, 2:6, :]
            near[column, 24 + 4 * r : 28 + 4 * r, :] = rhs[column + 3, r, 2:6, :]
        piece[to, 8:40, :] = near[column, 0:32, :]


def prepare_middle_kernel(k_early, k_flat, fx, fy, fz, w, k_mid, sums):
    k = Parted(Slabs(k_early, 24), Slabs(k_flat, 24), 8, 16)
    for x in range(12):
        both = k[2 * x] + k[2 * x + 1]
        for r in range(2):
            sums[r] = both[2 * r] + both[2 * r + 1]
            k_mid[x, r] = (sums[r, pl.ds(4, 8, 2), :] + sums[r, pl.ds(5, 8, 2), :]) * 0.125
    face_pass(10, k_mid, fx, fy, fz, w, 0.25)


def prepare_kernel(u0_early, u0, g_early, g_flat, k_early, k_flat, u_out, g_out, fx, fy, fz, w, k_rows):
    g, k = Parted(Slabs(g_early, 24), Slabs(g_flat, 24), 6, 14), Parted(Slabs(k_early, 24), Slabs(k_flat, 24), 8, 16)
    u0 = Parted(u0_early, u0, 5, 9)
    for i in range(14):
        u_out[i] = u0.part(i, 4, 16)
        k_rows[i] = k.part(i + 5, 4, 16)
    for i in range(12):
        g_out[i] = g.part(i + 4, 4, 16)
    face_pass(12, k_rows, fx, fy, fz, w, 1.0)


EDGE_ROWS = 4 * 20 + 2 * 20 + 16


def middle_kernel(me, gathered, u1, rhs, here, to_high, to_low, level_1):
    count = gathered.shape[0]
    for block in range(11):
        source = lax.rem(me[0] + (block - 5 + count * 5), count)
        for j in range(2):
            for array in range(2):
                at = 4 * array + 2 * j
                here[2 * j + array, 2 * block : 2 * block + 2, :] = gathered[source, at : at + 2, :]
    u_flat, r_flat = level_1.at[0:192], level_1.at[192:360]
    u, g = Slabs(u_flat, 8, 2), Slabs(r_flat, 8, 2)
    for x in range(6):
        u[3 + x] = u1[x]
    for x in range(8):
        g[1 + x] = rhs[x]
    for source, column, edge in ((lax.rem(me[0] + count - 1, count), 0, 0), (lax.rem(me[0] + 1, count), 9, 9)):
        for r in range(2):
            for x in range(3):
                at = 8 + 4 * (2 * x + r)
                to = 8 * (2 * (column + x) + r) + 2
                u_flat[to : to + 4, :] = gathered[source, at : at + 4, :]
            to = 8 * (2 * edge + r) + 2
            r_flat[to : to + 4, :] = gathered[source, 32 + 4 * r : 36 + 4 * r, :]
    for out, row, rhs_row in ((to_high, 4, 5), (to_low, 2, 2)):
        for slab in range(4):
            out[20 * slab : 20 * slab + 20] = here[slab, 1:21]
        for i in range(2):
            out[80 + 20 * i : 100 + 20 * i] = level_1[pl.ds(16 + row + i, 20, 8), :]
        out[120:136] = level_1[pl.ds(192 + 16 + rhs_row, 16, 8), :]


SPREAD = (16, 14, 12, 10, 8, 6)


def spread(j, upward):
    d = j if upward else 5 - j
    return 3 + d, SPREAD[d], 2 * sum(SPREAD[:d])


def three_kernel(me, here, low, high, to_first, to_second):
    blocks = (low, here, high)
    even = lax.rem(me[0], 2) == 0
    for take, to_high, to_low in ((even, to_second, to_first), (jnp.logical_not(even), to_first, to_second)):
        @pl.when(take)
        def _(to_high=to_high, to_low=to_low):
            for j in range(6):
                source = blocks[j // 2]
                for out, upward in ((to_high, False), (to_low, True)):
                    start, size, at = spread(j, upward)
                    for array in range(2):
                        slab = 2 * (j % 2) + array
                        if source is here:
                            values = here[slab, start : start + size]
                        else:
                            values = source[20 * slab + start - 1 : 20 * slab + start - 1 + size]
                        out[at + size * array : at + size * array + size] = values


def window(reach):
    return (7, 8) if reach <= 3 else (3, 16) if reach <= 7 else (1, 24)


def coarse_kernel(me, first, here, second, left, right, level_1, fx, fy, fz, w, v_flat_out, to_high, to_low,
                  u, other, c, start, weights, v_flat, r_flat, va):
    half = 0.5 * 0.0625
    even = lax.rem(me[0], 2) == 0
    for take, below, above in ((even, first, second), (jnp.logical_not(even), second, first)):
        @pl.when(take)
        def _(below=below, above=above):
            for j in range(6):
                for source, upward, y in ((below, False, j), (above, True, 12 + j)):
                    column, size, at = spread(j, upward)
                    start[y, column : column + size] = source[at : at + size]
                    c[y, column : column + size] = source[at + size : at + 2 * size]
    for j in range(6):
        block, slab = (left, here, right)[j // 2], 2 * (j % 2)
        if block is here:
            start[6 + j, 0:24] = here[slab, 0:24]
            c[6 + j, 0:24] = here[slab + 1, 0:24]
        else:
            start[6 + j, 1:21] = block[20 * slab : 20 * slab + 20]
            c[6 + j, 1:21] = block[20 * slab + 20 : 20 * slab + 40]

    def reach(y, step):
        return 9 - step - max(0, 7 - y, y - 10)

    def at(ref, y, lo, size):
        return ref[y, lo : lo + size]

    for y in range(1, 17):
        lo, size = window(reach(y, 1))
        k = at(c, y, lo, size)
        face_z = half * (k + pltpu.roll(k, LANES - 1, 1))
        faces = [half * (k + at(c, y, lo + 1, size)), half * (k + at(c, y, lo - 1, size))]
        faces += [half * (k + at(c, y + 1, lo, size)), half * (k + at(c, y - 1, lo, size))]
        faces += [face_z, pltpu.roll(face_z, 1, 1)]
        scale = DAMPING / (ABSORPTION + ((faces[0] + faces[1]) + (faces[2] + faces[3]) + (faces[4] + faces[5])))
        for i, face in enumerate(faces):
            weights[i, y, lo : lo + size] = scale * face
    old = start
    for step in range(1, 8):
        new = (u, other)[step % 2]
        for y in range(step, 18 - step):
            lo, size = window(reach(y, step))
            now = at(old, y, lo, size)
            along_x = at(weights.at[0], y, lo, size) * at(old, y, lo + 1, size) + at(weights.at[1], y, lo, size) * at(old, y, lo - 1, size)
            along_y = at(weights.at[2], y, lo, size) * at(old, y + 1, lo, size) + at(weights.at[3], y, lo, size) * at(old, y - 1, lo, size)
            along_z = (
                at(weights.at[4], y, lo, size) * pltpu.roll(now, LANES - 1, 1)
                + at(weights.at[5], y, lo, size) * pltpu.roll(now, 1, 1)
            )
            new[y, lo : lo + size] = ((1.0 - DAMPING) * now + at(start, y, lo, size)) + along_y + (along_x + along_z)
        old = new
    u = old
    v_flat[0:192] = level_1[0:192]
    r_flat[0:160] = level_1[192:352]
    for source, row, rhs_row in ((left, 0, 1), (right, 6, 6)):
        for i in range(2):
            v_flat[pl.ds(16 + row + i, 20, 8), :] = source[80 + 20 * i : 100 + 20 * i]
        r_flat[pl.ds(16 + rhs_row, 16, 8), :] = source[120:136]
    v, rhs = Slabs(v_flat, 8, 2), Slabs(r_flat, 8, 2)
    for x in range(6):
        rows = jnp.concatenate(
            [jnp.broadcast_to(u[7 + j, 8 + x : 9 + x, :], (2, LANES)) for j in range(4)], axis=0
        )
        for twin in range(2):
            v[2 * x + twin] = v[2 * x + twin] + rows[None]
    neighbour_sweep(10, v, rhs, 0, fx, fy, fz, w, va)
    neighbour_sweep(8, va, rhs, 1, fx, fy, fz, w, Slabs(v_flat_out, 8, 2))
    for out, row in ((to_high, 4), (to_low, 2)):
        for i in range(2):
            out[16 * i : 16 * i + 16] = v_flat_out[pl.ds(row + i, 16, 8), :]


def last_kernel(v_here, v_low, v_high, u0, g, fx, fy, fz, w, matrix, correction, residual, v_flat, wide, ua, ub, res, held, left):
    v_flat[...] = v_here[...]
    for source, row in ((v_low, 0), (v_high, 6)):
        for i in range(2):
            v_flat[pl.ds(row + i, 16, 8), :] = source[16 * i : 16 * i + 16]
    for x in range(8):
        for r in range(2):
            rows = v_flat[8 * (2 * x + r) : 8 * (2 * x + r) + 8]
            wide[x, r, pl.ds(0, 8, 2), :] = rows
            wide[x, r, pl.ds(1, 8, 2), :] = rows
    for i in range(14):
        fine = wide[(i + 1) // 2]
        ua[i] = u0[i] + jnp.stack([fine[0], fine[0], fine[1], fine[1]])
    sweep_pass(12, ua, 0, 0, g, 0, fx, fy, fz, w, ub, 0)
    sweep_pass(10, ub, 0, 1, g, 1, fx, fy, fz, w, ua, 0)
    copies = []

    def leave(index, source, at, out, start, size):
        rows = [
            jnp.concatenate([source[at + x, r, 4:12, :] for r in range(4)], axis=1) for x in range(start, start + size)
        ]
        held[index, start : start + size] = rearrange(jnp.concatenate(rows, axis=0), matrix[...]).reshape(size, 8, 512)
        part = pl.ds(start, size)
        copy = pltpu.make_async_copy(held.at[index, part], out.at[part], left.at[len(copies)])
        copy.start()
        copies.append(copy)

    leave(0, ua, 1, correction, 0, 8)
    sweep_pass(4, ua, 0, 2, g, 2, fx, fy, fz, w, res, 0, last=True)
    leave(1, res, 0, residual, 0, 4)
    sweep_pass(4, ua, 4, 6, g, 6, fx, fy, fz, w, res, 4, last=True)
    leave(1, res, 0, residual, 4, 4)
    for copy in copies:
        copy.wait()


VMEM = pl.BlockSpec(memory_space=pltpu.VMEM)
SMEM = pl.BlockSpec(memory_space=pltpu.SMEM)
HBM = pl.BlockSpec(memory_space=pltpu.HBM)


def call(kernel, outs, scratch, *arrays, scalars=0, to_hbm=False, extra=()):
    return pl.pallas_call(
        kernel,
        out_shape=[jax.ShapeDtypeStruct(shape, F32) for shape in outs],
        in_specs=[SMEM] * scalars + [VMEM] * (len(arrays) - scalars),
        out_specs=[HBM if to_hbm else VMEM] * len(outs),
        scratch_shapes=[pltpu.VMEM(shape, F32) for shape in scratch] + list(extra),
        compiler_params=pltpu.CompilerParams(vmem_limit_bytes=32 * 2**20),
    )(*arrays)


def shift(array, axis, by):
    count = lax.axis_size(axis)
    return lax.ppermute(array, axis, [(i, (i + by) % count) for i in range(count)])


def swap(array, axis, start, by=1):
    count = lax.axis_size(axis)
    pairs = [(i, (i + by) % count) for i in range(start, count, 2)]
    return lax.ppermute(array, axis, pairs + [(j, i) for i, j in pairs])


def per_device(right_side, coefficient):
    me_x = lax.axis_index("gx").astype(jnp.int32).reshape(1)
    me_y = lax.axis_index("gy").astype(jnp.int32).reshape(1)
    count = lax.axis_size("gx")
    border = (G_BORDER + K_BORDER, 4, 8, 128)
    own, first, second = call(
        permute_kernel, [(512, 128), border, border], [], me_x, jnp.stack([right_side, coefficient]), scalars=1
    )
    first, second = swap(first, "gx", 1), swap(second, "gx", 0)
    high, low = call(face_kernel, [(FACE_ROWS, 128), (FACE_ROWS, 128)], [], own)
    low, high = shift(high, "gy", 1), shift(low, "gy", -1)
    wide, high_corners, low_corners = call(
        wide_kernel, [((G_SLABS + K_SLABS) * 32, 128), (CORNER_ROWS, 128), (CORNER_ROWS, 128)], [],
        me_x, own, first, second, scalars=1,
    )
    low_corners, high_corners = shift(high_corners, "gy", 1), shift(low_corners, "gy", -1)
    fine, mid, last = (4, 24, 128), (2, 8, 128), (4, 16, 128)
    early = call(
        early_kernel,
        [(8 * 96, 128), (8 * 96, 128), (7, *fine), (6, *fine), (6, *fine), (6, *fine), (6, *fine), (4, *fine), (2, *fine)],
        [], own, low, high,
    )
    g_early, k_early, u0_early = early[0], early[1], early[7]
    piece, u0, g, k, u1, rhs = call(
        fine_kernel,
        [(count, 40, 128), (10, *fine), (12 * 96, 128), (16 * 96, 128), (6, *mid), (8, *mid)],
        [(4, *fine), (14, *fine), (14, *fine), (14, *fine), (14, *fine), (14, *fine), (14, *fine), (8, 2, 24, 128), (10, 2, 24, 128),
         (9, *mid), (8, *mid), (8, *mid), (8, *mid), (8, *mid), (4, *mid), (4, 16, 128), (2, 40, 128)],
        me_x, wide, low_corners, high_corners, *early, scalars=1,
    )
    piece, u0, g, k, u1, rhs = lax.optimization_barrier((piece, u0, g, k, u1, rhs))
    gathered = lax.all_to_all(piece, "gx", 0, 0)
    gathered, u0, g, k, u1, rhs = lax.optimization_barrier((gathered, u0, g, k, u1, rhs))
    here, high, low, level_1 = call(
        middle_kernel, [(4, 32, 128), (EDGE_ROWS, 128), (EDGE_ROWS, 128), (360, 128)], [], me_x, gathered, u1, rhs, scalars=1
    )
    low, high = shift(high, "gy", 1), shift(low, "gy", -1)
    first, second = call(three_kernel, [(136, 128), (136, 128)], [], me_y, here, low, high, scalars=1)
    first, second = swap(first, "gy", 1, 3), swap(second, "gy", 0, 3)
    faces = call(
        prepare_middle_kernel, [(11, *mid), (10, *mid), (10, *mid), (10, *mid)], [(12, *mid), (2, 24, 128)], k_early, k
    )
    rows = (18, 32, 128)
    v1, high_rows, low_rows = call(
        coarse_kernel, [(128, 128), (32, 128), (32, 128)],
        [rows, rows, rows, rows, (6, *rows), (216, 128), (168, 128), (10, *mid)],
        me_y, first, here, second, low, high, level_1, *faces, scalars=1,
    )
    u0, g, *faces = call(
        prepare_kernel, [(14, *last), (12, *last), (13, *last), (12, *last), (12, *last), (12, *last)], [(14, *last)],
        u0_early, u0, g_early, g, k_early, k,
    )
    low, high = shift(high_rows, "gy", 1), shift(low_rows, "gy", -1)
    return tuple(call(
        last_kernel, [(8, 8, 512), (8, 8, 512)],
        [(128, 128), (8, 2, 16, 128), (14, *last), (12, *last), (8, *last), (2, 8, 8, 512)],
        v1, low, high, u0, g, *faces, inverse_permutation(), to_hbm=True, extra=[pltpu.SemaphoreType.DMA((3,))],
    ))


def solution(mesh):
    placed = (P("gx", "gy", None), P("gx", "gy", None))
    return jax.shard_map(per_device, mesh=mesh, in_specs=placed, out_specs=placed, check_vma=False)
```

```python
import jax
import jax.numpy as jnp
import ml_dtypes
import numpy as np
from jax import lax
from jax.experimental import pallas as pl
from jax.experimental.pallas import tpu as pltpu
from jax.sharding import PartitionSpec as P

ABSORPTION = 0.05
DAMPING = 0.8
F32 = jnp.float32
LANES = 128


def z_next(v):
    first = pltpu.roll(v[0], LANES - 1, 1)[None]
    return first if v.shape[0] == 1 else jnp.concatenate([v[1:], first], axis=0)


def z_prev(v):
    last = pltpu.roll(v[-1], 1, 1)[None]
    return last if v.shape[0] == 1 else jnp.concatenate([last, v[:-1]], axis=0)


def y_next(v):
    return pltpu.roll(v, v.shape[1] - 1, 1)


def y_prev(v):
    return pltpu.roll(v, 1, 1)


def flux_sum(u, u_next, flux_low, fx, fy, fz):
    flux_high = fx * (u - u_next)
    flux_y = fy * (u - y_next(u))
    flux_z = fz * (u - z_next(u))
    total = (flux_high - flux_low) + (flux_y - y_prev(flux_y)) + (flux_z - z_prev(flux_z))
    return ABSORPTION * u + total, flux_high


class Slabs:
    def __init__(self, flat, rows, parts=4):
        self.flat, self.rows, self.parts = flat, rows, parts

    def at(self, i):
        size = self.parts * self.rows
        return pl.ds(i * size, size)

    def __getitem__(self, i):
        return self.flat[self.at(i), :].reshape(self.parts, self.rows, LANES)

    def __setitem__(self, i, value):
        self.flat[self.at(i), :] = value.reshape(self.parts * self.rows, LANES)

    def part(self, i, start, size, step=1):
        where = lambda r: pl.ds((self.parts * i + r) * self.rows + start, size, step)
        return jnp.stack([self.flat[where(r), :] for r in range(self.parts)])

    def put(self, i, start, value):
        for r in range(self.parts):
            self.flat[pl.ds((self.parts * i + r) * self.rows + start, value.shape[1]), :] = value[r]


class Parted:
    def __init__(self, inner, outer, start, stop):
        self.inner, self.outer, self.start, self.stop = inner, outer, start, stop

    def place(self, i):
        if self.start <= i < self.stop:
            return self.inner, i - self.start
        return self.outer, i if i < self.start else i - (self.stop - self.start)

    def __getitem__(self, i):
        buffer, at = self.place(i)
        return buffer[at]

    def __setitem__(self, i, value):
        buffer, at = self.place(i)
        buffer[at] = value

    def part(self, i, start, size):
        buffer, at = self.place(i)
        if isinstance(buffer, (Parted, Slabs)):
            return buffer.part(at, start, size)
        return buffer[at, :, start : start + size, :]


def get(ref, i, rows):
    if rows is None:
        return ref[i]
    return ref.part(i, *rows) if hasattr(ref, "part") else ref[i, :, rows[0] : rows[0] + rows[1], :]


def put(ref, i, rows, value):
    if isinstance(ref, Parted):
        put(*ref.place(i), rows, value)
    elif rows is None:
        ref[i] = value
    else:
        ref[i, :, rows[0] : rows[0] + rows[1], :] = value


def every_row(i):
    return None


def face_pass(count, k_ref, fx, fy, fz, w, scale, k_at=0, done=(), rows=every_row):
    half = 0.5 * scale
    for i in range(count + 1):
        if i not in done or i - 1 not in done:
            fx[i] = half * (k_ref[k_at + i] + k_ref[k_at + 1 + i])
        if i == 0 or i - 1 in done:
            continue
        some = rows(i - 1)
        k = get(k_ref, k_at + i, some)
        face_y = half * (k + y_next(k))
        face_z = half * (k + z_next(k))
        diag = ABSORPTION + (get(fx, i, some) + get(fx, i - 1, some) + face_y + y_prev(face_y) + face_z + z_prev(face_z))
        put(fy, i - 1, some, face_y)
        put(fz, i - 1, some, face_z)
        put(w, i - 1, some, DAMPING / diag)


def sweep_pass(count, u_ref, u_at, faces_at, g_ref, g_at, fx, fy, fz, w, out, out_at, last=False, done=(), rows=every_row):
    low, low_rows = None, None
    for i in range(count):
        if i in done:
            low = None
            continue
        some, f = rows(i), faces_at + i
        u, u_next = get(u_ref, u_at + 1 + i, some), get(u_ref, u_at + 2 + i, some)
        if low is None or low_rows != some:
            low = get(fx, f, some) * (get(u_ref, u_at + i, some) - u)
        applied, low = flux_sum(u, u_next, low, get(fx, f + 1, some), get(fy, f, some), get(fz, f, some))
        low_rows = some
        rest = get(g_ref, g_at + i, some) - applied
        put(out, out_at + i, some, rest if last else u + get(w, f, some) * rest)


def neighbour_sweep(count, u_ref, g_ref, at, fx, fy, fz, w, out):
    for i in range(count):
        f, u = at + i, u_ref[1 + i]
        face_y, face_z = fy[f], fz[f]
        along_x = fx[f + 1] * u_ref[2 + i] + fx[f] * u_ref[i]
        along_y = face_y * y_next(u) + y_prev(face_y) * y_prev(u)
        along_z = face_z * z_next(u) + z_prev(face_z) * z_prev(u)
        out[i] = (1.0 - DAMPING) * u + w[f] * ((g_ref[f] + along_x) + (along_y + along_z))


def inverse_permutation():
    z, at = np.arange(512)[None, :], np.arange(512)[:, None]
    return jnp.asarray((z == 4 * (at % LANES) + at // LANES).astype(ml_dtypes.bfloat16))


def permutation(inverse):
    z = lax.broadcasted_iota(jnp.int32, (512, 512), 1 if inverse else 0)
    at = lax.broadcasted_iota(jnp.int32, (512, 512), 0 if inverse else 1)
    return jnp.where(z == 4 * (at % LANES) + at // LANES, 1.0, 0.0).astype(jnp.bfloat16)


def rearrange(rows, matrix):
    count = rows.shape[0]
    top = rows.astype(jnp.bfloat16)
    rest = rows - top.astype(F32)
    middle = rest.astype(jnp.bfloat16)
    bottom = (rest - middle.astype(F32)).astype(jnp.bfloat16)
    parts = jnp.concatenate([top, middle, bottom], axis=0)
    moved = lax.dot_general(parts, matrix, (((1,), (0,)), ((), ())), preferred_element_type=F32)
    return (moved[0:count] + moved[count : 2 * count]) + moved[2 * count :]


def permute_kernel(me, held, own_flat, to_first, to_second):
    matrix = permutation(False)
    moved = rearrange(held[...].reshape(128, 512), matrix)
    for x in range(16):
        for r in range(4):
            own_flat[32 * x + 8 * r : 32 * x + 8 * r + 8] = moved[8 * x : 8 * x + 8, LANES * r : LANES * r + LANES]
    own = Slabs(own_flat, 8)
    even = lax.rem(me[0], 2) == 0
    for take, high, low in ((even, to_second, to_first), (jnp.logical_not(even), to_first, to_second)):
        @pl.when(take)
        def _(high=high, low=low):
            for i in range(6):
                high[i] = own[2 + i]
                low[i] = own[i]
            for i in range(6, 14):
                high[i] = own[2 + i]
                low[i] = own[2 + i]


G_BORDER, K_BORDER = 6, 8
G_SLABS, K_SLABS = 8 + 2 * G_BORDER, 8 + 2 * K_BORDER
G_REACH = (5, 4, 3, 2, 1, 0)
K_REACH = (6, 6, 4, 4, 2, 1, 0)


def row_parts():
    for array, reaches, border in ((0, G_REACH, G_BORDER), (1, K_REACH, K_BORDER)):
        for d, reach in enumerate(reaches, 1):
            yield array, d, reach, border


FACE_ROWS = 32 * (len(G_REACH) + len(K_REACH))
CORNER_ROWS = 8 * (sum(G_REACH) + sum(K_REACH)) + 8


def face_kernel(own, to_high, to_low):
    for i, (array, d, _, _) in enumerate(row_parts()):
        for out, y in ((to_high, 8 - d), (to_low, d - 1)):
            out[32 * i : 32 * i + 32] = own[pl.ds(256 * array + y, 32, 8), :]


def corners():
    at = 0
    for array, d, reach, border in row_parts():
        for column in (border - reach, border + 8):
            if reach:
                yield array, d, column, 4 * reach, at
                at += 4 * reach


def wide_kernel(me, own, first, second, flat, to_high, to_low):
    out, own = Slabs(flat, 8), Slabs(own, 8)

    def put(at, source, start, size):
        for i in range(size):
            out[at + i] = source[start + i]

    put(6, own, 0, 8)
    put(28, own, 8, 8)
    even = lax.rem(me[0], 2) == 0
    for take, left, right in ((even, first, second), (jnp.logical_not(even), second, first)):
        @pl.when(take)
        def _(left=left, right=right):
            put(0, left, 0, 6)
            put(14, right, 0, 6)
            put(20, left, 6, 8)
            put(36, right, 6, 8)
    for array, d, column, size, at in corners():
        base = (G_SLABS * array + column) * 32
        to_high[at : at + size] = flat[pl.ds(base + 8 - d, size, 8), :]
        to_low[at : at + size] = flat[pl.ds(base + d - 1, size, 8), :]


def early_kernel(own, low, high, g_flat, k_flat, fx, fy, fz, w, uf, u0, res):
    own, flats = Slabs(own, 8), (g_flat, k_flat)
    g, k = Slabs(g_flat, 24), Slabs(k_flat, 24)
    for i in range(8):
        g.put(i, 8, own[i])
        k.put(i, 8, own[8 + i])
    for i, (array, d, _, _) in enumerate(row_parts()):
        flats[array][pl.ds(8 - d, 32, 24), :] = low[32 * i : 32 * i + 32]
        flats[array][pl.ds(15 + d, 32, 24), :] = high[32 * i : 32 * i + 32]
    face_pass(6, k, fx, fy, fz, w, 1.0)
    for i in range(6):
        uf[i] = w[i] * g[1 + i]
    sweep_pass(4, uf, 0, 1, g, 2, fx, fy, fz, w, u0, 0)
    sweep_pass(2, u0, 0, 2, g, 3, fx, fy, fz, w, res, 0, last=True)


def fine_kernel(me, wide, low_corners, high_corners, g_early, k_early, fx_early, fy_early, fz_early, w_early, uf_early,
                u0_early, res_early, piece, u0_kept, g_flat, k_flat, u1, rhs, u0_edge, fx, fy, fz, w, uf, res, s1, sc,
                mx, my, mz, mw, mf, mr, ck, near):
    flats = g_flat, k_flat
    wide, g, k = Slabs(wide, 8), Slabs(g_flat, 24), Slabs(k_flat, 24)
    for i in range(12):
        g.put(i, 8, wide[i if i < 6 else i + 8])
    for i in range(16):
        k.put(i, 8, wide[G_SLABS + (i if i < 8 else i + 8)])
    for array, d, column, size, at in corners():
        slab = column if column < (G_BORDER, K_BORDER)[array] else column - 8
        flats[array][pl.ds(slab * 96 + 8 - d, size, 24), :] = low_corners[at : at + size]
        flats[array][pl.ds(slab * 96 + 15 + d, size, 24), :] = high_corners[at : at + size]
    g, k = Parted(Slabs(g_early, 24), g, 6, 14), Parted(Slabs(k_early, 24), k, 8, 16)
    fx = Parted(fx_early, fx, 7, 14)
    fy, fz, w, uf = [Parted(*pair, 7, 13) for pair in ((fy_early, fy), (fz_early, fz), (w_early, w), (uf_early, uf))]
    u0 = Parted(Parted(u0_early, u0_kept, 5, 9), u0_edge, 2, 16)
    res = Parted(res_early, res, 7, 9)
    def beside(first_x, border):
        return lambda i: (4, 16) if first_x + i <= -border or first_x + i >= 7 + border else None

    face_pass(20, k, fx, fy, fz, w, 1.0, k_at=1, done=range(7, 13), rows=beside(-6, 3))
    for i in range(20):
        if not 7 <= i < 13:
            some = beside(-6, 3)(i)
            put(uf, i, some, get(w, i, some) * get(g, i, some))
    sweep_pass(18, uf, 0, 1, g, 1, fx, fy, fz, w, u0, 0, done=range(7, 11), rows=beside(-5, 2))
    sweep_pass(16, u0, 0, 2, g, 2, fx, fy, fz, w, res, 0, last=True, done=range(7, 9), rows=beside(-4, 1))
    for x in range(8):
        both = res[2 * x] + res[2 * x + 1]
        s1[x, 0] = both[0] + both[1]
        s1[x, 1] = both[2] + both[3]
    for x in range(10):
        both = k[2 + 2 * x] + k[3 + 2 * x]
        sc[x, 0] = both[0] + both[1]
        sc[x, 1] = both[2] + both[3]

    def rows(ref, x, start):
        return jnp.stack(
            [ref[x, r, pl.ds(start, 8, 2), :] + ref[x, r, pl.ds(start + 1, 8, 2), :] for r in range(2)]
        ) * 0.125

    half = 0.5 * 0.25
    k_mid = [rows(sc, x, 4) for x in range(10)]
    mx[0] = half * (k_mid[0] + k_mid[1])
    for x in range(8):
        here = k_mid[x + 1]
        face_x = half * (here + k_mid[x + 2])
        face_y = half * (here + rows(sc, x + 1, 6))
        face_z = half * (here + z_next(here))
        diag = ABSORPTION + (
            mx[x] + face_x + face_y + half * (here + rows(sc, x + 1, 2)) + face_z + z_prev(face_z)
        )
        mx[x + 1], my[x], mz[x] = face_x, face_y, face_z
        mw[x] = DAMPING / diag
        rhs[x] = rows(s1, x, 4)
        mf[x] = mw[x] * rhs[x]
    neighbour_sweep(6, mf, rhs, 1, mx, my, mz, mw, u1)
    sweep_pass(4, u1, 0, 2, rhs, 2, mx, my, mz, mw, mr, 0, last=True)
    for x in range(4):
        both = k_mid[2 * x + 1] + k_mid[2 * x + 2]
        ck[x, 0:8] = both[0] + both[1]
    k2 = [(ck[x, pl.ds(0, 4, 2), :] + ck[x, pl.ds(1, 4, 2), :]) * 0.125 for x in range(4)]
    half = 0.5 * 0.0625
    for x in range(2):
        here = k2[x + 1][1:3]
        face_z = half * (here + pltpu.roll(here, LANES - 1, 1))
        diag = ABSORPTION + (
            half * (here + k2[x][1:3]) + half * (here + k2[x + 2][1:3])
            + half * (here + k2[x + 1][0:2]) + half * (here + k2[x + 1][2:4])
            + face_z + pltpu.roll(face_z, 1, 1)
        )
        both = mr[2 * x] + mr[2 * x + 1]
        ck[x, 0:8] = both[0] + both[1]
        first_sweep = DAMPING / diag * ((ck[x, pl.ds(2, 2, 2), :] + ck[x, pl.ds(3, 2, 2), :]) * 0.125)
        for j in range(2):
            ck[3, 2 * j + x : 2 * j + x + 1, :] = first_sweep[j : j + 1]
            ck[3, 4 + 2 * j + x : 5 + 2 * j + x, :] = here[j : j + 1]
    level_2 = ck[3, 0:8]
    for to in range(piece.shape[0]):
        piece[to, 0:8, :] = level_2
    count = piece.shape[0]
    for to, column in ((lax.rem(me[0] + 1, count), 0), (lax.rem(me[0] + count - 1, count), 1)):
        for r in range(2):
            for x in range(3):
                at = 4 * (2 * x + r)
                near[column, at : at + 4, :] = u1[column + x + 1, r, 2:6, :]
            near[column, 24 + 4 * r : 28 + 4 * r, :] = rhs[column + 3, r, 2:6, :]
        piece[to, 8:40, :] = near[column, 0:32, :]


def prepare_middle_kernel(k_early, k_flat, fx, fy, fz, w, k_mid, sums):
    k = Parted(Slabs(k_early, 24), Slabs(k_flat, 24), 8, 16)
    for x in range(12):
        both = k[2 * x] + k[2 * x + 1]
        for r in range(2):
            sums[r] = both[2 * r] + both[2 * r + 1]
            k_mid[x, r] = (sums[r, pl.ds(4, 8, 2), :] + sums[r, pl.ds(5, 8, 2), :]) * 0.125
    face_pass(10, k_mid, fx, fy, fz, w, 0.25)


def prepare_kernel(u0_early, u0, g_early, g_flat, k_early, k_flat, u_out, g_out, fx, fy, fz, w, k_rows):
    g, k = Parted(Slabs(g_early, 24), Slabs(g_flat, 24), 6, 14), Parted(Slabs(k_early, 24), Slabs(k_flat, 24), 8, 16)
    u0 = Parted(u0_early, u0, 5, 9)
    for i in range(14):
        u_out[i] = u0.part(i, 4, 16)
        k_rows[i] = k.part(i + 5, 4, 16)
    for i in range(12):
        g_out[i] = g.part(i + 4, 4, 16)
    face_pass(12, k_rows, fx, fy, fz, w, 1.0)


EDGE_ROWS = 4 * 20 + 2 * 20 + 16


def middle_kernel(me, gathered, u1, rhs, here, to_high, to_low, level_1):
    count = gathered.shape[0]
    for block in range(11):
        source = lax.rem(me[0] + (block - 5 + count * 5), count)
        for j in range(2):
            for array in range(2):
                at = 4 * array + 2 * j
                here[2 * j + array, 2 * block : 2 * block + 2, :] = gathered[source, at : at + 2, :]
    u_flat, r_flat = level_1.at[0:192], level_1.at[192:360]
    u, g = Slabs(u_flat, 8, 2), Slabs(r_flat, 8, 2)
    for x in range(6):
        u[3 + x] = u1[x]
    for x in range(8):
        g[1 + x] = rhs[x]
    for source, column, edge in ((lax.rem(me[0] + count - 1, count), 0, 0), (lax.rem(me[0] + 1, count), 9, 9)):
        for r in range(2):
            for x in range(3):
                at = 8 + 4 * (2 * x + r)
                to = 8 * (2 * (column + x) + r) + 2
                u_flat[to : to + 4, :] = gathered[source, at : at + 4, :]
            to = 8 * (2 * edge + r) + 2
            r_flat[to : to + 4, :] = gathered[source, 32 + 4 * r : 36 + 4 * r, :]
    for out, row, rhs_row in ((to_high, 4, 5), (to_low, 2, 2)):
        for slab in range(4):
            out[20 * slab : 20 * slab + 20] = here[slab, 1:21]
        for i in range(2):
            out[80 + 20 * i : 100 + 20 * i] = level_1[pl.ds(16 + row + i, 20, 8), :]
        out[120:136] = level_1[pl.ds(192 + 16 + rhs_row, 16, 8), :]


SPREAD = (16, 14, 12, 10, 8, 6)


def spread(j, upward):
    d = j if upward else 5 - j
    return 3 + d, SPREAD[d], 2 * sum(SPREAD[:d])


def three_kernel(me, here, low, high, to_first, to_second):
    blocks = (low, here, high)
    even = lax.rem(me[0], 2) == 0
    for take, to_high, to_low in ((even, to_second, to_first), (jnp.logical_not(even), to_first, to_second)):
        @pl.when(take)
        def _(to_high=to_high, to_low=to_low):
            for j in range(6):
                source = blocks[j // 2]
                for out, upward in ((to_high, False), (to_low, True)):
                    start, size, at = spread(j, upward)
                    for array in range(2):
                        slab = 2 * (j % 2) + array
                        if source is here:
                            values = here[slab, start : start + size]
                        else:
                            values = source[20 * slab + start - 1 : 20 * slab + start - 1 + size]
                        out[at + size * array : at + size * array + size] = values


def window(reach):
    return (7, 8) if reach <= 3 else (3, 16) if reach <= 7 else (1, 24)


def coarse_kernel(me, first, here, second, left, right, level_1, fx, fy, fz, w, v_flat_out, to_high, to_low,
                  u, other, c, start, weights, v_flat, r_flat, va):
    half = 0.5 * 0.0625
    even = lax.rem(me[0], 2) == 0
    for take, below, above in ((even, first, second), (jnp.logical_not(even), second, first)):
        @pl.when(take)
        def _(below=below, above=above):
            for j in range(6):
                for source, upward, y in ((below, False, j), (above, True, 12 + j)):
                    column, size, at = spread(j, upward)
                    start[y, column : column + size] = source[at : at + size]
                    c[y, column : column + size] = source[at + size : at + 2 * size]
    for j in range(6):
        block, slab = (left, here, right)[j // 2], 2 * (j % 2)
        if block is here:
            start[6 + j, 0:24] = here[slab, 0:24]
            c[6 + j, 0:24] = here[slab + 1, 0:24]
        else:
            start[6 + j, 1:21] = block[20 * slab : 20 * slab + 20]
            c[6 + j, 1:21] = block[20 * slab + 20 : 20 * slab + 40]

    def reach(y, step):
        return 9 - step - max(0, 7 - y, y - 10)

    def at(ref, y, lo, size):
        return ref[y, lo : lo + size]

    for y in range(1, 17):
        lo, size = window(reach(y, 1))
        k = at(c, y, lo, size)
        face_z = half * (k + pltpu.roll(k, LANES - 1, 1))
        faces = [half * (k + at(c, y, lo + 1, size)), half * (k + at(c, y, lo - 1, size))]
        faces += [half * (k + at(c, y + 1, lo, size)), half * (k + at(c, y - 1, lo, size))]
        faces += [face_z, pltpu.roll(face_z, 1, 1)]
        scale = DAMPING / (ABSORPTION + ((faces[0] + faces[1]) + (faces[2] + faces[3]) + (faces[4] + faces[5])))
        for i, face in enumerate(faces):
            weights[i, y, lo : lo + size] = scale * face
    old = start
    for step in range(1, 8):
        new = (u, other)[step % 2]
        for y in range(step, 18 - step):
            lo, size = window(reach(y, step))
            now = at(old, y, lo, size)
            along_x = at(weights.at[0], y, lo, size) * at(old, y, lo + 1, size) + at(weights.at[1], y, lo, size) * at(old, y, lo - 1, size)
            along_y = at(weights.at[2], y, lo, size) * at(old, y + 1, lo, size) + at(weights.at[3], y, lo, size) * at(old, y - 1, lo, size)
            along_z = (
                at(weights.at[4], y, lo, size) * pltpu.roll(now, LANES - 1, 1)
                + at(weights.at[5], y, lo, size) * pltpu.roll(now, 1, 1)
            )
            new[y, lo : lo + size] = ((1.0 - DAMPING) * now + at(start, y, lo, size)) + along_y + (along_x + along_z)
        old = new
    u = old
    v_flat[0:192] = level_1[0:192]
    r_flat[0:160] = level_1[192:352]
    for source, row, rhs_row in ((left, 0, 1), (right, 6, 6)):
        for i in range(2):
            v_flat[pl.ds(16 + row + i, 20, 8), :] = source[80 + 20 * i : 100 + 20 * i]
        r_flat[pl.ds(16 + rhs_row, 16, 8), :] = source[120:136]
    v, rhs = Slabs(v_flat, 8, 2), Slabs(r_flat, 8, 2)
    for x in range(6):
        rows = jnp.concatenate(
            [jnp.broadcast_to(u[7 + j, 8 + x : 9 + x, :], (2, LANES)) for j in range(4)], axis=0
        )
        for twin in range(2):
            v[2 * x + twin] = v[2 * x + twin] + rows[None]
    neighbour_sweep(10, v, rhs, 0, fx, fy, fz, w, va)
    neighbour_sweep(8, va, rhs, 1, fx, fy, fz, w, Slabs(v_flat_out, 8, 2))
    for out, row in ((to_high, 4), (to_low, 2)):
        for i in range(2):
            out[16 * i : 16 * i + 16] = v_flat_out[pl.ds(row + i, 16, 8), :]


def last_kernel(v_here, v_low, v_high, u0, g, fx, fy, fz, w, matrix, correction, residual, v_flat, wide, ua, ub, res, held, left):
    v_flat[...] = v_here[...]
    for source, row in ((v_low, 0), (v_high, 6)):
        for i in range(2):
            v_flat[pl.ds(row + i, 16, 8), :] = source[16 * i : 16 * i + 16]
    for x in range(8):
        for r in range(2):
            rows = v_flat[8 * (2 * x + r) : 8 * (2 * x + r) + 8]
            wide[x, r, pl.ds(0, 8, 2), :] = rows
            wide[x, r, pl.ds(1, 8, 2), :] = rows
    for i in range(14):
        fine = wide[(i + 1) // 2]
        ua[i] = u0[i] + jnp.stack([fine[0], fine[0], fine[1], fine[1]])
    sweep_pass(12, ua, 0, 0, g, 0, fx, fy, fz, w, ub, 0)
    sweep_pass(10, ub, 0, 1, g, 1, fx, fy, fz, w, ua, 0)
    copies = []

    def leave(index, source, at, out, start, size):
        rows = [
            jnp.concatenate([source[at + x, r, 4:12, :] for r in range(4)], axis=1) for x in range(start, start + size)
        ]
        held[index, start : start + size] = rearrange(jnp.concatenate(rows, axis=0), matrix[...]).reshape(size, 8, 512)
        part = pl.ds(start, size)
        copy = pltpu.make_async_copy(held.at[index, part], out.at[part], left.at[len(copies)])
        copy.start()
        copies.append(copy)

    leave(0, ua, 1, correction, 0, 8)
    sweep_pass(4, ua, 0, 2, g, 2, fx, fy, fz, w, res, 0, last=True)
    leave(1, res, 0, residual, 0, 4)
    sweep_pass(4, ua, 4, 6, g, 6, fx, fy, fz, w, res, 4, last=True)
    leave(1, res, 0, residual, 4, 4)
    for copy in copies:
        copy.wait()


VMEM = pl.BlockSpec(memory_space=pltpu.VMEM)
SMEM = pl.BlockSpec(memory_space=pltpu.SMEM)
HBM = pl.BlockSpec(memory_space=pltpu.HBM)


def call(kernel, outs, scratch, *arrays, scalars=0, to_hbm=False, extra=()):
    return pl.pallas_call(
        kernel,
        out_shape=[jax.ShapeDtypeStruct(shape, F32) for shape in outs],
        in_specs=[SMEM] * scalars + [VMEM] * (len(arrays) - scalars),
        out_specs=[HBM if to_hbm else VMEM] * len(outs),
        scratch_shapes=[pltpu.VMEM(shape, F32) for shape in scratch] + list(extra),
        compiler_params=pltpu.CompilerParams(vmem_limit_bytes=32 * 2**20),
    )(*arrays)


def shift(array, axis, by):
    count = lax.axis_size(axis)
    return lax.ppermute(array, axis, [(i, (i + by) % count) for i in range(count)])


def swap(array, axis, start, by=1):
    count = lax.axis_size(axis)
    pairs = [(i, (i + by) % count) for i in range(start, count, 2)]
    return lax.ppermute(array, axis, pairs + [(j, i) for i, j in pairs])


def per_device(right_side, coefficient):
    me_x = lax.axis_index("gx").astype(jnp.int32).reshape(1)
    me_y = lax.axis_index("gy").astype(jnp.int32).reshape(1)
    count = lax.axis_size("gx")
    border = (G_BORDER + K_BORDER, 4, 8, 128)
    own, first, second = call(
        permute_kernel, [(512, 128), border, border], [], me_x, jnp.stack([right_side, coefficient]), scalars=1
    )
    first, second = swap(first, "gx", 1), swap(second, "gx", 0)
    high, low = call(face_kernel, [(FACE_ROWS, 128), (FACE_ROWS, 128)], [], own)
    low, high = shift(high, "gy", 1), shift(low, "gy", -1)
    wide, high_corners, low_corners = call(
        wide_kernel, [((G_SLABS + K_SLABS) * 32, 128), (CORNER_ROWS, 128), (CORNER_ROWS, 128)], [],
        me_x, own, first, second, scalars=1,
    )
    low_corners, high_corners = shift(high_corners, "gy", 1), shift(low_corners, "gy", -1)
    fine, mid, last = (4, 24, 128), (2, 8, 128), (4, 16, 128)
    early = call(
        early_kernel,
        [(8 * 96, 128), (8 * 96, 128), (7, *fine), (6, *fine), (6, *fine), (6, *fine), (6, *fine), (4, *fine), (2, *fine)],
        [], own, low, high,
    )
    g_early, k_early, u0_early = early[0], early[1], early[7]
    piece, u0, g, k, u1, rhs = call(
        fine_kernel,
        [(count, 40, 128), (10, *fine), (12 * 96, 128), (16 * 96, 128), (6, *mid), (8, *mid)],
        [(4, *fine), (14, *fine), (14, *fine), (14, *fine), (14, *fine), (14, *fine), (14, *fine), (8, 2, 24, 128), (10, 2, 24, 128),
         (9, *mid), (8, *mid), (8, *mid), (8, *mid), (8, *mid), (4, *mid), (4, 16, 128), (2, 40, 128)],
        me_x, wide, low_corners, high_corners, *early, scalars=1,
    )
    piece, u0, g, k, u1, rhs = lax.optimization_barrier((piece, u0, g, k, u1, rhs))
    gathered = lax.all_to_all(piece, "gx", 0, 0)
    gathered, u0, g, k, u1, rhs = lax.optimization_barrier((gathered, u0, g, k, u1, rhs))
    here, high, low, level_1 = call(
        middle_kernel, [(4, 32, 128), (EDGE_ROWS, 128), (EDGE_ROWS, 128), (360, 128)], [], me_x, gathered, u1, rhs, scalars=1
    )
    low, high = shift(high, "gy", 1), shift(low, "gy", -1)
    first, second = call(three_kernel, [(136, 128), (136, 128)], [], me_y, here, low, high, scalars=1)
    first, second = swap(first, "gy", 1, 3), swap(second, "gy", 0, 3)
    faces = call(
        prepare_middle_kernel, [(11, *mid), (10, *mid), (10, *mid), (10, *mid)], [(12, *mid), (2, 24, 128)], k_early, k
    )
    rows = (18, 32, 128)
    v1, high_rows, low_rows = call(
        coarse_kernel, [(128, 128), (32, 128), (32, 128)],
        [rows, rows, rows, rows, (6, *rows), (216, 128), (168, 128), (10, *mid)],
        me_y, first, here, second, low, high, level_1, *faces, scalars=1,
    )
    u0, g, *faces = call(
        prepare_kernel, [(14, *last), (12, *last), (13, *last), (12, *last), (12, *last), (12, *last)], [(14, *last)],
        u0_early, u0, g_early, g, k_early, k,
    )
    low, high = shift(high_rows, "gy", 1), shift(low_rows, "gy", -1)
    return tuple(call(
        last_kernel, [(8, 8, 512), (8, 8, 512)],
        [(128, 128), (8, 2, 16, 128), (14, *last), (12, *last), (8, *last), (2, 8, 8, 512)],
        v1, low, high, u0, g, *faces, inverse_permutation(), to_hbm=True, extra=[pltpu.SemaphoreType.DMA((3,))],
    ))


def solution(mesh):
    placed = (P("gx", "gy", None), P("gx", "gy", None))
    return jax.shard_map(per_device, mesh=mesh, in_specs=placed, out_specs=placed, check_vma=False)
```

```python
import jax
import jax.numpy as jnp
import ml_dtypes
import numpy as np
from jax import lax
from jax.experimental import pallas as pl
from jax.experimental.pallas import tpu as pltpu
from jax.sharding import PartitionSpec as P

ABSORPTION = 0.05
DAMPING = 0.8
F32 = jnp.float32
LANES = 128


def z_next(v):
    first = pltpu.roll(v[0], LANES - 1, 1)[None]
    return first if v.shape[0] == 1 else jnp.concatenate([v[1:], first], axis=0)


def z_prev(v):
    last = pltpu.roll(v[-1], 1, 1)[None]
    return last if v.shape[0] == 1 else jnp.concatenate([last, v[:-1]], axis=0)


def y_next(v):
    return pltpu.roll(v, v.shape[1] - 1, 1)


def y_prev(v):
    return pltpu.roll(v, 1, 1)


def flux_sum(u, u_next, flux_low, fx, fy, fz):
    flux_high = fx * (u - u_next)
    flux_y = fy * (u - y_next(u))
    flux_z = fz * (u - z_next(u))
    total = (flux_high - flux_low) + (flux_y - y_prev(flux_y)) + (flux_z - z_prev(flux_z))
    return ABSORPTION * u + total, flux_high


class Slabs:
    def __init__(self, flat, rows, parts=4):
        self.flat, self.rows, self.parts = flat, rows, parts

    def at(self, i):
        size = self.parts * self.rows
        return pl.ds(i * size, size)

    def __getitem__(self, i):
        return self.flat[self.at(i), :].reshape(self.parts, self.rows, LANES)

    def __setitem__(self, i, value):
        self.flat[self.at(i), :] = value.reshape(self.parts * self.rows, LANES)

    def part(self, i, start, size, step=1):
        where = lambda r: pl.ds((self.parts * i + r) * self.rows + start, size, step)
        return jnp.stack([self.flat[where(r), :] for r in range(self.parts)])

    def put(self, i, start, value):
        for r in range(self.parts):
            self.flat[pl.ds((self.parts * i + r) * self.rows + start, value.shape[1]), :] = value[r]


class Parted:
    def __init__(self, inner, outer, start, stop):
        self.inner, self.outer, self.start, self.stop = inner, outer, start, stop

    def place(self, i):
        if self.start <= i < self.stop:
            return self.inner, i - self.start
        return self.outer, i if i < self.start else i - (self.stop - self.start)

    def __getitem__(self, i):
        buffer, at = self.place(i)
        return buffer[at]

    def __setitem__(self, i, value):
        buffer, at = self.place(i)
        buffer[at] = value

    def part(self, i, start, size):
        buffer, at = self.place(i)
        if isinstance(buffer, (Parted, Slabs)):
            return buffer.part(at, start, size)
        return buffer[at, :, start : start + size, :]


def get(ref, i, rows):
    if rows is None:
        return ref[i]
    return ref.part(i, *rows) if hasattr(ref, "part") else ref[i, :, rows[0] : rows[0] + rows[1], :]


def put(ref, i, rows, value):
    if isinstance(ref, Parted):
        put(*ref.place(i), rows, value)
    elif rows is None:
        ref[i] = value
    else:
        ref[i, :, rows[0] : rows[0] + rows[1], :] = value


def every_row(i):
    return None


def face_pass(count, k_ref, fx, fy, fz, w, scale, k_at=0, done=(), rows=every_row):
    half = 0.5 * scale
    for i in range(count + 1):
        if i not in done or i - 1 not in done:
            fx[i] = half * (k_ref[k_at + i] + k_ref[k_at + 1 + i])
        if i == 0 or i - 1 in done:
            continue
        some = rows(i - 1)
        k = get(k_ref, k_at + i, some)
        face_y = half * (k + y_next(k))
        face_z = half * (k + z_next(k))
        diag = ABSORPTION + (get(fx, i, some) + get(fx, i - 1, some) + face_y + y_prev(face_y) + face_z + z_prev(face_z))
        put(fy, i - 1, some, face_y)
        put(fz, i - 1, some, face_z)
        put(w, i - 1, some, DAMPING / diag)


def sweep_pass(count, u_ref, u_at, faces_at, g_ref, g_at, fx, fy, fz, w, out, out_at, last=False, done=(), rows=every_row):
    low, low_rows = None, None
    for i in range(count):
        if i in done:
            low = None
            continue
        some, f = rows(i), faces_at + i
        u, u_next = get(u_ref, u_at + 1 + i, some), get(u_ref, u_at + 2 + i, some)
        if low is None or low_rows != some:
            low = get(fx, f, some) * (get(u_ref, u_at + i, some) - u)
        applied, low = flux_sum(u, u_next, low, get(fx, f + 1, some), get(fy, f, some), get(fz, f, some))
        low_rows = some
        rest = get(g_ref, g_at + i, some) - applied
        put(out, out_at + i, some, rest if last else u + get(w, f, some) * rest)


def neighbour_sweep(count, u_ref, g_ref, at, fx, fy, fz, w, out):
    for i in range(count):
        f, u = at + i, u_ref[1 + i]
        face_y, face_z = fy[f], fz[f]
        along_x = fx[f + 1] * u_ref[2 + i] + fx[f] * u_ref[i]
        along_y = face_y * y_next(u) + y_prev(face_y) * y_prev(u)
        along_z = face_z * z_next(u) + z_prev(face_z) * z_prev(u)
        out[i] = (1.0 - DAMPING) * u + w[f] * ((g_ref[f] + along_x) + (along_y + along_z))


def inverse_permutation():
    z, at = np.arange(512)[None, :], np.arange(512)[:, None]
    return jnp.asarray((z == 4 * (at % LANES) + at // LANES).astype(ml_dtypes.bfloat16))


def permutation(inverse):
    z = lax.broadcasted_iota(jnp.int32, (512, 512), 1 if inverse else 0)
    at = lax.broadcasted_iota(jnp.int32, (512, 512), 0 if inverse else 1)
    return jnp.where(z == 4 * (at % LANES) + at // LANES, 1.0, 0.0).astype(jnp.bfloat16)


def rearrange(rows, matrix):
    count = rows.shape[0]
    top = rows.astype(jnp.bfloat16)
    rest = rows - top.astype(F32)
    middle = rest.astype(jnp.bfloat16)
    bottom = (rest - middle.astype(F32)).astype(jnp.bfloat16)
    parts = jnp.concatenate([top, middle, bottom], axis=0)
    moved = lax.dot_general(parts, matrix, (((1,), (0,)), ((), ())), preferred_element_type=F32)
    return (moved[0:count] + moved[count : 2 * count]) + moved[2 * count :]


def permute_kernel(me, held, own_flat, to_first, to_second):
    matrix = permutation(False)
    moved = rearrange(held[...].reshape(128, 512), matrix)
    for x in range(16):
        for r in range(4):
            own_flat[32 * x + 8 * r : 32 * x + 8 * r + 8] = moved[8 * x : 8 * x + 8, LANES * r : LANES * r + LANES]
    own = Slabs(own_flat, 8)
    even = lax.rem(me[0], 2) == 0
    for take, high, low in ((even, to_second, to_first), (jnp.logical_not(even), to_first, to_second)):
        @pl.when(take)
        def _(high=high, low=low):
            for i in range(6):
                high[i] = own[2 + i]
                low[i] = own[i]
            for i in range(6, 14):
                high[i] = own[2 + i]
                low[i] = own[2 + i]


G_BORDER, K_BORDER = 6, 8
G_SLABS, K_SLABS = 8 + 2 * G_BORDER, 8 + 2 * K_BORDER
G_REACH = (5, 4, 3, 2, 1, 0)
K_REACH = (6, 6, 4, 4, 2, 1, 0)


def row_parts():
    for array, reaches, border in ((0, G_REACH, G_BORDER), (1, K_REACH, K_BORDER)):
        for d, reach in enumerate(reaches, 1):
            yield array, d, reach, border


FACE_ROWS = 32 * (len(G_REACH) + len(K_REACH))
CORNER_ROWS = 8 * (sum(G_REACH) + sum(K_REACH)) + 8


def face_kernel(own, to_high, to_low):
    for i, (array, d, _, _) in enumerate(row_parts()):
        for out, y in ((to_high, 8 - d), (to_low, d - 1)):
            out[32 * i : 32 * i + 32] = own[pl.ds(256 * array + y, 32, 8), :]


def corners():
    at = 0
    for array, d, reach, border in row_parts():
        for column in (border - reach, border + 8):
            if reach:
                yield array, d, column, 4 * reach, at
                at += 4 * reach


def wide_kernel(me, own, first, second, flat, to_high, to_low):
    out, own = Slabs(flat, 8), Slabs(own, 8)

    def put(at, source, start, size):
        for i in range(size):
            out[at + i] = source[start + i]

    put(6, own, 0, 8)
    put(28, own, 8, 8)
    even = lax.rem(me[0], 2) == 0
    for take, left, right in ((even, first, second), (jnp.logical_not(even), second, first)):
        @pl.when(take)
        def _(left=left, right=right):
            put(0, left, 0, 6)
            put(14, right, 0, 6)
            put(20, left, 6, 8)
            put(36, right, 6, 8)
    for array, d, column, size, at in corners():
        base = (G_SLABS * array + column) * 32
        to_high[at : at + size] = flat[pl.ds(base + 8 - d, size, 8), :]
        to_low[at : at + size] = flat[pl.ds(base + d - 1, size, 8), :]


def early_kernel(own, low, high, g_flat, k_flat, fx, fy, fz, w, uf, u0, res):
    own, flats = Slabs(own, 8), (g_flat, k_flat)
    g, k = Slabs(g_flat, 24), Slabs(k_flat, 24)
    for i in range(8):
        g.put(i, 8, own[i])
        k.put(i, 8, own[8 + i])
    for i, (array, d, _, _) in enumerate(row_parts()):
        flats[array][pl.ds(8 - d, 32, 24), :] = low[32 * i : 32 * i + 32]
        flats[array][pl.ds(15 + d, 32, 24), :] = high[32 * i : 32 * i + 32]
    face_pass(6, k, fx, fy, fz, w, 1.0)
    for i in range(6):
        uf[i] = w[i] * g[1 + i]
    sweep_pass(4, uf, 0, 1, g, 2, fx, fy, fz, w, u0, 0)
    sweep_pass(2, u0, 0, 2, g, 3, fx, fy, fz, w, res, 0, last=True)


def fine_kernel(me, wide, low_corners, high_corners, g_early, k_early, fx_early, fy_early, fz_early, w_early, uf_early,
                u0_early, res_early, piece, u0_kept, g_flat, k_flat, u1, rhs, u0_edge, fx, fy, fz, w, uf, res, s1, sc,
                mx, my, mz, mw, mf, mr, ck, near, md):
    flats = g_flat, k_flat
    wide, g, k = Slabs(wide, 8), Slabs(g_flat, 24), Slabs(k_flat, 24)
    for i in range(12):
        g.put(i, 8, wide[i if i < 6 else i + 8])
    for i in range(16):
        k.put(i, 8, wide[G_SLABS + (i if i < 8 else i + 8)])
    for array, d, column, size, at in corners():
        slab = column if column < (G_BORDER, K_BORDER)[array] else column - 8
        flats[array][pl.ds(slab * 96 + 8 - d, size, 24), :] = low_corners[at : at + size]
        flats[array][pl.ds(slab * 96 + 15 + d, size, 24), :] = high_corners[at : at + size]
    g, k = Parted(Slabs(g_early, 24), g, 6, 14), Parted(Slabs(k_early, 24), k, 8, 16)
    fx = Parted(fx_early, fx, 7, 14)
    fy, fz, w, uf = [Parted(*pair, 7, 13) for pair in ((fy_early, fy), (fz_early, fz), (w_early, w), (uf_early, uf))]
    u0 = Parted(Parted(u0_early, u0_kept, 5, 9), u0_edge, 2, 16)
    res = Parted(res_early, res, 7, 9)
    def beside(first_x, border):
        return lambda i: (4, 16) if first_x + i <= -border or first_x + i >= 7 + border else None

    face_pass(20, k, fx, fy, fz, w, 1.0, k_at=1, done=range(7, 13), rows=beside(-6, 3))
    for i in range(20):
        if not 7 <= i < 13:
            some = beside(-6, 3)(i)
            put(uf, i, some, get(w, i, some) * get(g, i, some))
    sweep_pass(18, uf, 0, 1, g, 1, fx, fy, fz, w, u0, 0, done=range(7, 11), rows=beside(-5, 2))
    sweep_pass(16, u0, 0, 2, g, 2, fx, fy, fz, w, res, 0, last=True, done=range(7, 9), rows=beside(-4, 1))
    for x in range(8):
        both = res[2 * x] + res[2 * x + 1]
        s1[x, 0] = both[0] + both[1]
        s1[x, 1] = both[2] + both[3]
    for x in range(10):
        both = k[2 + 2 * x] + k[3 + 2 * x]
        sc[x, 0] = both[0] + both[1]
        sc[x, 1] = both[2] + both[3]

    def rows(ref, x, start):
        return jnp.stack(
            [ref[x, r, pl.ds(start, 8, 2), :] + ref[x, r, pl.ds(start + 1, 8, 2), :] for r in range(2)]
        ) * 0.125

    half = 0.5 * 0.25
    k_mid = [rows(sc, x, 4) for x in range(10)]
    mx[0] = half * (k_mid[0] + k_mid[1])
    for x in range(8):
        here = k_mid[x + 1]
        face_x = half * (here + k_mid[x + 2])
        face_y = half * (here + rows(sc, x + 1, 6))
        face_z = half * (here + z_next(here))
        diag = ABSORPTION + (
            mx[x] + face_x + face_y + half * (here + rows(sc, x + 1, 2)) + face_z + z_prev(face_z)
        )
        mx[x + 1], my[x], mz[x] = face_x, face_y, face_z
        mw[x] = DAMPING / diag
        md[x] = diag
        rhs[x] = rows(s1, x, 4)
        mf[x] = mw[x] * rhs[x]
    neighbour_sweep(6, mf, rhs, 1, mx, my, mz, mw, u1)
    for i in range(4):
        f, u = 2 + i, u1[1 + i]
        along_x = mx[f + 1] * u1[2 + i] + mx[f] * u1[i]
        along_y = my[f] * y_next(u) + y_prev(my[f]) * y_prev(u)
        along_z = mz[f] * z_next(u) + z_prev(mz[f]) * z_prev(u)
        mr[i] = (rhs[f] - md[f] * u) + (along_x + (along_y + along_z))
    for x in range(4):
        both = k_mid[2 * x + 1] + k_mid[2 * x + 2]
        ck[x, 0:8] = both[0] + both[1]
    k2 = [(ck[x, pl.ds(0, 4, 2), :] + ck[x, pl.ds(1, 4, 2), :]) * 0.125 for x in range(4)]
    half = 0.5 * 0.0625
    for x in range(2):
        here = k2[x + 1][1:3]
        face_z = half * (here + pltpu.roll(here, LANES - 1, 1))
        diag = ABSORPTION + (
            half * (here + k2[x][1:3]) + half * (here + k2[x + 2][1:3])
            + half * (here + k2[x + 1][0:2]) + half * (here + k2[x + 1][2:4])
            + face_z + pltpu.roll(face_z, 1, 1)
        )
        both = mr[2 * x] + mr[2 * x + 1]
        ck[x, 0:8] = both[0] + both[1]
        first_sweep = DAMPING / diag * ((ck[x, pl.ds(2, 2, 2), :] + ck[x, pl.ds(3, 2, 2), :]) * 0.125)
        for j in range(2):
            ck[3, 2 * j + x : 2 * j + x + 1, :] = first_sweep[j : j + 1]
            ck[3, 4 + 2 * j + x : 5 + 2 * j + x, :] = here[j : j + 1]
    level_2 = ck[3, 0:8]
    for to in range(piece.shape[0]):
        piece[to, 0:8, :] = level_2
    count = piece.shape[0]
    for to, column in ((lax.rem(me[0] + 1, count), 0), (lax.rem(me[0] + count - 1, count), 1)):
        for r in range(2):
            for x in range(3):
                at = 4 * (2 * x + r)
                near[column, at : at + 4, :] = u1[column + x + 1, r, 2:6, :]
            near[column, 24 + 4 * r : 28 + 4 * r, :] = rhs[column + 3, r, 2:6, :]
        piece[to, 8:40, :] = near[column, 0:32, :]


def prepare_middle_kernel(k_early, k_flat, fx, fy, fz, w, k_mid, sums):
    k = Parted(Slabs(k_early, 24), Slabs(k_flat, 24), 8, 16)
    for x in range(12):
        both = k[2 * x] + k[2 * x + 1]
        for r in range(2):
            sums[r] = both[2 * r] + both[2 * r + 1]
            k_mid[x, r] = (sums[r, pl.ds(4, 8, 2), :] + sums[r, pl.ds(5, 8, 2), :]) * 0.125
    face_pass(10, k_mid, fx, fy, fz, w, 0.25)


def prepare_kernel(u0_early, u0, g_early, g_flat, k_early, k_flat, u_out, g_out, fx, fy, fz, w, k_rows):
    g, k = Parted(Slabs(g_early, 24), Slabs(g_flat, 24), 6, 14), Parted(Slabs(k_early, 24), Slabs(k_flat, 24), 8, 16)
    u0 = Parted(u0_early, u0, 5, 9)
    for i in range(14):
        u_out[i] = u0.part(i, 4, 16)
        k_rows[i] = k.part(i + 5, 4, 16)
    for i in range(12):
        g_out[i] = g.part(i + 4, 4, 16)
    face_pass(12, k_rows, fx, fy, fz, w, 1.0)


EDGE_ROWS = 4 * 20 + 2 * 20 + 16


def middle_kernel(me, gathered, u1, rhs, here, to_high, to_low, level_1):
    count = gathered.shape[0]
    for block in range(11):
        source = lax.rem(me[0] + (block - 5 + count * 5), count)
        for j in range(2):
            for array in range(2):
                at = 4 * array + 2 * j
                here[2 * j + array, 2 * block : 2 * block + 2, :] = gathered[source, at : at + 2, :]
    u_flat, r_flat = level_1.at[0:192], level_1.at[192:360]
    u, g = Slabs(u_flat, 8, 2), Slabs(r_flat, 8, 2)
    for x in range(6):
        u[3 + x] = u1[x]
    for x in range(8):
        g[1 + x] = rhs[x]
    for source, column, edge in ((lax.rem(me[0] + count - 1, count), 0, 0), (lax.rem(me[0] + 1, count), 9, 9)):
        for r in range(2):
            for x in range(3):
                at = 8 + 4 * (2 * x + r)
                to = 8 * (2 * (column + x) + r) + 2
                u_flat[to : to + 4, :] = gathered[source, at : at + 4, :]
            to = 8 * (2 * edge + r) + 2
            r_flat[to : to + 4, :] = gathered[source, 32 + 4 * r : 36 + 4 * r, :]
    for out, row, rhs_row in ((to_high, 4, 5), (to_low, 2, 2)):
        for slab in range(4):
            out[20 * slab : 20 * slab + 20] = here[slab, 1:21]
        for i in range(2):
            out[80 + 20 * i : 100 + 20 * i] = level_1[pl.ds(16 + row + i, 20, 8), :]
        out[120:136] = level_1[pl.ds(192 + 16 + rhs_row, 16, 8), :]


SPREAD = (16, 14, 12, 10, 8, 6)


def spread(j, upward):
    d = j if upward else 5 - j
    return 3 + d, SPREAD[d], 2 * sum(SPREAD[:d])


def three_kernel(me, here, low, high, to_first, to_second):
    blocks = (low, here, high)
    even = lax.rem(me[0], 2) == 0
    for take, to_high, to_low in ((even, to_second, to_first), (jnp.logical_not(even), to_first, to_second)):
        @pl.when(take)
        def _(to_high=to_high, to_low=to_low):
            for j in range(6):
                source = blocks[j // 2]
                for out, upward in ((to_high, False), (to_low, True)):
                    start, size, at = spread(j, upward)
                    for array in range(2):
                        slab = 2 * (j % 2) + array
                        if source is here:
                            values = here[slab, start : start + size]
                        else:
                            values = source[20 * slab + start - 1 : 20 * slab + start - 1 + size]
                        out[at + size * array : at + size * array + size] = values


def window(reach):
    return (7, 8) if reach <= 3 else (3, 16) if reach <= 7 else (1, 24)


def coarse_kernel(me, first, here, second, left, right, level_1, fx, fy, fz, w, v_flat_out, to_high, to_low,
                  u, other, c, start, weights, v_flat, r_flat, va):
    half = 0.5 * 0.0625
    even = lax.rem(me[0], 2) == 0
    for take, below, above in ((even, first, second), (jnp.logical_not(even), second, first)):
        @pl.when(take)
        def _(below=below, above=above):
            for j in range(6):
                for source, upward, y in ((below, False, j), (above, True, 12 + j)):
                    column, size, at = spread(j, upward)
                    start[y, column : column + size] = source[at : at + size]
                    c[y, column : column + size] = source[at + size : at + 2 * size]
    for j in range(6):
        block, slab = (left, here, right)[j // 2], 2 * (j % 2)
        if block is here:
            start[6 + j, 0:24] = here[slab, 0:24]
            c[6 + j, 0:24] = here[slab + 1, 0:24]
        else:
            start[6 + j, 1:21] = block[20 * slab : 20 * slab + 20]
            c[6 + j, 1:21] = block[20 * slab + 20 : 20 * slab + 40]

    def reach(y, step):
        return 9 - step - max(0, 7 - y, y - 10)

    def at(ref, y, lo, size):
        return ref[y, lo : lo + size]

    for y in range(1, 17):
        lo, size = window(reach(y, 1))
        k = at(c, y, lo, size)
        face_z = half * (k + pltpu.roll(k, LANES - 1, 1))
        faces = [half * (k + at(c, y, lo + 1, size)), half * (k + at(c, y, lo - 1, size))]
        faces += [half * (k + at(c, y + 1, lo, size)), half * (k + at(c, y - 1, lo, size))]
        faces += [face_z, pltpu.roll(face_z, 1, 1)]
        scale = DAMPING / (ABSORPTION + ((faces[0] + faces[1]) + (faces[2] + faces[3]) + (faces[4] + faces[5])))
        for i, face in enumerate(faces):
            weights[i, y, lo : lo + size] = scale * face
    old = start
    for step in range(1, 8):
        new = (u, other)[step % 2]
        for y in range(step, 18 - step):
            lo, size = window(reach(y, step))
            now = at(old, y, lo, size)
            along_x = at(weights.at[0], y, lo, size) * at(old, y, lo + 1, size) + at(weights.at[1], y, lo, size) * at(old, y, lo - 1, size)
            along_y = at(weights.at[2], y, lo, size) * at(old, y + 1, lo, size) + at(weights.at[3], y, lo, size) * at(old, y - 1, lo, size)
            along_z = (
                at(weights.at[4], y, lo, size) * pltpu.roll(now, LANES - 1, 1)
                + at(weights.at[5], y, lo, size) * pltpu.roll(now, 1, 1)
            )
            new[y, lo : lo + size] = ((1.0 - DAMPING) * now + at(start, y, lo, size)) + along_y + (along_x + along_z)
        old = new
    u = old
    v_flat[0:192] = level_1[0:192]
    r_flat[0:160] = level_1[192:352]
    for source, row, rhs_row in ((left, 0, 1), (right, 6, 6)):
        for i in range(2):
            v_flat[pl.ds(16 + row + i, 20, 8), :] = source[80 + 20 * i : 100 + 20 * i]
        r_flat[pl.ds(16 + rhs_row, 16, 8), :] = source[120:136]
    v, rhs = Slabs(v_flat, 8, 2), Slabs(r_flat, 8, 2)
    for x in range(6):
        rows = jnp.concatenate(
            [jnp.broadcast_to(u[7 + j, 8 + x : 9 + x, :], (2, LANES)) for j in range(4)], axis=0
        )
        for twin in range(2):
            v[2 * x + twin] = v[2 * x + twin] + rows[None]
    neighbour_sweep(10, v, rhs, 0, fx, fy, fz, w, va)
    neighbour_sweep(8, va, rhs, 1, fx, fy, fz, w, Slabs(v_flat_out, 8, 2))
    for out, row in ((to_high, 4), (to_low, 2)):
        for i in range(2):
            out[16 * i : 16 * i + 16] = v_flat_out[pl.ds(row + i, 16, 8), :]


def last_kernel(v_here, v_low, v_high, u0, g, fx, fy, fz, w, matrix, correction, residual, v_flat, wide, ua, ub, res, held, left):
    v_flat[...] = v_here[...]
    for source, row in ((v_low, 0), (v_high, 6)):
        for i in range(2):
            v_flat[pl.ds(row + i, 16, 8), :] = source[16 * i : 16 * i + 16]
    for x in range(8):
        for r in range(2):
            rows = v_flat[8 * (2 * x + r) : 8 * (2 * x + r) + 8]
            wide[x, r, pl.ds(0, 8, 2), :] = rows
            wide[x, r, pl.ds(1, 8, 2), :] = rows
    for i in range(14):
        fine = wide[(i + 1) // 2]
        ua[i] = u0[i] + jnp.stack([fine[0], fine[0], fine[1], fine[1]])
    sweep_pass(12, ua, 0, 0, g, 0, fx, fy, fz, w, ub, 0)
    sweep_pass(10, ub, 0, 1, g, 1, fx, fy, fz, w, ua, 0)
    copies = []

    def leave(index, source, at, out, start, size):
        rows = [
            jnp.concatenate([source[at + x, r, 4:12, :] for r in range(4)], axis=1) for x in range(start, start + size)
        ]
        held[index, start : start + size] = rearrange(jnp.concatenate(rows, axis=0), matrix[...]).reshape(size, 8, 512)
        part = pl.ds(start, size)
        copy = pltpu.make_async_copy(held.at[index, part], out.at[part], left.at[len(copies)])
        copy.start()
        copies.append(copy)

    leave(0, ua, 1, correction, 0, 8)
    sweep_pass(4, ua, 0, 2, g, 2, fx, fy, fz, w, res, 0, last=True)
    leave(1, res, 0, residual, 0, 4)
    sweep_pass(4, ua, 4, 6, g, 6, fx, fy, fz, w, res, 4, last=True)
    leave(1, res, 0, residual, 4, 4)
    for copy in copies:
        copy.wait()


VMEM = pl.BlockSpec(memory_space=pltpu.VMEM)
SMEM = pl.BlockSpec(memory_space=pltpu.SMEM)
HBM = pl.BlockSpec(memory_space=pltpu.HBM)


def call(kernel, outs, scratch, *arrays, scalars=0, to_hbm=False, extra=()):
    return pl.pallas_call(
        kernel,
        out_shape=[jax.ShapeDtypeStruct(shape, F32) for shape in outs],
        in_specs=[SMEM] * scalars + [VMEM] * (len(arrays) - scalars),
        out_specs=[HBM if to_hbm else VMEM] * len(outs),
        scratch_shapes=[pltpu.VMEM(shape, F32) for shape in scratch] + list(extra),
        compiler_params=pltpu.CompilerParams(vmem_limit_bytes=32 * 2**20),
    )(*arrays)


def shift(array, axis, by):
    count = lax.axis_size(axis)
    return lax.ppermute(array, axis, [(i, (i + by) % count) for i in range(count)])


def swap(array, axis, start, by=1):
    count = lax.axis_size(axis)
    pairs = [(i, (i + by) % count) for i in range(start, count, 2)]
    return lax.ppermute(array, axis, pairs + [(j, i) for i, j in pairs])


def per_device(right_side, coefficient):
    me_x = lax.axis_index("gx").astype(jnp.int32).reshape(1)
    me_y = lax.axis_index("gy").astype(jnp.int32).reshape(1)
    count = lax.axis_size("gx")
    border = (G_BORDER + K_BORDER, 4, 8, 128)
    own, first, second = call(
        permute_kernel, [(512, 128), border, border], [], me_x, jnp.stack([right_side, coefficient]), scalars=1
    )
    first, second = swap(first, "gx", 1), swap(second, "gx", 0)
    high, low = call(face_kernel, [(FACE_ROWS, 128), (FACE_ROWS, 128)], [], own)
    low, high = shift(high, "gy", 1), shift(low, "gy", -1)
    wide, high_corners, low_corners = call(
        wide_kernel, [((G_SLABS + K_SLABS) * 32, 128), (CORNER_ROWS, 128), (CORNER_ROWS, 128)], [],
        me_x, own, first, second, scalars=1,
    )
    low_corners, high_corners = shift(high_corners, "gy", 1), shift(low_corners, "gy", -1)
    fine, mid, last = (4, 24, 128), (2, 8, 128), (4, 16, 128)
    early = call(
        early_kernel,
        [(8 * 96, 128), (8 * 96, 128), (7, *fine), (6, *fine), (6, *fine), (6, *fine), (6, *fine), (4, *fine), (2, *fine)],
        [], own, low, high,
    )
    g_early, k_early, u0_early = early[0], early[1], early[7]
    piece, u0, g, k, u1, rhs = call(
        fine_kernel,
        [(count, 40, 128), (10, *fine), (12 * 96, 128), (16 * 96, 128), (6, *mid), (8, *mid)],
        [(4, *fine), (14, *fine), (14, *fine), (14, *fine), (14, *fine), (14, *fine), (14, *fine), (8, 2, 24, 128), (10, 2, 24, 128),
         (9, *mid), (8, *mid), (8, *mid), (8, *mid), (8, *mid), (4, *mid), (4, 16, 128), (2, 40, 128), (8, *mid)],
        me_x, wide, low_corners, high_corners, *early, scalars=1,
    )
    piece, u0, g, k, u1, rhs = lax.optimization_barrier((piece, u0, g, k, u1, rhs))
    gathered = lax.all_to_all(piece, "gx", 0, 0)
    gathered, u0, g, k, u1, rhs = lax.optimization_barrier((gathered, u0, g, k, u1, rhs))
    here, high, low, level_1 = call(
        middle_kernel, [(4, 32, 128), (EDGE_ROWS, 128), (EDGE_ROWS, 128), (360, 128)], [], me_x, gathered, u1, rhs, scalars=1
    )
    low, high = shift(high, "gy", 1), shift(low, "gy", -1)
    first, second = call(three_kernel, [(136, 128), (136, 128)], [], me_y, here, low, high, scalars=1)
    first, second = swap(first, "gy", 1, 3), swap(second, "gy", 0, 3)
    faces = call(
        prepare_middle_kernel, [(11, *mid), (10, *mid), (10, *mid), (10, *mid)], [(12, *mid), (2, 24, 128)], k_early, k
    )
    rows = (18, 32, 128)
    v1, high_rows, low_rows = call(
        coarse_kernel, [(128, 128), (32, 128), (32, 128)],
        [rows, rows, rows, rows, (6, *rows), (216, 128), (168, 128), (10, *mid)],
        me_y, first, here, second, low, high, level_1, *faces, scalars=1,
    )
    u0, g, *faces = call(
        prepare_kernel, [(14, *last), (12, *last), (13, *last), (12, *last), (12, *last), (12, *last)], [(14, *last)],
        u0_early, u0, g_early, g, k_early, k,
    )
    low, high = shift(high_rows, "gy", 1), shift(low_rows, "gy", -1)
    return tuple(call(
        last_kernel, [(8, 8, 512), (8, 8, 512)],
        [(128, 128), (8, 2, 16, 128), (14, *last), (12, *last), (8, *last), (2, 8, 8, 512)],
        v1, low, high, u0, g, *faces, inverse_permutation(), to_hbm=True, extra=[pltpu.SemaphoreType.DMA((3,))],
    ))


def solution(mesh):
    placed = (P("gx", "gy", None), P("gx", "gy", None))
    return jax.shard_map(per_device, mesh=mesh, in_specs=placed, out_specs=placed, check_vma=False)
```
